32 devices in a mesh: dp: 4 (over z), expert: 8 (over y, x, core).
Axes of the slice: x: 2, y: 2, z: 4, core: 2. Of those that a mesh axis runs over, the one named last changes fastest.
Arguments:
- tokens: bfloat16 [4096, 2048], P(('dp', 'expert')), may hold values from -6 to 6
- expert_ids: int32 [4096, 2], P(('dp', 'expert')), may hold values from 0 to 7, all different within a row; in each aligned block of 128 rows (0 to 127, 128 to 255, ...) at most 64 rows name the same one
- gate_probs: float32 [4096, 2], P(('dp', 'expert')), may hold values from 0.1 to 1
- w_gate: bfloat16 [8, 2048, 768], P('expert'), may hold values from -0.125 to 0.125
- w_up: bfloat16 [8, 2048, 768], P('expert'), may hold values from -0.125 to 0.125
- w_down: bfloat16 [8, 2048, 768], P('expert'), may hold values from -0.21875 to 0.21875
- out_grad: bfloat16 [4096, 2048], P(('dp', 'expert')), may hold values from -6 to 6
Outputs:
- mixed: bfloat16 [4096, 2048], P(('dp', 'expert'))
- tokens_grad: bfloat16 [4096, 2048], P(('dp', 'expert'))
- grad_gate: bfloat16 [8, 2048, 768], P('expert', 'dp')
- grad_up: bfloat16 [8, 2048, 768], P('expert', 'dp')
- grad_down: bfloat16 [8, 2048, 768], P('expert', 'dp')
The draws below stay inside these ranges and needn't reach their ends.
Inputs may be any that keep to these rules, and one draw needn't show every extreme that they name: `expert_ids`: within each group of 128 tokens no expert is chosen by more than 64 tokens, and some expert reaches 64; a token's 2 experts differ; every expert is chosen somewhere.
All inputs are finite; a program needn't handle non-finite values.
Results may differ from the reference program's by a relative error of at most 0.014.
Values may be sent and summed in bfloat16 or wider, within the bound.
No kernel may reach another device: no remote copies, remote signals or barrier semaphores. Data moves between devices by JAX's collectives and lax.ppermute only.
A program may use at most 128 MiB of HBM per device.

```python
import math
import jax
import jax.numpy as jnp
import numpy as np
from jax import lax

D = 2048
H = 768
TOP = 2
TOK_DEV = 128
EXPERTS = 8
CAP = 64
TOKENS = 4096
N_DP = 4
N_EXPERT = 8


def raised(entries, own_key, source, target, parts, factor):
    def block_of(dim):
        return (jnp.arange(entries.shape[dim]) // (entries.shape[dim] // parts)).reshape((-1,) + (1,) * (entries.ndim - 1 - dim))

    one_side = jax.random.permutation(own_key, parts)[block_of(target)]
    other_side = (block_of(target) + parts // 2) % parts
    return jnp.where((block_of(source) == one_side) | (block_of(source) == other_side), factor * entries, entries)


def levels(stream_key, shape, split, smallest, top_value):
    factor_of, own = 1.0, jax.random.fold_in(stream_key, 6)
    for dim, blocks in split:
        steps = jnp.exp(jax.random.uniform(jax.random.fold_in(own, dim), (blocks,), jnp.float32, smallest / len(split), top_value / len(split)))
        factor_of = factor_of * jnp.repeat(steps, shape[dim] // blocks).reshape([-1 if axis == dim else 1 for axis in range(len(shape))])
    return factor_of


def routed_block(rng, own, number, rows, amount, top, limit, skew):
    ranking = jax.random.permutation(rng, amount)
    crowded, usual = portions_of(amount, rows * top, limit, skew, True), portions_of(amount, rows * top, limit, skew, False)
    places = jnp.arange(amount)

    def named(tallies, offset_by):
        used = int((tallies > 0).sum())
        fixed = max(1, used // 4)
        shifted = fixed + (places - fixed + offset_by * (used - fixed)) % max(1, amount - fixed)
        return jnp.zeros((amount,), jnp.int32).at[ranking[jnp.where(places < fixed, places, shifted)]].set(jnp.asarray(tallies, jnp.int32))

    tallies = jnp.where(number % 4 == 0, named(crowded, number // 4), named(usual, number - number // 4 - 1))
    mixed = jax.random.permutation(jax.random.fold_in(own, 3), amount)
    source_of, sink = mixed[0:amount // 2 * 2:2], mixed[1:amount // 2 * 2:2]
    slack = jnp.minimum(tallies[source_of] - 1, limit - tallies[sink]) // 2
    slack = jnp.where((source_of == ranking[0]) | (sink == ranking[0]) | (tallies[sink] == 0), 0, jnp.maximum(slack, 0))
    shifted = jax.random.randint(jax.random.fold_in(own, 4), (amount // 2,), 0, 1 << 20) % (slack + 1)
    tallies = tallies.at[source_of].add(-shifted).at[sink].add(shifted)
    labels = jnp.searchsorted(jnp.cumsum(tallies), jnp.arange(rows * top), side="right").astype(jnp.int32)
    table = labels.reshape(top, rows).T
    table = table[jax.random.permutation(jax.random.fold_in(own, 1), rows)]
    offset_by = jax.random.randint(jax.random.fold_in(own, 2), (rows, 1), 0, top)
    return jnp.take_along_axis(table, (jnp.arange(top)[None, :] + offset_by) % top, axis=1)


def portions_of(count, total, reach, slope, full):
    portions = [(1 << 20) // math.isqrt(grade ** slope) + 1 for grade in range(1, count + 1)]
    largest = reach if full else min(reach, max(-(-total // count), total * portions[0] // sum(portions)))
    least = 1 if total - largest >= count - 1 else 0
    holding, spare = [largest] + [least] * (count - 1), total - largest - least * (count - 1)
    while spare > 0:
        free = [i for i in range(1, count) if holding[i] < largest] or [i for i in range(1, count) if holding[i] < reach]
        pool, budget = sum([portions[i] for i in free]), spare
        for i in free:
            addition = min(reach - holding[i], max(1, budget * portions[i] // pool), spare)
            holding[i] = holding[i] + addition
            spare = spare - addition
    return np.array(holding)


def normal_values(own_key, shape, spread, limit, cuts=(), held_as=jnp.bfloat16):
    array = spread * jax.random.normal(own_key, shape, jnp.float32)
    if cuts:
        array = array * levels(own_key, shape, cuts, -0.22, 0.18)
    return jnp.clip(array, -limit, limit).astype(held_as)


def gaussian_with(rng, extent, deviation, most, cuts, heavy, held_as=jnp.bfloat16):
    result = deviation * jax.random.normal(rng, extent, jnp.float32)
    if cuts:
        result = result * levels(rng, extent, cuts, -0.22, 0.18)
    return jnp.clip(raised(result, jax.random.fold_in(rng, 3), *heavy), -most, most).astype(held_as)


def setup_inputs(seed: int = 0) -> dict:
    key_of = jax.random.split(jax.random.key(seed), 8)
    tokens = gaussian_with(key_of[0], (TOKENS, D), 1.0, 6.0, ((0, 32),), (0, 1, 32, 2.75))
    expert_ids_keys = jax.random.split(jax.random.fold_in(key_of[1], 1), TOKENS // TOK_DEV)
    expert_ids_turns = jax.random.permutation(jax.random.fold_in(key_of[1], 3), TOKENS // TOK_DEV)
    expert_ids = jax.vmap(lambda own, number: routed_block(jax.random.fold_in(key_of[1], 2), own, number, TOK_DEV, EXPERTS, TOP, CAP, 2))(expert_ids_keys, expert_ids_turns).reshape((TOKENS, TOP))
    gate_probs = jnp.clip(0.1 + 0.9 * jax.random.uniform(key_of[2], (TOKENS, TOP), jnp.float32) ** levels(key_of[2], (TOKENS, TOP), ((0, 32),), -0.2, 0.2), 0.1, 1.0)
    w_gate = normal_values(key_of[3], (EXPERTS, D, H), D ** -0.5, 0.125, ((0, 8),))
    w_up = normal_values(key_of[4], (EXPERTS, D, H), D ** -0.5, 0.125, ((0, 8),))
    w_down = normal_values(key_of[5], (EXPERTS, D, H), H ** -0.5, 0.21875, ((0, 8),))
    out_grad = normal_values(key_of[6], (TOKENS, D), 1.0, 6.0, ((0, 32),))
    return {"tokens": tokens, "expert_ids": expert_ids, "gate_probs": gate_probs, "w_gate": w_gate, "w_up": w_up, "w_down": w_down, "out_grad": out_grad}


def route_slots(ids):
    flat = ids.reshape(-1).astype(jnp.int32)
    onehot = (flat[:, None] == jnp.arange(EXPERTS, dtype=jnp.int32)[None, :]).astype(jnp.int32)
    before = jnp.cumsum(onehot, axis=0) - onehot
    position = jnp.sum(before * onehot, axis=1).astype(jnp.int32)
    return (flat * CAP + position).astype(jnp.int32)


def place_rows(rows, slot):
    empty = jnp.zeros((EXPERTS * CAP, D), rows.dtype)
    return empty.at[slot].set(rows)


def pick_rows(table, slot):
    return jnp.take(table, slot, axis=0)


def reference(tokens, expert_ids, gate_probs, w_gate, w_up, w_down, out_grad):
    wg32 = w_gate.astype(jnp.float32)
    wu32 = w_up.astype(jnp.float32)
    wd32 = w_down.astype(jnp.float32)
    tok_sets = tokens.reshape(N_DP, N_EXPERT, TOK_DEV, D)
    id_sets = expert_ids.reshape(N_DP, N_EXPERT, TOK_DEV, TOP)
    prob_sets = gate_probs.reshape(N_DP, N_EXPERT, TOK_DEV, TOP)
    dy_sets = out_grad.reshape(N_DP, N_EXPERT, TOK_DEV, D)

    def one_set(carry, inputs):
        xs, ids, probs, dys = inputs
        slots = jax.vmap(route_slots)(ids)
        x_routes = jnp.repeat(xs, TOP, axis=1)
        x_slot = jax.vmap(place_rows)(x_routes, slots).reshape(N_EXPERT, EXPERTS, CAP, D)
        xf = x_slot.astype(jnp.float32)
        gact = jnp.einsum('secd,edh->sech', xf, wg32)
        uact = jnp.einsum('secd,edh->sech', xf, wu32)
        hidden = (jax.nn.silu(gact) * uact).astype(jnp.bfloat16)
        o_slot = jnp.einsum('sech,edh->secd', hidden.astype(jnp.float32), wd32).astype(jnp.bfloat16)
        picked = jax.vmap(pick_rows)(o_slot.reshape(N_EXPERT, EXPERTS * CAP, D), slots)
        picked = picked.astype(jnp.float32).reshape(N_EXPERT, TOK_DEV, TOP, D)
        mixed = jnp.sum(picked * probs[..., None], axis=2).astype(jnp.bfloat16)
        dy_routes = jnp.repeat(dys, TOP, axis=1).astype(jnp.float32) * probs.reshape(N_EXPERT, TOK_DEV * TOP)[..., None]
        dy_slot = jax.vmap(place_rows)(dy_routes.astype(jnp.bfloat16), slots).reshape(N_EXPERT, EXPERTS, CAP, D)
        dyf = dy_slot.astype(jnp.float32)
        dh = jnp.einsum('secd,edh->sech', dyf, wd32)
        sig = jax.nn.sigmoid(gact)
        dg = (dh * uact * sig * (1.0 + gact * (1.0 - sig))).astype(jnp.bfloat16)
        du = (dh * gact * sig).astype(jnp.bfloat16)
        dgf = dg.astype(jnp.float32)
        duf = du.astype(jnp.float32)
        dx_slot = (jnp.einsum('sech,edh->secd', dgf, wg32) + jnp.einsum('sech,edh->secd', duf, wu32)).astype(jnp.bfloat16)
        dx_picked = jax.vmap(pick_rows)(dx_slot.reshape(N_EXPERT, EXPERTS * CAP, D), slots)
        dx_tok = jnp.sum(dx_picked.astype(jnp.float32).reshape(N_EXPERT, TOK_DEV, TOP, D), axis=2).astype(jnp.bfloat16)
        part_g = jnp.einsum('secd,sech->edh', xf, dgf).astype(jnp.bfloat16)
        part_u = jnp.einsum('secd,sech->edh', xf, duf).astype(jnp.bfloat16)
        part_d = jnp.einsum('secd,sech->edh', dyf, hidden.astype(jnp.float32)).astype(jnp.bfloat16)
        part_g, part_u, part_d = lax.optimization_barrier((part_g, part_u, part_d))
        carry = (carry[0] + part_g.astype(jnp.float32), carry[1] + part_u.astype(jnp.float32), carry[2] + part_d.astype(jnp.float32))
        return carry, (mixed, dx_tok)

    zero = jnp.zeros((EXPERTS, D, H), jnp.float32)
    sums, outs = lax.scan(one_set, (zero, zero, zero), (tok_sets, id_sets, prob_sets, dy_sets))
    mixed = outs[0].reshape(TOKENS, D)
    tokens_grad = outs[1].reshape(TOKENS, D)
    return (mixed, tokens_grad, sums[0].astype(jnp.bfloat16), sums[1].astype(jnp.bfloat16), sums[2].astype(jnp.bfloat16))
```

```python
import functools

import jax
import jax.numpy as jnp
from jax import lax
from jax.experimental import pallas as pl
from jax.experimental.pallas import tpu as pltpu
from jax.sharding import PartitionSpec as P

F32 = jnp.float32
BF16 = jnp.bfloat16
VMEM_LIMIT = 48 * 1024 * 1024


def route_slots(expert_ids, experts, capacity):
    flat = expert_ids.reshape(-1)
    onehot = (flat[:, None] == jnp.arange(experts, dtype=jnp.int32)[None, :]).astype(jnp.int32)
    before = jnp.cumsum(onehot, axis=0) - onehot
    position = jnp.sum(before * onehot, axis=1)
    return flat * capacity + position


def local_any(tokens, expert_ids, gate_probs, w_gate, w_up, w_down, out_grad):
    token_count, top_count = expert_ids.shape
    width = tokens.shape[1]
    local_experts = w_gate.shape[0]
    peers = lax.axis_size("expert")
    experts = local_experts * peers
    capacity = max(2, 2 * token_count * top_count // experts)
    slot_total = experts * capacity
    route_total = token_count * top_count
    slot = route_slots(expert_ids, experts, capacity)
    owner = slot[None, :] == jnp.arange(slot_total, dtype=jnp.int32)[:, None]
    live = jnp.any(owner, axis=1)
    route_index = jnp.sum(
        jnp.where(owner, jnp.arange(route_total, dtype=jnp.int32)[None, :], 0), axis=1
    )
    token_of_slot = route_index // top_count
    slot_prob = jnp.sum(jnp.where(owner, gate_probs.reshape(-1)[None, :], 0.0), axis=1)
    dispatched = jnp.where(
        live[:, None], jnp.take(tokens, token_of_slot, axis=0), jnp.zeros((), tokens.dtype)
    )
    dispatched = dispatched.reshape(peers, local_experts, capacity, width)
    received = lax.all_to_all(dispatched, "expert", split_axis=0, concat_axis=0, tiled=True)
    gate_act = jnp.einsum("secd,edh->sech", received, w_gate, preferred_element_type=F32)
    up_act = jnp.einsum("secd,edh->sech", received, w_up, preferred_element_type=F32)
    hidden = (jax.nn.silu(gate_act) * up_act).astype(BF16)
    result = jnp.einsum("sech,edh->secd", hidden, w_down, preferred_element_type=F32).astype(BF16)
    returned = lax.all_to_all(result, "expert", split_axis=0, concat_axis=0, tiled=True)
    picked = jnp.take(returned.reshape(slot_total, width), slot, axis=0).astype(F32)
    picked = picked.reshape(token_count, top_count, width)
    mixed = jnp.sum(picked * gate_probs[:, :, None], axis=1).astype(BF16)
    dy_rows = jnp.where(
        live[:, None], jnp.take(out_grad, token_of_slot, axis=0), jnp.zeros((), out_grad.dtype)
    )
    dy_slot = (dy_rows.astype(F32) * slot_prob[:, None]).astype(BF16)
    dy_slot = dy_slot.reshape(peers, local_experts, capacity, width)
    dy_recv = lax.all_to_all(dy_slot, "expert", split_axis=0, concat_axis=0, tiled=True)
    d_hidden = jnp.einsum("secd,edh->sech", dy_recv, w_down, preferred_element_type=F32)
    sigma = jax.nn.sigmoid(gate_act)
    d_gate = (d_hidden * up_act * sigma * (1.0 + gate_act * (1.0 - sigma))).astype(BF16)
    d_up = (d_hidden * gate_act * sigma).astype(BF16)
    dx_slot = jnp.einsum("sech,edh->secd", d_gate, w_gate, preferred_element_type=F32)
    dx_slot = (
        dx_slot + jnp.einsum("sech,edh->secd", d_up, w_up, preferred_element_type=F32)
    ).astype(BF16)
    dx_back = lax.all_to_all(dx_slot, "expert", split_axis=0, concat_axis=0, tiled=True)
    dx_picked = jnp.take(dx_back.reshape(slot_total, width), slot, axis=0).astype(F32)
    tokens_grad = jnp.sum(dx_picked.reshape(token_count, top_count, width), axis=1).astype(BF16)
    first = jnp.einsum("secd,sech->deh", received, d_gate, preferred_element_type=F32)
    second = jnp.einsum("secd,sech->deh", received, d_up, preferred_element_type=F32)
    third = jnp.einsum("secd,sech->deh", dy_recv, hidden, preferred_element_type=F32)
    share = lax.psum_scatter(
        jnp.stack([first, second, third], axis=1).astype(BF16),
        "dp",
        scatter_dimension=0,
        tiled=True,
    )
    grads = [jnp.transpose(share[:, k], (1, 0, 2)) for k in range(3)]
    return (mixed, tokens_grad, *grads)


def cost(macs, size):
    return pl.CostEstimate(flops=2 * macs, bytes_accessed=size, transcendentals=0)


def params(steps=0):
    kwargs = {"vmem_limit_bytes": VMEM_LIMIT}
    if steps:
        kwargs["dimension_semantics"] = ("arbitrary",) * steps
    return pltpu.CompilerParams(**kwargs)


def nn(a, b):
    return lax.dot_general(a, b, (((1,), (0,)), ((), ())), preferred_element_type=F32)


def nt(a, b):
    return lax.dot_general(a, b, (((1,), (1,)), ((), ())), preferred_element_type=F32)


def tn(a, b):
    return lax.dot_general(a, b, (((0,), (0,)), ((), ())), preferred_element_type=F32)


def routed_here(meta, me, rank_ref, prob_ref):
    expert = me.astype(F32)
    first, second = meta[:, 0, :] == expert, meta[:, 1, :] == expert
    named = (first | second).astype(F32)
    count = named.shape[1]
    earlier = lax.broadcasted_iota(jnp.int32, (count, count), 0) < lax.broadcasted_iota(
        jnp.int32, (count, count), 1
    )
    rank = nn(named.astype(BF16), earlier.astype(F32).astype(BF16))
    rank_ref[...] = jnp.where(named > 0, rank, -1.0)
    if prob_ref is not None:
        prob_ref[...] = jnp.where(first, meta[:, 2, :], jnp.where(second, meta[:, 3, :], 0.0))


def group_blocks(refs):
    own, bx, by, da, db, c_own, c_bx, c_by, c_da, c_db = refs
    whole = {0: own, 1: c_own, 2: bx, 3: c_bx, 4: by, 5: c_by}
    for k in range(8):
        if k in whole:
            yield k, whole[k][...]
        else:
            top, bottom = (da, db) if k == 6 else (c_da, c_db)
            yield k, jnp.concatenate([top[...], bottom[...]], axis=0)


def fill_slots(me, blocks, rank_ref, prob_ref, out_ref, capacity):
    for k, rows in group_blocks(blocks):
        source = jnp.bitwise_xor(me, k)
        rank = rank_ref[pl.ds(source, 1), :]
        place = lax.broadcasted_iota(jnp.int32, (capacity, rank.shape[1]), 0).astype(F32)
        hit = place == rank
        picked = nn(hit.astype(F32).astype(BF16), rows)
        if prob_ref is not None:
            scale = jnp.sum(jnp.where(hit, prob_ref[pl.ds(source, 1), :], 0.0), axis=1, keepdims=True)
            picked = picked * scale
        start = pl.multiple_of(source * capacity, capacity)
        out_ref[pl.ds(start, capacity), :] = picked.astype(BF16)


def forward_kernel(capacity, pos_ref, meta_ref, *refs):
    blocks, (wg_ref, wu_ref, x_ref, h_ref, a_ref, b_ref, rank_ref) = refs[:10], refs[10:]
    me = pos_ref[0]

    @pl.when(pl.program_id(0) == 0)
    def _():
        routed_here(meta_ref[...], me, rank_ref, None)
        fill_slots(me, blocks, rank_ref, None, x_ref, capacity)

    x = x_ref[...]
    g = nn(x, wg_ref[...])
    u = nn(x, wu_ref[...])
    s = jax.nn.sigmoid(g)
    b = g * s
    h_ref[...] = (b * u).astype(BF16)
    a_ref[...] = u * s * (1.0 + g * (1.0 - s))
    b_ref[...] = b


def forward(pos, meta, blocks, w_gate, w_up, capacity):
    width, hid = w_gate.shape
    slots = 8 * capacity
    tile = 256
    full = lambda a: pl.BlockSpec(a.shape, lambda i, p, n=a.ndim: (0,) * n)
    wide = pl.BlockSpec((width, tile), lambda i, p: (0, i))
    out = pl.BlockSpec((slots, tile), lambda i, p: (0, i))
    return pl.pallas_call(
        functools.partial(forward_kernel, capacity),
        grid_spec=pltpu.PrefetchScalarGridSpec(
            num_scalar_prefetch=1,
            grid=(hid // tile,),
            in_specs=[full(meta)] + [full(b) for b in blocks] + [wide, wide],
            out_specs=[pl.BlockSpec((slots, width), lambda i, p: (0, 0)), out, out, out],
            scratch_shapes=[pltpu.VMEM((8, meta.shape[2]), F32)],
        ),
        out_shape=[
            jax.ShapeDtypeStruct((slots, width), BF16),
            jax.ShapeDtypeStruct((slots, hid), BF16),
            jax.ShapeDtypeStruct((slots, hid), F32),
            jax.ShapeDtypeStruct((slots, hid), F32),
        ],
        compiler_params=params(1),
        cost_estimate=cost(2 * slots * width * hid, 16 << 20),
        name="forward",
    )(pos, meta, *blocks, w_gate, w_up)


def cotangent_kernel(capacity, chunk, pos_ref, meta_ref, *refs):
    blocks, (h_ref, dy_ref, far_ref, rank_ref, prob_ref) = refs[:10], refs[10:]
    me = pos_ref[0]
    routed_here(meta_ref[...], me, rank_ref, prob_ref)
    fill_slots(me, blocks, rank_ref, prob_ref, dy_ref, capacity)
    start = pl.multiple_of(pos_ref[1] * chunk, chunk)
    far_ref[...] = tn(dy_ref[:, pl.ds(start, chunk)], h_ref[...]).astype(BF16)


def cotangent(pos, meta, blocks, h, chunk, capacity):
    width = blocks[0].shape[1]
    slots, hid = h.shape
    vmem = pl.BlockSpec(memory_space=pltpu.VMEM)
    return pl.pallas_call(
        functools.partial(cotangent_kernel, capacity, chunk),
        in_specs=[pl.BlockSpec(memory_space=pltpu.SMEM)] + [vmem] * (len(blocks) + 2),
        out_specs=[vmem, vmem],
        scratch_shapes=[pltpu.VMEM((8, meta.shape[2]), F32)] * 2,
        out_shape=[
            jax.ShapeDtypeStruct((slots, width), BF16),
            jax.ShapeDtypeStruct((chunk, hid), BF16),
        ],
        compiler_params=params(),
        cost_estimate=cost(slots * chunk * hid, 8 << 20),
        name="cotangent",
    )(pos, meta, *blocks, h)


def backward_kernel(dy_ref, wd_ref, a_ref, b_ref, dg_ref, du_ref):
    dh = nn(dy_ref[...], wd_ref[...])
    dg_ref[...] = (dh * a_ref[...]).astype(BF16)
    du_ref[...] = (dh * b_ref[...]).astype(BF16)


def backward(dy, w_down, a, b):
    width, hid = w_down.shape
    slots = dy.shape[0]
    tile = 256
    out = pl.BlockSpec((slots, tile), lambda i: (0, i))
    return pl.pallas_call(
        backward_kernel,
        grid=(hid // tile,),
        in_specs=[
            pl.BlockSpec((slots, width), lambda i: (0, 0)),
            pl.BlockSpec((width, tile), lambda i: (0, i)),
            out,
            out,
        ],
        out_specs=[out, out],
        out_shape=[jax.ShapeDtypeStruct((slots, hid), BF16)] * 2,
        compiler_params=params(1),
        cost_estimate=cost(slots * width * hid, 10 << 20),
        name="backward",
    )(dy, w_down, a, b)


def gradient_kernel(lefts, count, dtype, pos_ref, *refs):
    ins, outs = refs[: len(refs) - count], refs[len(refs) - count :]
    pairs = ins[:lefts], ins[lefts:]
    for n, out in enumerate(outs):
        total = None
        for left, right in outs_of(n, lefts, count):
            term = tn(pairs[0][left][...], pairs[1][right][...])
            total = term if total is None else total + term
        out[...] = total.astype(dtype)


def outs_of(n, lefts, count):
    if lefts == 1:
        return [(0, n)]
    if lefts == 2:
        return [(0 if n < 2 else 1, n)]
    return [(0 if n < 2 else 1, n), (2 if n < 2 else 3, 3 + n)]


def gradient(pos, which, lefts, rights, chunk, dtype, count):
    slots, hid = rights[0].shape
    left_spec = pl.BlockSpec((slots, chunk), lambda i, p: (0, p[which]))
    right_spec = pl.BlockSpec((slots, hid), lambda i, p: (0, 0))
    out = pl.BlockSpec((chunk, hid), lambda i, p: (0, 0))
    return pl.pallas_call(
        functools.partial(gradient_kernel, len(lefts), count, dtype),
        grid_spec=pltpu.PrefetchScalarGridSpec(
            num_scalar_prefetch=1,
            grid=(1,),
            in_specs=[left_spec] * len(lefts) + [right_spec] * len(rights),
            out_specs=[out] * count,
        ),
        out_shape=[jax.ShapeDtypeStruct((chunk, hid), dtype)] * count,
        compiler_params=params(1),
        cost_estimate=cost(len(rights) * slots * chunk * hid, 4 << 20),
        name="gradient",
    )(pos, *lefts, *rights)


def rows_kernel(count, *refs):
    out = refs[-1]
    total = nt(refs[0][...], refs[1][...])
    for k in range(1, count):
        total = total + nt(refs[2 * k][...], refs[2 * k + 1][...])
    out[...] = total.astype(BF16)


def rows_back(pairs):
    slots, hid = pairs[0][0].shape
    width = pairs[0][1].shape[0]
    tile = 512
    specs = [
        pl.BlockSpec((slots, hid), lambda i: (0, 0)),
        pl.BlockSpec((tile, hid), lambda i: (i, 0)),
    ] * len(pairs)
    return pl.pallas_call(
        functools.partial(rows_kernel, len(pairs)),
        grid=(width // tile,),
        in_specs=specs,
        out_specs=pl.BlockSpec((slots, tile), lambda i: (0, i)),
        out_shape=jax.ShapeDtypeStruct((slots, width), BF16),
        compiler_params=params(1),
        cost_estimate=cost(len(pairs) * slots * hid * width, 8 << 20),
        name="rows_back",
    )(*[a for pair in pairs for a in pair])


def combine_kernel(capacity, scaled, ids_ref, prob_ref, rows_ref, out_ref):
    ids = ids_ref[...]
    count = ids.shape[0]
    slots = rows_ref.shape[0]
    lane = lax.broadcasted_iota(jnp.int32, (count, 128), 1)
    named = ((lane == ids[:, 0:1]) | (lane == ids[:, 1:2])).astype(F32)
    earlier = lax.broadcasted_iota(jnp.int32, (count, count), 1) < lax.broadcasted_iota(
        jnp.int32, (count, count), 0
    )
    rank = nn(earlier.astype(F32).astype(BF16), named.astype(BF16))
    place = lax.broadcasted_iota(jnp.int32, (count, slots), 1)
    hits = []
    for k in range(2):
        own = ids[:, k : k + 1]
        at = jnp.sum(jnp.where(lane == own, rank, 0.0), axis=1, keepdims=True).astype(jnp.int32)
        hits.append((place == own * capacity + at).astype(F32).astype(BF16))
    rows = rows_ref[...]
    if scaled:
        probs = prob_ref[...]
        total = nn(hits[0], rows) * probs[:, 0:1] + nn(hits[1], rows) * probs[:, 1:2]
    else:
        total = nn(hits[0] + hits[1], rows)
    out_ref[...] = total.astype(BF16)


def combine(ids, probs, rows, capacity, scaled):
    count = ids.shape[0]
    slots, width = rows.shape
    tile = 512
    return pl.pallas_call(
        functools.partial(combine_kernel, capacity, scaled),
        grid=(width // tile,),
        in_specs=[
            pl.BlockSpec(ids.shape, lambda i: (0, 0)),
            pl.BlockSpec(probs.shape, lambda i: (0, 0)),
            pl.BlockSpec((slots, tile), lambda i: (0, i)),
        ],
        out_specs=pl.BlockSpec((count, tile), lambda i: (0, i)),
        out_shape=jax.ShapeDtypeStruct((count, width), BF16),
        compiler_params=params(1),
        cost_estimate=cost(2 * count * slots * width, 3 << 20),
        name="combine",
    )(ids, probs, rows)


def local_pairs(tokens, expert_ids, gate_probs, w_gate, w_up, w_down, out_grad):
    count, top = expert_ids.shape
    width = tokens.shape[1]
    w_gate, w_up, w_down = w_gate[0], w_up[0], w_down[0]
    planes, peers = lax.axis_size("dp"), lax.axis_size("expert")
    capacity = 2 * count * top // peers
    chunk = width // planes
    z = lax.axis_index("dp")
    me = lax.axis_index("expert")
    left = z < 2
    far = jnp.where(left, 3, 0)
    near = jnp.where(left, 2, 1)
    pos = jnp.stack([me, far, near, z]).astype(jnp.int32)

    def over(x, bit):
        return lax.ppermute(x, "expert", [(i, i ^ bit) for i in range(peers)])

    def gather(x):
        half = x.shape[0] // 2
        bx, by = over(x, 2), over(x, 4)
        da, db = over(by[:half], 2), over(bx[half:], 4)
        held = (x, bx, by, da, db)
        return held + tuple(over(t, 1) for t in held)

    def partner(x):
        return lax.ppermute(x, "dp", [(i, i ^ 1) for i in range(planes)])

    def inward(x):
        return lax.ppermute(x, "dp", [(0, 1), (3, 2)])

    def across_far(x):
        return lax.ppermute(x, "dp", [(1, 3), (2, 0)])

    def across_near(x):
        return lax.ppermute(x, "dp", [(1, 2), (2, 1)])

    meta = jnp.concatenate([expert_ids.astype(F32), gate_probs], axis=1).T
    meta = jnp.concatenate([meta, partner(meta)], axis=0)
    meta = lax.all_gather(meta, "expert", axis=0)
    meta, meta_p = meta[:, :4], meta[:, 4:]
    tokens_p, out_grad_p = partner(tokens), partner(out_grad)

    x, h, a, b = forward(pos, meta, gather(tokens), w_gate, w_up, capacity)
    dy, far_down = cotangent(pos, meta, gather(out_grad), h, chunk, capacity)
    dg, du = backward(dy, w_down, a, b)
    far_gate, far_up = gradient(pos, 1, [x], [dg, du], chunk, BF16, 2)
    near_gate, near_up, near_down = gradient(pos, 2, [x, dy], [dg, du, h], chunk, BF16, 3)

    def add(p, q):
        return (p.astype(F32) + q.astype(F32)).astype(BF16)

    got_far, got_near = {}, {}
    for name, piece in (("down", far_down), ("gate", far_gate), ("up", far_up)):
        got_far[name] = across_far(add(piece, inward(piece)))
    for name, piece in (("down", near_down), ("gate", near_gate), ("up", near_up)):
        got_near[name] = across_near(add(piece, inward(piece)))

    o = rows_back([(h, w_down)])
    dx = rows_back([(dg, w_gate), (du, w_up)])

    def give_back(rows):
        rows = rows.reshape(peers, capacity, width)
        rows = lax.all_to_all(rows, "expert", split_axis=0, concat_axis=0, tiled=True)
        return rows.reshape(peers * capacity, width)

    mixed = combine(expert_ids, gate_probs, give_back(o), capacity, True)
    tokens_grad = combine(expert_ids, gate_probs, give_back(dx), capacity, False)

    x_p, h_p, a_p, b_p = forward(pos, meta_p, gather(tokens_p), w_gate, w_up, capacity)
    dy_p, _ = cotangent(pos, meta_p, gather(out_grad_p), h_p, chunk, capacity)
    dg_p, du_p = backward(dy_p, w_down, a_p, b_p)
    own = gradient(pos, 3, [x, dy, x_p, dy_p], [dg, du, h, dg_p, du_p, h_p], chunk, F32, 3)
    grads = []
    for name, mine in zip(("gate", "up", "down"), own):
        total = mine + got_far[name].astype(F32) + got_near[name].astype(F32)
        grads.append(total.astype(BF16)[None])
    return (mixed, tokens_grad, *grads)


def solution(mesh):
    placed = (
        P(("dp", "expert"), None),
        P(("dp", "expert"), None),
        P(("dp", "expert"), None),
        P("expert", None, None),
        P("expert", None, None),
        P("expert", None, None),
        P(("dp", "expert"), None),
    )
    paired = mesh.shape["dp"] == 4 and mesh.shape["expert"] == 8
    return jax.shard_map(
        local_pairs if paired else local_any,
        mesh=mesh,
        in_specs=placed,
        out_specs=(
            P(("dp", "expert"), None),
            P(("dp", "expert"), None),
            P("expert", "dp", None),
            P("expert", "dp", None),
            P("expert", "dp", None),
        ),
        check_vma=False,
    )
```

```python
import functools

import jax
import jax.numpy as jnp
from jax import lax
from jax.experimental import pallas as pl
from jax.experimental.pallas import tpu as pltpu
from jax.sharding import PartitionSpec as P

F32 = jnp.float32
BF16 = jnp.bfloat16


def route_slots(expert_ids, experts, capacity):
    flat = expert_ids.reshape(-1)
    onehot = (flat[:, None] == jnp.arange(experts, dtype=jnp.int32)[None, :]).astype(jnp.int32)
    before = jnp.cumsum(onehot, axis=0) - onehot
    position = jnp.sum(before * onehot, axis=1)
    return flat * capacity + position


def local_any(tokens, expert_ids, gate_probs, w_gate, w_up, w_down, out_grad):
    token_count, top_count = expert_ids.shape
    width = tokens.shape[1]
    local_experts = w_gate.shape[0]
    peers = lax.axis_size("expert")
    experts = local_experts * peers
    capacity = max(2, 2 * token_count * top_count // experts)
    slot_total = experts * capacity
    route_total = token_count * top_count
    slot = route_slots(expert_ids, experts, capacity)
    owner = slot[None, :] == jnp.arange(slot_total, dtype=jnp.int32)[:, None]
    live = jnp.any(owner, axis=1)
    route_index = jnp.sum(
        jnp.where(owner, jnp.arange(route_total, dtype=jnp.int32)[None, :], 0), axis=1
    )
    token_of_slot = route_index // top_count
    slot_prob = jnp.sum(jnp.where(owner, gate_probs.reshape(-1)[None, :], 0.0), axis=1)
    dispatched = jnp.where(
        live[:, None], jnp.take(tokens, token_of_slot, axis=0), jnp.zeros((), tokens.dtype)
    )
    dispatched = dispatched.reshape(peers, local_experts, capacity, width)
    received = lax.all_to_all(dispatched, "expert", split_axis=0, concat_axis=0, tiled=True)
    gate_act = jnp.einsum("secd,edh->sech", received, w_gate, preferred_element_type=F32)
    up_act = jnp.einsum("secd,edh->sech", received, w_up, preferred_element_type=F32)
    hidden = (jax.nn.silu(gate_act) * up_act).astype(BF16)
    result = jnp.einsum("sech,edh->secd", hidden, w_down, preferred_element_type=F32).astype(BF16)
    returned = lax.all_to_all(result, "expert", split_axis=0, concat_axis=0, tiled=True)
    picked = jnp.take(returned.reshape(slot_total, width), slot, axis=0).astype(F32)
    picked = picked.reshape(token_count, top_count, width)
    mixed = jnp.sum(picked * gate_probs[:, :, None], axis=1).astype(BF16)
    dy_rows = jnp.where(
        live[:, None], jnp.take(out_grad, token_of_slot, axis=0), jnp.zeros((), out_grad.dtype)
    )
    dy_slot = (dy_rows.astype(F32) * slot_prob[:, None]).astype(BF16)
    dy_slot = dy_slot.reshape(peers, local_experts, capacity, width)
    dy_recv = lax.all_to_all(dy_slot, "expert", split_axis=0, concat_axis=0, tiled=True)
    d_hidden = jnp.einsum("secd,edh->sech", dy_recv, w_down, preferred_element_type=F32)
    sigma = jax.nn.sigmoid(gate_act)
    d_gate = (d_hidden * up_act * sigma * (1.0 + gate_act * (1.0 - sigma))).astype(BF16)
    d_up = (d_hidden * gate_act * sigma).astype(BF16)
    dx_slot = jnp.einsum("sech,edh->secd", d_gate, w_gate, preferred_element_type=F32)
    dx_slot = (
        dx_slot + jnp.einsum("sech,edh->secd", d_up, w_up, preferred_element_type=F32)
    ).astype(BF16)
    dx_back = lax.all_to_all(dx_slot, "expert", split_axis=0, concat_axis=0, tiled=True)
    dx_picked = jnp.take(dx_back.reshape(slot_total, width), slot, axis=0).astype(F32)
    tokens_grad = jnp.sum(dx_picked.reshape(token_count, top_count, width), axis=1).astype(BF16)
    first = jnp.einsum("secd,sech->deh", received, d_gate, preferred_element_type=F32)
    second = jnp.einsum("secd,sech->deh", received, d_up, preferred_element_type=F32)
    third = jnp.einsum("secd,sech->deh", dy_recv, hidden, preferred_element_type=F32)
    share = lax.psum_scatter(
        jnp.stack([first, second, third], axis=1).astype(BF16),
        "dp",
        scatter_dimension=0,
        tiled=True,
    )
    grads = [jnp.transpose(share[:, k], (1, 0, 2)) for k in range(3)]
    return (mixed, tokens_grad, *grads)


EXTRA = 16
TILE = 256
VMEM = pl.BlockSpec(memory_space=pltpu.VMEM)
SMEM = pl.BlockSpec(memory_space=pltpu.SMEM)
ANY = pl.BlockSpec(memory_space=pl.ANY)


def nn(a, b):
    return lax.dot_general(a, b, (((1,), (0,)), ((), ())), preferred_element_type=F32)


def nt(a, b):
    return lax.dot_general(a, b, (((1,), (1,)), ((), ())), preferred_element_type=F32)


def tn(a, b):
    return lax.dot_general(a, b, (((0,), (0,)), ((), ())), preferred_element_type=F32)


def shape(*sizes, dtype=BF16):
    return jax.ShapeDtypeStruct(sizes, dtype)


def run(name, kernel, operands, outs, after=(), held=None, out_held=None, scratch=(), us=1.0, limit=14):
    skip, count = len(after), len(operands) + len(outs)

    def body(*refs):
        refs = refs[skip:]
        kernel(*refs[:count], *refs[count + 1 :])

    return pl.pallas_call(
        body,
        in_specs=[ANY] * skip + list(held or [VMEM] * len(operands)),
        out_specs=list(out_held or [VMEM] * len(outs)) + [VMEM],
        out_shape=list(outs) + [shape(8, 128, dtype=F32)],
        scratch_shapes=list(scratch),
        compiler_params=pltpu.CompilerParams(vmem_limit_bytes=limit * 1024 * 1024),
        cost_estimate=pl.CostEstimate(flops=int(us * 1e9), bytes_accessed=1 << 16, transcendentals=0),
        name=name,
    )(*after, *operands)


def tie(x, after):
    return pl.pallas_call(
        lambda *refs: None,
        in_specs=[ANY] * (1 + len(after)),
        out_specs=ANY,
        out_shape=jax.ShapeDtypeStruct(x.shape, x.dtype),
        input_output_aliases={0: 0},
        cost_estimate=pl.CostEstimate(flops=8, bytes_accessed=8, transcendentals=0),
        name="tie",
    )(x, *after)


def tiles(size, body, tile=TILE):
    @pl.loop(0, size // tile)
    def _(i):
        body(pl.ds(pl.multiple_of(i * tile, tile), tile))


def columns(start, size):
    return pl.ds(pl.multiple_of(start * size, size), size)


def start_all(pairs, sem):
    copies = [pltpu.make_async_copy(src, dst, sem.at[n]) for n, (src, dst) in enumerate(pairs)]
    for copy in copies:
        copy.start()
    return copies


def wait_all(copies):
    for copy in copies:
        copy.wait()


def cut_rows(ref, parts):
    size = ref.shape[0] // parts
    return [pl.ds(n * size, size) for n in range(parts)]


def pack_kernel(tokens_in, grad_in, ids_in, prob_in, rows_ref, grad_ref, raw_ref, meta_ref, ids_ref, prob_ref, sem):
    count, width = tokens_in.shape
    small = start_all([(ids_in, ids_ref), (prob_in, prob_ref)], sem.at[0])
    pairs = []
    for src, to, offset in ((tokens_in, rows_ref, 0), (grad_in, grad_ref, count + EXTRA)):
        for r in cut_rows(src, 2):
            pairs.append((src.at[r, :], to.at[r, :]))
            pairs.append((src.at[r, :], raw_ref.at[pl.ds(offset + r.start, r.size), :]))
    copies = start_all(pairs, sem.at[1])
    wait_all(small)
    rows = [ids_ref[...].astype(F32)]
    for k in range(2):
        rest = prob_ref[k : k + 1, :]
        for _ in range(3):
            rows.append(rest.astype(BF16).astype(F32))
            rest = rest - rows[-1]
    meta = jnp.concatenate(rows + [jnp.zeros((EXTRA - 8, count), F32)], axis=0).astype(BF16)
    meta_ref[...] = meta
    behind = pl.ds(count, EXTRA)
    for ref in (rows_ref, raw_ref):
        ref[behind, :count] = meta
        ref[behind, count:] = jnp.zeros((EXTRA, width - count), BF16)
    wait_all(copies)


def pack(tokens, grad, ids, probs):
    count, width = tokens.shape
    return run(
        "pack",
        pack_kernel,
        [tokens, grad, ids.T, probs.T],
        [shape(count + EXTRA, width), shape(count, width), shape(2 * count + EXTRA, width), shape(EXTRA, count)],
        held=[ANY] * 4,
        scratch=[pltpu.VMEM((2, count), jnp.int32), pltpu.VMEM((2, count), F32), pltpu.SemaphoreType.DMA((2, 8))],
    )


def split_kernel(bx_ref, by_ref, top_ref, bottom_ref, sem):
    half = top_ref.shape[0]
    bottom = pl.ds(half, bottom_ref.shape[0])
    wait_all(start_all([(by_ref.at[pl.ds(0, half), :], top_ref), (bx_ref.at[bottom, :], bottom_ref)], sem))


def split(bx, by, half, after=()):
    rows, width = bx.shape
    outs = [shape(half, width), shape(rows - half, width)]
    return run("split", split_kernel, [bx, by], outs, after, scratch=[pltpu.SemaphoreType.DMA((2,))])


def merge_kernel(own_ref, bx_ref, by_ref, da_ref, db_ref, out_ref, sem):
    half = da_ref.shape[0]
    pairs = [(ref, out_ref.at[k]) for k, ref in enumerate((own_ref, bx_ref, by_ref))]
    pairs.append((da_ref, out_ref.at[3, pl.ds(0, half), :]))
    pairs.append((db_ref, out_ref.at[3, pl.ds(half, db_ref.shape[0]), :]))
    wait_all(start_all(pairs, sem))


def merge(own, bx, by, da, db, after=()):
    outs = [shape(4, *own.shape)]
    return run("merge", merge_kernel, [own, bx, by, da, db], outs, after, scratch=[pltpu.SemaphoreType.DMA((5,))])


def warm(weights, after):
    return run("warm", lambda *refs: None, weights, [], after)


def group_rows(refs):
    own, bx, by, da, db, c_own, c_bx, c_by, c_da, c_db = refs
    for ref in (own, c_own, bx, c_bx, by, c_by):
        yield ref[...]
    for top, bottom in ((da, db), (c_da, c_db)):
        yield jnp.concatenate([top[...], bottom[...]], axis=0)


def route(me, metas, rank_ref, prob_ref):
    expert = me.astype(F32)
    named, probs = [], []
    for meta in metas:
        meta = meta.astype(F32)
        first, second = meta[0:1] == expert, meta[1:2] == expert
        p0 = (meta[2:3] + meta[3:4]) + meta[4:5]
        p1 = (meta[5:6] + meta[6:7]) + meta[7:8]
        named.append((first | second).astype(F32))
        probs.append(jnp.where(first, p0, jnp.where(second, p1, 0.0)))
    named = jnp.concatenate(named, axis=0)
    count = named.shape[1]
    earlier = lax.broadcasted_iota(jnp.int32, (count, count), 0) < lax.broadcasted_iota(
        jnp.int32, (count, count), 1
    )
    rank = nn(named.astype(BF16), earlier.astype(F32).astype(BF16))
    rank_ref[...] = jnp.where(named > 0, rank, -1.0)
    prob_ref[...] = jnp.concatenate(probs, axis=0)


def slot_rows(rows, rank, prob, capacity):
    hit = lax.broadcasted_iota(jnp.int32, (capacity, rank.shape[1]), 0).astype(F32) == rank
    picked = nn(hit.astype(F32).astype(BF16), rows)
    if prob is not None:
        picked = picked * jnp.sum(jnp.where(hit, prob, 0.0), axis=1, keepdims=True)
    return picked.astype(BF16)


def slot_range(me, k, capacity):
    return pl.ds(pl.multiple_of(jnp.bitwise_xor(me, k) * capacity, capacity), capacity)


def activate(cols, x, wg_ref, wu_ref, h_ref):
    g, u = nn(x, wg_ref[:, cols]), nn(x, wu_ref[:, cols])
    s = jax.nn.sigmoid(g)
    b = g * s
    h_ref[:, cols] = (b * u).astype(BF16)
    return u * s * (1.0 + g * (1.0 - s)), b


def forward_kernel(capacity, pos_ref, *refs):
    wg_ref, wu_ref, x_ref, rank_ref, prob_ref, h_ref, a_ref, b_ref = refs[10:]
    count, me = rank_ref.shape[1], pos_ref[0]
    groups = list(group_rows(refs[:10]))
    route(me, [rows[count:, :count] for rows in groups], rank_ref, prob_ref)
    for k, rows in enumerate(groups):
        x_ref[slot_range(me, k, capacity), :] = slot_rows(rows[:count], rank_ref[k : k + 1], None, capacity)

    def step(cols):
        a_ref[:, cols], b_ref[:, cols] = activate(cols, x_ref[...], wg_ref, wu_ref, h_ref)

    tiles(wg_ref.shape[1], step)


def forward(pos, groups, w_gate, w_up, capacity, after):
    width, hid = w_gate.shape
    slots, count = 8 * capacity, groups[0].shape[0] - EXTRA
    return run(
        "forward",
        functools.partial(forward_kernel, capacity),
        [pos, *groups, w_gate, w_up],
        [shape(slots, width)]
        + [shape(8, count, dtype=F32)] * 2
        + [shape(slots, hid)]
        + [shape(slots, hid, dtype=F32)] * 2,
        after,
        held=[SMEM] + [VMEM] * 12,
        us=6,
    )


def far_down_kernel(capacity, pos_ref, *refs):
    rank_ref, prob_ref, h_ref, dy_ref, far_ref = refs[10:]
    for k, rows in enumerate(group_rows(refs[:10])):
        rank, prob = rank_ref[k : k + 1], prob_ref[k : k + 1]
        dy_ref[slot_range(pos_ref[0], k, capacity), :] = slot_rows(rows, rank, prob, capacity)
    far_ref[...] = tn(dy_ref[:, columns(pos_ref[1], far_ref.shape[0])], h_ref[...]).astype(BF16)


def far_down_of(pos, groups, rank, prob, h, chunk, capacity):
    width = groups[0].shape[1]
    slots, hid = h.shape
    return run(
        "far_down",
        functools.partial(far_down_kernel, capacity),
        [pos, *groups, rank, prob, h],
        [shape(slots, width), shape(chunk, hid)],
        held=[SMEM] + [VMEM] * 13,
        us=3,
    )


def retreat(cols, dy, wd_ref, a, b, dg_ref, du_ref):
    dh = nn(dy, wd_ref[:, cols])
    dg_ref[:, cols] = (dh * a).astype(BF16)
    du_ref[:, cols] = (dh * b).astype(BF16)


def backward_kernel(pos_ref, x_ref, dy_ref, a_ref, b_ref, h_ref, wd_ref, dg_ref, du_ref, *outs):
    def step(cols):
        retreat(cols, dy_ref[...], wd_ref, a_ref[:, cols], b_ref[:, cols], dg_ref, du_ref)

    tiles(wd_ref.shape[1], step)
    for n, out in enumerate(outs):
        at = columns(pos_ref[1 + (n + 1) // 3], out.shape[0])
        left, right = ((x_ref, dg_ref), (x_ref, du_ref), (dy_ref, h_ref))[n if n < 2 else (n - 2) % 3]
        out[...] = tn(left[:, at], right[...]).astype(out.dtype)


def backward(pos, x, dy, a, b, h, w_down, chunk, after):
    slots, hid = a.shape
    return run(
        "backward",
        backward_kernel,
        [pos, x, dy, a, b, h, w_down],
        [shape(slots, hid)] * 2 + [shape(chunk, hid)] * 5 + [shape(chunk, hid, dtype=F32)] * 3,
        after,
        held=[SMEM] + [VMEM] * 6,
        us=9,
    )


def add_kernel(p_ref, q_ref, out_ref):
    out_ref[...] = (p_ref[...].astype(F32) + q_ref[...].astype(F32)).astype(BF16)


def add(p, q, after=()):
    return run("add", add_kernel, [p, q], [shape(*p.shape)], after)


def rows_kernel(capacity, h_ref, dg_ref, du_ref, wd_ref, wg_ref, wu_ref, out_ref):
    groups = out_ref.shape[0]
    for r in cut_rows(wd_ref, 4):
        o = nt(h_ref[...], wd_ref[r, :]).astype(BF16)
        dx = (nt(dg_ref[...], wg_ref[r, :]) + nt(du_ref[...], wu_ref[r, :])).astype(BF16)
        for k in range(groups):
            at = slice(k * capacity, (k + 1) * capacity)
            out_ref[k, :capacity, r] = o[at]
            out_ref[k, capacity:, r] = dx[at]


def rows_back(h, dg, du, w_down, w_gate, w_up, capacity, after=()):
    slots, hid = h.shape
    return run(
        "rows_back",
        functools.partial(rows_kernel, capacity),
        [h, dg, du, w_down, w_gate, w_up],
        [shape(slots // capacity, 2 * capacity, w_gate.shape[0])],
        after,
        us=7,
    )


def combine_kernel(capacity, meta_ref, rows_ref, *refs):
    outs, (held_ref, mixed_ref, grad_ref, sem_in, sem_out) = refs[:2], refs[2:]
    parts, slots, part = held_ref.shape
    arrivals = []
    for n in range(parts):
        src = rows_ref.at[:, pl.ds(n * part, part)]
        arrivals += start_all([(src, held_ref.at[n])], sem_in.at[pl.ds(n, 1)])
    count = meta_ref.shape[1]
    same = lax.broadcasted_iota(jnp.int32, (EXTRA, EXTRA), 0) == lax.broadcasted_iota(jnp.int32, (EXTRA, EXTRA), 1)
    cols = tn(meta_ref[...], same.astype(F32).astype(BF16))
    ids = cols[:, 0:2].astype(jnp.int32)
    probs = [(cols[:, k : k + 1] + cols[:, k + 1 : k + 2]) + cols[:, k + 2 : k + 3] for k in (2, 5)]
    lane = lax.broadcasted_iota(jnp.int32, (count, 128), 1)
    named = ((lane == ids[:, 0:1]) | (lane == ids[:, 1:2])).astype(F32)
    earlier = lax.broadcasted_iota(jnp.int32, (count, count), 1) < lax.broadcasted_iota(
        jnp.int32, (count, count), 0
    )
    rank = nn(earlier.astype(F32).astype(BF16), named.astype(BF16))
    place = lax.broadcasted_iota(jnp.int32, (count, slots), 1)
    hits, both = [], 0.0
    for k in range(2):
        own = ids[:, k : k + 1]
        at = jnp.sum(jnp.where(lane == own, rank, 0.0), axis=1, keepdims=True).astype(jnp.int32)
        at = own * (2 * capacity) + at
        hits.append((place == at).astype(F32).astype(BF16))
        both = both + (place == at + capacity).astype(F32)
    both = both.astype(BF16)
    copies = []
    for n in range(parts):
        arrivals[n].wait()
        rows = held_ref[n]
        mixed_ref[n] = (nn(hits[0], rows) * probs[0] + nn(hits[1], rows) * probs[1]).astype(BF16)
        grad_ref[n] = nn(both, rows).astype(BF16)
        at = pl.ds(n * part, part)
        copies += start_all(
            [(ref.at[n], out.at[:, at]) for ref, out in zip((mixed_ref, grad_ref), outs)], sem_out.at[n]
        )
    wait_all(copies)


def combine(meta, rows, capacity, after=()):
    count = meta.shape[1]
    slots, width = rows.shape
    parts = 4
    return run(
        "combine",
        functools.partial(combine_kernel, capacity),
        [meta, rows],
        [shape(count, width)] * 2,
        after,
        held=[VMEM, ANY],
        out_held=[ANY] * 2,
        scratch=[pltpu.VMEM((parts, slots, width // parts), BF16)]
        + [pltpu.VMEM((parts, count, width // parts), BF16)] * 2
        + [pltpu.SemaphoreType.DMA((parts,)), pltpu.SemaphoreType.DMA((parts, 2))],
        us=5,
    )


def partner_kernel(capacity, pos_ref, own_ref, core_ref, wg_ref, wu_ref, wd_ref, *refs):
    x_ref, dy_ref, dg_ref, du_ref, h_ref, rank_ref, prob_ref = refs
    count = rank_ref.shape[1]
    groups = [(ref, k) for ref in (own_ref, core_ref) for k in range(4)]
    route(pos_ref[0], [ref[k, count : count + EXTRA, :count] for ref, k in groups], rank_ref, prob_ref)
    for n, ref in enumerate((own_ref, core_ref)):

        @pl.loop(0, 4)
        def _(k):
            at = pl.ds(pl.multiple_of((4 * n + k) * capacity, capacity), capacity)
            rank, prob = rank_ref[pl.ds(4 * n + k, 1), :], prob_ref[pl.ds(4 * n + k, 1), :]
            x_ref[at, :] = slot_rows(ref[k, :count], rank, None, capacity)
            dy_ref[at, :] = slot_rows(ref[k, count + EXTRA :], rank, prob, capacity)

    def step(cols):
        a, b = activate(cols, x_ref[...], wg_ref, wu_ref, h_ref)
        retreat(cols, dy_ref[...], wd_ref, a, b, dg_ref, du_ref)

    tiles(wg_ref.shape[1], step)


def partner(pos, own, core, weights, capacity, count, after):
    width, hid = weights[0].shape
    slots = 8 * capacity
    return run(
        "partner",
        functools.partial(partner_kernel, capacity),
        [pos, own, core, *weights],
        [shape(slots, width)] * 2 + [shape(slots, hid)] * 3,
        after,
        held=[SMEM] + [VMEM] * 5,
        scratch=[pltpu.VMEM((8, count), F32)] * 2,
        us=7,
    )


def both_kernel(pos_ref, x_ref, dy_ref, dg_ref, du_ref, h_ref, *refs):
    for left, right, own, out in zip((x_ref, x_ref, dy_ref), (dg_ref, du_ref, h_ref), refs[:3], refs[3:]):
        out[...] = own[...] + tn(left[:, columns(pos_ref[3], out.shape[0])], right[...])


def both(pos, slots, mine, after):
    return run(
        "both",
        both_kernel,
        [pos, *slots, *mine],
        [shape(*m.shape, dtype=F32) for m in mine],
        after,
        held=[SMEM] + [VMEM] * 8,
        us=3,
    )


def local_pairs(tokens, expert_ids, gate_probs, w_gate, w_up, w_down, out_grad):
    count, top = expert_ids.shape
    width = tokens.shape[1]
    w_gate, w_up, w_down = w_gate[0], w_up[0], w_down[0]
    planes, peers = lax.axis_size("dp"), lax.axis_size("expert")
    capacity = 2 * count * top // peers
    chunk, half = width // planes, count // 2
    z = lax.axis_index("dp")
    me = lax.axis_index("expert")
    left = z < 2
    far = jnp.where(left, 3, 0)
    near = jnp.where(left, 2, 1)
    pos = jnp.stack([me, far, near, z]).astype(jnp.int32)

    def over(x, bit):
        return lax.ppermute(x, "expert", [(i, i ^ bit) for i in range(peers)])

    def swap(x):
        return lax.ppermute(x, "dp", [(i, i ^ 1) for i in range(planes)])

    def inward(x):
        return lax.ppermute(x, "dp", [(0, 1), (3, 2)])

    def across_far(x):
        return lax.ppermute(x, "dp", [(1, 3), (2, 0)])

    def across_near(x):
        return lax.ppermute(x, "dp", [(1, 2), (2, 1)])

    def relay(bx, by, half, after=()):
        top, bottom, token = split(bx, by, half, after)
        return over(top, 2), over(bottom, 4), token

    def doubled(*held):
        return held + tuple(over(t, 1) for t in held)

    rows, grad, raw, meta, _ = pack(tokens, out_grad, expert_ids, gate_probs)
    raw = swap(raw)
    bx, by = over(rows, 2), over(rows, 4)
    da, db, token = relay(bx, by, half)
    groups = doubled(rows, bx, by, da, db)
    warmed = warm([w_gate, w_up, w_down], [token])
    grad = tie(grad, [da, db])
    bx, by = over(grad, 2), over(grad, 4)
    da, db, token = relay(bx, by, half)
    cotangents = doubled(grad, bx, by, da, db)
    raw = tie(raw, [da, db])
    raw_x, raw_y = over(raw, 2), over(raw, 4)

    x, rank, prob, h, a, b, token = forward(pos, groups, w_gate, w_up, capacity, warmed)
    dy, far_down, token = far_down_of(pos, cotangents, rank, prob, h, chunk, capacity)
    in_far_down = inward(far_down)
    dg, du, far_gate, far_up, near_gate, near_up, near_down, *mine, token = backward(
        pos, x, dy, a, b, h, w_down, chunk, [token]
    )
    in_far_gate = inward(far_gate)
    back, token = rows_back(h, dg, du, w_down, w_gate, w_up, capacity, [token])
    sum_far_down, token = add(far_down, in_far_down, [token])
    got_down = [across_far(sum_far_down)]
    in_far_up = inward(tie(far_up, [token]))
    raw_a, raw_b, token = relay(raw_x, raw_y, count + EXTRA, [token])
    sum_far_gate, token = add(far_gate, in_far_gate, [token])
    got_gate = [across_far(sum_far_gate)]
    in_near_down = inward(tie(near_down, [token]))
    back = lax.all_to_all(tie(back, [raw_a, raw_b]), "expert", split_axis=0, concat_axis=0, tiled=True)
    back = back.reshape(2 * peers * capacity, width)
    sum_far_up, token = add(far_up, in_far_up, [token, got_down[0]])
    got_up = [across_far(sum_far_up)]
    in_near_gate = inward(tie(near_gate, [token]))
    raw_own, token = merge(raw, raw_x, raw_y, raw_a, raw_b, [token])
    raw_core = over(raw_own, 1)
    sum_near_down, token = add(near_down, in_near_down, [token, got_gate[0]])
    got_down.append(across_near(sum_near_down))
    in_near_up = inward(tie(near_up, [token]))
    *slots, token = partner(pos, raw_own, raw_core, (w_gate, w_up, w_down), capacity, count, [token])
    *mine, token = both(pos, slots, mine, [token])
    sum_near_gate, token = add(near_gate, in_near_gate, [token, got_up[0]])
    got_gate.append(across_near(sum_near_gate))
    sum_near_up, token = add(near_up, in_near_up, [token, got_down[1]])
    got_up.append(across_near(sum_near_up))
    mixed, tokens_grad, token = combine(meta, back, capacity, [token])

    grads = []
    for own, got in zip(mine, (got_gate, got_up, got_down)):
        total = own + got[0].astype(F32) + got[1].astype(F32)
        grads.append(total.astype(BF16)[None])
    return (mixed, tokens_grad, *grads)


def solution(mesh):
    placed = (
        P(("dp", "expert"), None),
        P(("dp", "expert"), None),
        P(("dp", "expert"), None),
        P("expert", None, None),
        P("expert", None, None),
        P("expert", None, None),
        P(("dp", "expert"), None),
    )
    paired = mesh.shape["dp"] == 4 and mesh.shape["expert"] == 8
    return jax.shard_map(
        local_pairs if paired else local_any,
        mesh=mesh,
        in_specs=placed,
        out_specs=(
            P(("dp", "expert"), None),
            P(("dp", "expert"), None),
            P("expert", "dp", None),
            P("expert", "dp", None),
            P("expert", "dp", None),
        ),
        check_vma=False,
    )
```

```python
import functools

import jax
import jax.numpy as jnp
from jax import lax
from jax.experimental import pallas as pl
from jax.experimental.pallas import tpu as pltpu
from jax.sharding import PartitionSpec as P

F32 = jnp.float32
BF16 = jnp.bfloat16


def route_slots(expert_ids, experts, capacity):
    flat = expert_ids.reshape(-1)
    onehot = (flat[:, None] == jnp.arange(experts, dtype=jnp.int32)[None, :]).astype(jnp.int32)
    before = jnp.cumsum(onehot, axis=0) - onehot
    position = jnp.sum(before * onehot, axis=1)
    return flat * capacity + position


def local_any(tokens, expert_ids, gate_probs, w_gate, w_up, w_down, out_grad):
    token_count, top_count = expert_ids.shape
    width = tokens.shape[1]
    local_experts = w_gate.shape[0]
    peers = lax.axis_size("expert")
    experts = local_experts * peers
    capacity = max(2, 2 * token_count * top_count // experts)
    slot_total = experts * capacity
    route_total = token_count * top_count
    slot = route_slots(expert_ids, experts, capacity)
    owner = slot[None, :] == jnp.arange(slot_total, dtype=jnp.int32)[:, None]
    live = jnp.any(owner, axis=1)
    route_index = jnp.sum(
        jnp.where(owner, jnp.arange(route_total, dtype=jnp.int32)[None, :], 0), axis=1
    )
    token_of_slot = route_index // top_count
    slot_prob = jnp.sum(jnp.where(owner, gate_probs.reshape(-1)[None, :], 0.0), axis=1)
    dispatched = jnp.where(
        live[:, None], jnp.take(tokens, token_of_slot, axis=0), jnp.zeros((), tokens.dtype)
    )
    dispatched = dispatched.reshape(peers, local_experts, capacity, width)
    received = lax.all_to_all(dispatched, "expert", split_axis=0, concat_axis=0, tiled=True)
    gate_act = jnp.einsum("secd,edh->sech", received, w_gate, preferred_element_type=F32)
    up_act = jnp.einsum("secd,edh->sech", received, w_up, preferred_element_type=F32)
    hidden = (jax.nn.silu(gate_act) * up_act).astype(BF16)
    result = jnp.einsum("sech,edh->secd", hidden, w_down, preferred_element_type=F32).astype(BF16)
    returned = lax.all_to_all(result, "expert", split_axis=0, concat_axis=0, tiled=True)
    picked = jnp.take(returned.reshape(slot_total, width), slot, axis=0).astype(F32)
    picked = picked.reshape(token_count, top_count, width)
    mixed = jnp.sum(picked * gate_probs[:, :, None], axis=1).astype(BF16)
    dy_rows = jnp.where(
        live[:, None], jnp.take(out_grad, token_of_slot, axis=0), jnp.zeros((), out_grad.dtype)
    )
    dy_slot = (dy_rows.astype(F32) * slot_prob[:, None]).astype(BF16)
    dy_slot = dy_slot.reshape(peers, local_experts, capacity, width)
    dy_recv = lax.all_to_all(dy_slot, "expert", split_axis=0, concat_axis=0, tiled=True)
    d_hidden = jnp.einsum("secd,edh->sech", dy_recv, w_down, preferred_element_type=F32)
    sigma = jax.nn.sigmoid(gate_act)
    d_gate = (d_hidden * up_act * sigma * (1.0 + gate_act * (1.0 - sigma))).astype(BF16)
    d_up = (d_hidden * gate_act * sigma).astype(BF16)
    dx_slot = jnp.einsum("sech,edh->secd", d_gate, w_gate, preferred_element_type=F32)
    dx_slot = (
        dx_slot + jnp.einsum("sech,edh->secd", d_up, w_up, preferred_element_type=F32)
    ).astype(BF16)
    dx_back = lax.all_to_all(dx_slot, "expert", split_axis=0, concat_axis=0, tiled=True)
    dx_picked = jnp.take(dx_back.reshape(slot_total, width), slot, axis=0).astype(F32)
    tokens_grad = jnp.sum(dx_picked.reshape(token_count, top_count, width), axis=1).astype(BF16)
    first = jnp.einsum("secd,sech->deh", received, d_gate, preferred_element_type=F32)
    second = jnp.einsum("secd,sech->deh", received, d_up, preferred_element_type=F32)
    third = jnp.einsum("secd,sech->deh", dy_recv, hidden, preferred_element_type=F32)
    share = lax.psum_scatter(
        jnp.stack([first, second, third], axis=1).astype(BF16),
        "dp",
        scatter_dimension=0,
        tiled=True,
    )
    grads = [jnp.transpose(share[:, k], (1, 0, 2)) for k in range(3)]
    return (mixed, tokens_grad, *grads)


EXTRA = 16
TILE = 256
VMEM = pl.BlockSpec(memory_space=pltpu.VMEM)
SMEM = pl.BlockSpec(memory_space=pltpu.SMEM)
ANY = pl.BlockSpec(memory_space=pl.ANY)


def nn(a, b):
    return lax.dot_general(a, b, (((1,), (0,)), ((), ())), preferred_element_type=F32)


def nt(a, b):
    return lax.dot_general(a, b, (((1,), (1,)), ((), ())), preferred_element_type=F32)


def tn(a, b):
    return lax.dot_general(a, b, (((0,), (0,)), ((), ())), preferred_element_type=F32)


def shape(*sizes, dtype=BF16):
    return jax.ShapeDtypeStruct(sizes, dtype)


def run(name, kernel, operands, outs, after=(), held=None, out_held=None, scratch=(), us=1.0, limit=11):
    skip, count = len(after), len(operands) + len(outs)

    def body(*refs):
        refs = refs[skip:]
        kernel(*refs[:count], *refs[count + 1 :])

    return pl.pallas_call(
        body,
        in_specs=[ANY] * skip + list(held or [VMEM] * len(operands)),
        out_specs=list(out_held or [VMEM] * len(outs)) + [VMEM],
        out_shape=list(outs) + [shape(8, 128, dtype=F32)],
        scratch_shapes=list(scratch),
        compiler_params=pltpu.CompilerParams(vmem_limit_bytes=limit * 1024 * 1024),
        cost_estimate=pl.CostEstimate(flops=int(us * 1e9), bytes_accessed=1 << 16, transcendentals=0),
        name=name,
    )(*after, *operands)


def tie(x, after):
    return pl.pallas_call(
        lambda *refs: None,
        in_specs=[ANY] * (1 + len(after)),
        out_specs=ANY,
        out_shape=jax.ShapeDtypeStruct(x.shape, x.dtype),
        input_output_aliases={0: 0},
        compiler_params=pltpu.CompilerParams(vmem_limit_bytes=1024 * 1024),
        cost_estimate=pl.CostEstimate(flops=8, bytes_accessed=8, transcendentals=0),
        name="tie",
    )(x, *after)


def tiles(size, body, tile=TILE):
    @pl.loop(0, size // tile)
    def _(i):
        body(pl.ds(pl.multiple_of(i * tile, tile), tile))


def columns(start, size):
    return pl.ds(pl.multiple_of(start * size, size), size)


def start_all(pairs, sem):
    copies = [pltpu.make_async_copy(src, dst, sem.at[n]) for n, (src, dst) in enumerate(pairs)]
    for copy in copies:
        copy.start()
    return copies


def wait_all(copies):
    for copy in copies:
        copy.wait()


def cut_rows(ref, parts):
    size = ref.shape[0] // parts
    return [pl.ds(n * size, size) for n in range(parts)]


def pack_kernel(pos_ref, tokens_in, grad_in, ids_in, prob_in, out_ref, rows_ref, far_ref, rest_ref, raw_ref, meta_ref, ids_ref, prob_ref, sem):
    count, width = tokens_in.shape
    for n in range(pos_ref.shape[0]):
        out_ref[n] = pos_ref[n]
    small = start_all([(ids_in, ids_ref), (prob_in, prob_ref)], sem.at[0])
    chunk, rest = far_ref.shape[1], rest_ref.shape[1]
    others = pl.ds(pl.multiple_of(jnp.where(pos_ref[1] == 0, chunk, 0), chunk), rest)
    pairs = []
    for r in cut_rows(tokens_in, 2):
        pairs.append((tokens_in.at[r, :], rows_ref.at[r, :]))
        pairs.append((tokens_in.at[r, :], raw_ref.at[r, :]))
        pairs.append((grad_in.at[r, :], raw_ref.at[pl.ds(count + EXTRA + r.start, r.size), :]))
    pairs.append((grad_in.at[:, columns(pos_ref[1], chunk)], far_ref))
    pairs.append((grad_in.at[:, others], rest_ref))
    copies = start_all(pairs, sem.at[1])
    wait_all(small)
    rows = [ids_ref[...].astype(F32)]
    for k in range(2):
        rest = prob_ref[k : k + 1, :]
        for _ in range(3):
            rows.append(rest.astype(BF16).astype(F32))
            rest = rest - rows[-1]
    meta = jnp.concatenate(rows + [jnp.zeros((EXTRA - 8, count), F32)], axis=0).astype(BF16)
    meta_ref[...] = meta
    behind = pl.ds(count, EXTRA)
    for ref in (rows_ref, raw_ref):
        ref[behind, :count] = meta
        ref[behind, count:] = jnp.zeros((EXTRA, width - count), BF16)
    wait_all(copies)


def pack(pos, tokens, grad, ids, probs, chunk):
    count, width = tokens.shape
    return run(
        "pack",
        pack_kernel,
        [pos, tokens, grad, ids.T, probs.T],
        [shape(*pos.shape, dtype=jnp.int32), shape(count + EXTRA, width)]
        + [shape(count, chunk), shape(count, width - chunk)]
        + [shape(2 * count + EXTRA, width), shape(EXTRA, count)],
        held=[SMEM] + [ANY] * 4,
        out_held=[SMEM] + [VMEM] * 5,
        limit=4,
        scratch=[pltpu.VMEM((2, count), jnp.int32), pltpu.VMEM((2, count), F32), pltpu.SemaphoreType.DMA((2, 8))],
    )


def split_kernel(bx_ref, by_ref, top_ref, bottom_ref):
    half = top_ref.shape[0]
    top_ref[...] = by_ref[:half]
    bottom_ref[...] = bx_ref[half:]


def split(bx, by, half, after=()):
    rows, width = bx.shape
    return run("split", split_kernel, [bx, by], [shape(half, width), shape(rows - half, width)], after, limit=4)


def warm(weights, after):
    return run("warm", lambda *refs: None, weights, [], after, limit=11)


def group_rows(refs):
    own, bx, by, da, db, c_own, c_bx, c_by, c_da, c_db = refs
    for ref in (own, c_own, bx, c_bx, by, c_by):
        yield ref[...]
    for top, bottom in ((da, db), (c_da, c_db)):
        yield jnp.concatenate([top[...], bottom[...]], axis=0)


def route(me, metas, rank_ref, prob_ref):
    expert = me.astype(F32)
    named, probs = [], []
    for meta in metas:
        meta = meta.astype(F32)
        first, second = meta[0:1] == expert, meta[1:2] == expert
        p0 = (meta[2:3] + meta[3:4]) + meta[4:5]
        p1 = (meta[5:6] + meta[6:7]) + meta[7:8]
        named.append((first | second).astype(F32))
        probs.append(jnp.where(first, p0, jnp.where(second, p1, 0.0)))
    named = jnp.concatenate(named, axis=0)
    count = named.shape[1]
    earlier = lax.broadcasted_iota(jnp.int32, (count, count), 0) < lax.broadcasted_iota(
        jnp.int32, (count, count), 1
    )
    rank = nn(named.astype(BF16), earlier.astype(F32).astype(BF16))
    rank_ref[...] = jnp.where(named > 0, rank, -1.0)
    prob_ref[...] = jnp.concatenate(probs, axis=0)


def slot_rows(rows, rank, prob, capacity):
    hit = lax.broadcasted_iota(jnp.int32, (capacity, rank.shape[1]), 0).astype(F32) == rank
    picked = nn(hit.astype(F32).astype(BF16), rows)
    if prob is not None:
        picked = picked * jnp.sum(jnp.where(hit, prob, 0.0), axis=1, keepdims=True)
    return picked.astype(BF16)


def slot_range(me, k, capacity):
    return pl.ds(pl.multiple_of(jnp.bitwise_xor(me, k) * capacity, capacity), capacity)


def activate(cols, x, wg_ref, wu_ref, h_ref):
    g, u = nn(x, wg_ref[:, cols]), nn(x, wu_ref[:, cols])
    s = jax.nn.sigmoid(g)
    b = g * s
    h_ref[:, cols] = (b * u).astype(BF16)
    return u * s * (1.0 + g * (1.0 - s)), b


def forward_kernel(capacity, pos_ref, *refs):
    wg_ref, wu_ref, x_ref, rank_ref, prob_ref, h_ref, a_ref, b_ref = refs[10:]
    count, me = rank_ref.shape[1], pos_ref[0]
    groups = list(group_rows(refs[:10]))
    route(me, [rows[count:, :count] for rows in groups], rank_ref, prob_ref)
    for k, rows in enumerate(groups):
        x_ref[slot_range(me, k, capacity), :] = slot_rows(rows[:count], rank_ref[k : k + 1], None, capacity)

    def step(cols):
        a_ref[:, cols], b_ref[:, cols] = activate(cols, x_ref[...], wg_ref, wu_ref, h_ref)

    tiles(wg_ref.shape[1], step)


def forward(pos, groups, w_gate, w_up, capacity, after):
    width, hid = w_gate.shape
    slots, count = 8 * capacity, groups[0].shape[0] - EXTRA
    return run(
        "forward",
        functools.partial(forward_kernel, capacity),
        [pos, *groups, w_gate, w_up],
        [shape(slots, width)]
        + [shape(8, count, dtype=F32)] * 2
        + [shape(slots, hid)]
        + [shape(slots, hid, dtype=F32)] * 2,
        after,
        held=[SMEM] + [VMEM] * 12,
        us=6,
    )


def far_down_kernel(capacity, pos_ref, *refs):
    rank_ref, prob_ref, h_ref, dy_ref, far_ref = refs[8:]
    for k, ref in enumerate(refs[:8]):
        rank, prob = rank_ref[k : k + 1], prob_ref[k : k + 1]
        dy_ref[slot_range(pos_ref[0], k, capacity), :] = slot_rows(ref[...], rank, prob, capacity)
    far_ref[...] = tn(dy_ref[...], h_ref[...]).astype(BF16)


def far_down_of(pos, groups, rank, prob, h, capacity):
    chunk = groups[0].shape[1]
    slots, hid = h.shape
    return run(
        "far_down",
        functools.partial(far_down_kernel, capacity),
        [pos, *groups, rank, prob, h],
        [shape(slots, chunk), shape(chunk, hid)],
        held=[SMEM] + [VMEM] * 11,
        us=3,
    )


def retreat(cols, dy, wd_ref, a, b, dg_ref, du_ref):
    dh = nn(dy, wd_ref[:, cols])
    dg_ref[:, cols] = (dh * a).astype(BF16)
    du_ref[:, cols] = (dh * b).astype(BF16)


def backward_kernel(capacity, pos_ref, *refs):
    far_ref, rank_ref, prob_ref, x_ref, a_ref, b_ref, wd_ref, dy_ref, dg_ref, du_ref, out_ref = refs[10:]
    chunk, rest = far_ref.shape[1], refs[0].shape[1]
    far = columns(pos_ref[1], chunk)
    dy_ref[:, far] = far_ref[...]
    others = pl.ds(pl.multiple_of(jnp.where(pos_ref[1] == 0, chunk, 0), chunk), rest)
    for k, rows in enumerate(group_rows(refs[:10])):
        rank, prob = rank_ref[k : k + 1], prob_ref[k : k + 1]
        dy_ref[slot_range(pos_ref[0], k, capacity), others] = slot_rows(rows, rank, prob, capacity)

    def step(cols):
        retreat(cols, dy_ref[...], wd_ref, a_ref[:, cols], b_ref[:, cols], dg_ref, du_ref)
        out_ref[:, cols] = tn(x_ref[:, far], dg_ref[:, cols]).astype(BF16)

    tiles(wd_ref.shape[1], step)


def backward(pos, groups, far_rows, rank, prob, x, a, b, w_down, capacity, after):
    slots, hid = a.shape
    width, chunk = x.shape[1], far_rows.shape[1]
    return run(
        "backward",
        functools.partial(backward_kernel, capacity),
        [pos, *groups, far_rows, rank, prob, x, a, b, w_down],
        [shape(slots, width)] + [shape(slots, hid)] * 2 + [shape(chunk, hid)],
        after,
        held=[SMEM] + [VMEM] * 17,
        us=1,
        limit=12,
    )


def gradients_kernel(pos_ref, x_ref, dy_ref, dg_ref, du_ref, h_ref, *outs):
    for n, out in enumerate(outs):
        at = columns(pos_ref[1 + (n + 2) // 3], out.shape[0])
        left, right = ((x_ref, dg_ref), (x_ref, du_ref), (dy_ref, h_ref))[1 if n == 0 else (n - 1) % 3]
        out[...] = tn(left[:, at], right[...]).astype(out.dtype)


def gradients(pos, x, dy, dg, du, h, chunk, after):
    return run(
        "gradients",
        gradients_kernel,
        [pos, x, dy, dg, du, h],
        [shape(chunk, h.shape[1])] * 7,
        after,
        held=[SMEM] + [VMEM] * 5,
        us=0.5,
    )


def step_kernel(extra, pos_ref, raw_ref, mine_ref, got_ref, *refs):
    out_ref = refs[-1 - extra[1]]
    total = (mine_ref[...].astype(F32) + got_ref[...].astype(F32)).astype(BF16)
    out_ref[...] = jnp.where(pos_ref[4] == 1, raw_ref[...], total)
    if extra == (2, 2):
        bx_ref, by_ref, _, top_ref, bottom_ref = refs
        half = top_ref.shape[0]
        top_ref[...] = by_ref[:half]
        bottom_ref[...] = bx_ref[half:]
    if extra == (5, 1):
        half = refs[3].shape[0]
        for k in range(3):
            refs[-1][k] = refs[k][...]
        refs[-1][3, :half] = refs[3][...]
        refs[-1][3, half:] = refs[4][...]


def step(pos, raw, mine, got, after, extra=(), outs=()):
    return run(
        "step",
        functools.partial(step_kernel, (len(extra), len(outs))),
        [pos, raw, mine, got, *extra],
        [shape(*mine.shape), *outs],
        after,
        held=[SMEM] + [VMEM] * (3 + len(extra)),
        us=8,
        limit=14 if extra else 6,
    )


def rows_kernel(capacity, h_ref, dg_ref, du_ref, wd_ref, wg_ref, wu_ref, out_ref):
    groups = out_ref.shape[0]
    for r in cut_rows(wd_ref, 4):
        o = nt(h_ref[...], wd_ref[r, :]).astype(BF16)
        dx = (nt(dg_ref[...], wg_ref[r, :]) + nt(du_ref[...], wu_ref[r, :])).astype(BF16)
        for k in range(groups):
            at = slice(k * capacity, (k + 1) * capacity)
            out_ref[k, :capacity, r] = o[at]
            out_ref[k, capacity:, r] = dx[at]


def rows_back(h, dg, du, w_down, w_gate, w_up, capacity, after=()):
    slots, hid = h.shape
    return run(
        "rows_back",
        functools.partial(rows_kernel, capacity),
        [h, dg, du, w_down, w_gate, w_up],
        [shape(slots // capacity, 2 * capacity, w_gate.shape[0])],
        after,
        us=7,
    )


def combine_kernel(capacity, meta_ref, rows_ref, *refs):
    outs, (held_ref, mixed_ref, grad_ref, sem_in, sem_out) = refs[:2], refs[2:]
    parts, slots, part = held_ref.shape
    arrivals = []
    for n in range(parts):
        src = rows_ref.at[:, pl.ds(n * part, part)]
        arrivals += start_all([(src, held_ref.at[n])], sem_in.at[pl.ds(n, 1)])
    count = meta_ref.shape[1]
    same = lax.broadcasted_iota(jnp.int32, (EXTRA, EXTRA), 0) == lax.broadcasted_iota(jnp.int32, (EXTRA, EXTRA), 1)
    cols = tn(meta_ref[...], same.astype(F32).astype(BF16))
    ids = cols[:, 0:2].astype(jnp.int32)
    probs = [(cols[:, k : k + 1] + cols[:, k + 1 : k + 2]) + cols[:, k + 2 : k + 3] for k in (2, 5)]
    lane = lax.broadcasted_iota(jnp.int32, (count, 128), 1)
    named = ((lane == ids[:, 0:1]) | (lane == ids[:, 1:2])).astype(F32)
    earlier = lax.broadcasted_iota(jnp.int32, (count, count), 1) < lax.broadcasted_iota(
        jnp.int32, (count, count), 0
    )
    rank = nn(earlier.astype(F32).astype(BF16), named.astype(BF16))
    place = lax.broadcasted_iota(jnp.int32, (count, slots), 1)
    hits, both = [], 0.0
    for k in range(2):
        own = ids[:, k : k + 1]
        at = jnp.sum(jnp.where(lane == own, rank, 0.0), axis=1, keepdims=True).astype(jnp.int32)
        at = own * (2 * capacity) + at
        hits.append((place == at).astype(F32).astype(BF16))
        both = both + (place == at + capacity).astype(F32)
    both = both.astype(BF16)
    copies = []
    for n in range(parts):
        arrivals[n].wait()
        rows = held_ref[n]
        mixed_ref[n] = (nn(hits[0], rows) * probs[0] + nn(hits[1], rows) * probs[1]).astype(BF16)
        grad_ref[n] = nn(both, rows).astype(BF16)
        at = pl.ds(n * part, part)
        copies += start_all(
            [(ref.at[n], out.at[:, at]) for ref, out in zip((mixed_ref, grad_ref), outs)], sem_out.at[n]
        )
    wait_all(copies)


def combine(meta, rows, capacity, after=()):
    count = meta.shape[1]
    slots, width = rows.shape
    parts = 4
    return run(
        "combine",
        functools.partial(combine_kernel, capacity),
        [meta, rows],
        [shape(count, width)] * 2,
        after,
        held=[VMEM, ANY],
        out_held=[ANY] * 2,
        scratch=[pltpu.VMEM((parts, slots, width // parts), BF16)]
        + [pltpu.VMEM((parts, count, width // parts), BF16)] * 2
        + [pltpu.SemaphoreType.DMA((parts,)), pltpu.SemaphoreType.DMA((parts, 2))],
        us=5,
    )


def partner_kernel(capacity, pos_ref, own_ref, core_ref, wg_ref, wu_ref, wd_ref, *refs):
    x_ref, dy_ref, dg_ref, du_ref, h_ref, rank_ref, prob_ref = refs
    count = rank_ref.shape[1]
    groups = [(ref, k) for ref in (own_ref, core_ref) for k in range(4)]
    route(pos_ref[0], [ref[k, count : count + EXTRA, :count] for ref, k in groups], rank_ref, prob_ref)
    for n, ref in enumerate((own_ref, core_ref)):

        @pl.loop(0, 4)
        def _(k):
            at = pl.ds(pl.multiple_of((4 * n + k) * capacity, capacity), capacity)
            rank, prob = rank_ref[pl.ds(4 * n + k, 1), :], prob_ref[pl.ds(4 * n + k, 1), :]
            x_ref[at, :] = slot_rows(ref[k, :count], rank, None, capacity)
            dy_ref[at, :] = slot_rows(ref[k, count + EXTRA :], rank, prob, capacity)

    def step(cols):
        a, b = activate(cols, x_ref[...], wg_ref, wu_ref, h_ref)
        retreat(cols, dy_ref[...], wd_ref, a, b, dg_ref, du_ref)

    tiles(wg_ref.shape[1], step)


def partner(pos, own, core, weights, capacity, count, after):
    width, hid = weights[0].shape
    slots = 8 * capacity
    return run(
        "partner",
        functools.partial(partner_kernel, capacity),
        [pos, own, core, *weights],
        [shape(slots, width)] * 2 + [shape(slots, hid)] * 3,
        after,
        held=[SMEM] + [VMEM] * 5,
        scratch=[pltpu.VMEM((8, count), F32)] * 2,
        us=7,
    )


def both_kernel(pos_ref, x_ref, dy_ref, dg_ref, du_ref, h_ref, *refs):
    for left, right, own, out in zip((x_ref, x_ref, dy_ref), (dg_ref, du_ref, h_ref), refs[:3], refs[3:]):
        total = own[...].astype(F32) + tn(left[:, columns(pos_ref[3], out.shape[0])], right[...])
        out[...] = total.astype(BF16)


def both(pos, slots, mine, after):
    return run(
        "both",
        both_kernel,
        [pos, *slots, *mine],
        [shape(*m.shape) for m in mine],
        after,
        held=[SMEM] + [VMEM] * 8,
        us=3,
    )


def local_pairs(tokens, expert_ids, gate_probs, w_gate, w_up, w_down, out_grad):
    count, top = expert_ids.shape
    width = tokens.shape[1]
    w_gate, w_up, w_down = w_gate[0], w_up[0], w_down[0]
    planes, peers = lax.axis_size("dp"), lax.axis_size("expert")
    capacity = 2 * count * top // peers
    chunk, half = width // planes, count // 2
    z = lax.axis_index("dp")
    me = lax.axis_index("expert")
    left = z < 2
    far = jnp.where(left, 3, 0)
    near = jnp.where(left, 2, 1)
    outer = ((z == 0) | (z == planes - 1)).astype(jnp.int32)
    pos = jnp.stack([me, far, near, z, outer]).astype(jnp.int32)

    def over(x, bit):
        return lax.ppermute(x, "expert", [(i, i ^ bit) for i in range(peers)])

    def swap(x):
        return lax.ppermute(x, "dp", [(i, i ^ 1) for i in range(planes)])

    inwards, across, middle = [(0, 1), (3, 2)], [(1, 3), (2, 0)], [(1, 2), (2, 1)]

    def along(x, pairs):
        return lax.ppermute(x, "dp", pairs)

    def relay(bx, by, half, after=()):
        top, bottom, token = split(bx, by, half, after)
        return over(top, 2), over(bottom, 4), token

    def doubled(*held):
        return held + tuple(over(t, 1) for t in held)

    pos, rows, far_grad, rest_grad, raw, meta, _ = pack(pos, tokens, out_grad, expert_ids, gate_probs, chunk)
    raw = swap(raw)
    bx, by = over(rows, 2), over(rows, 4)
    warmed = warm([w_gate, w_up, w_down], [meta])
    da, db, token = relay(bx, by, half, warmed)
    groups = doubled(rows, bx, by, da, db)
    far_grad = tie(far_grad, [da, db, raw])
    far_groups = []
    for f in (far_grad, over(far_grad, 2), over(far_grad, 4), over(far_grad, 6)):
        far_groups += [f, over(f, 1)]
    rest_grad = tie(rest_grad, [da, db])
    bx, by = over(rest_grad, 2), over(rest_grad, 4)
    x, rank, prob, h, a, b, token = forward(pos, groups, w_gate, w_up, capacity, [])
    far_rows, far_down, token = far_down_of(pos, far_groups, rank, prob, h, capacity)
    da, db, _ = relay(bx, by, half, [token])
    rest_groups = doubled(rest_grad, bx, by, da, db)
    raw = tie(raw, [da, db])
    raw_x, raw_y = over(raw, 2), over(raw, 4)

    y1 = along(far_down, inwards)
    dy, dg, du, far_gate, token = backward(
        pos, rest_groups, far_rows, rank, prob, x, a, b, w_down, capacity, [token]
    )
    y2 = along(far_gate, inwards)
    far_up, near_gate, near_up, near_down, *mine, token = gradients(pos, x, dy, dg, du, h, chunk, [y1])
    halves = [shape(count + EXTRA, width), shape(count, width)]
    x3, top, bottom, token = step(pos, far_up, far_down, y1, [token], [raw_x, raw_y], halves)
    y3 = along(x3, inwards + across)
    raw_a, raw_b = over(top, 2), over(bottom, 4)
    back, _ = rows_back(h, dg, du, w_down, w_gate, w_up, capacity)
    back = lax.all_to_all(back, "expert", split_axis=0, concat_axis=0, tiled=True)
    x4, token = step(pos, near_down, far_gate, y2, [token])
    y4 = along(x4, inwards + across)
    blocks = [raw, raw_x, raw_y, raw_a, raw_b]
    x5, raw_own, token = step(pos, near_gate, far_up, y3, [token], blocks, [shape(4, *raw.shape)])
    y5 = along(x5, inwards + across)
    near_up = tie(near_up, [token])
    y6 = along(near_up, inwards)
    raw_core = over(raw_own, 1)
    x6, token = step(pos, near_down, near_down, y4, [token])
    z_down = along(x6, middle)
    x7, token = step(pos, near_gate, near_gate, y5, [token])
    z_gate = along(x7, middle)
    *slots, token = partner(pos, raw_own, raw_core, (w_gate, w_up, w_down), capacity, count, [token])
    x8, token = step(pos, near_up, near_up, y6, [token])
    z_up = along(x8, middle)
    *mine, _ = both(pos, slots, mine, [token])
    mixed, tokens_grad, _ = combine(meta, back.reshape(2 * peers * capacity, width), capacity, [token])

    grads = []
    for own, far_sum, near_sum in zip(mine, (y4, y5, y3), (z_gate, z_up, z_down)):
        total = own.astype(F32) + jnp.where(outer == 1, far_sum, near_sum).astype(F32)
        grads.append(total.astype(BF16)[None])
    return (mixed, tokens_grad, *grads)


def solution(mesh):
    placed = (
        P(("dp", "expert"), None),
        P(("dp", "expert"), None),
        P(("dp", "expert"), None),
        P("expert", None, None),
        P("expert", None, None),
        P("expert", None, None),
        P(("dp", "expert"), None),
    )
    paired = mesh.shape["dp"] == 4 and mesh.shape["expert"] == 8
    return jax.shard_map(
        local_pairs if paired else local_any,
        mesh=mesh,
        in_specs=placed,
        out_specs=(
            P(("dp", "expert"), None),
            P(("dp", "expert"), None),
            P("expert", "dp", None),
            P("expert", "dp", None),
            P("expert", "dp", None),
        ),
        check_vma=False,
    )
```

```python
import functools

import jax
import jax.numpy as jnp
from jax import lax
from jax.experimental import pallas as pl
from jax.experimental.pallas import tpu as pltpu
from jax.sharding import PartitionSpec as P

F32 = jnp.float32
BF16 = jnp.bfloat16


def route_slots(expert_ids, experts, capacity):
    flat = expert_ids.reshape(-1)
    onehot = (flat[:, None] == jnp.arange(experts, dtype=jnp.int32)[None, :]).astype(jnp.int32)
    before = jnp.cumsum(onehot, axis=0) - onehot
    position = jnp.sum(before * onehot, axis=1)
    return flat * capacity + position


def local_any(tokens, expert_ids, gate_probs, w_gate, w_up, w_down, out_grad):
    token_count, top_count = expert_ids.shape
    width = tokens.shape[1]
    local_experts = w_gate.shape[0]
    peers = lax.axis_size("expert")
    experts = local_experts * peers
    capacity = max(2, 2 * token_count * top_count // experts)
    slot_total = experts * capacity
    route_total = token_count * top_count
    slot = route_slots(expert_ids, experts, capacity)
    owner = slot[None, :] == jnp.arange(slot_total, dtype=jnp.int32)[:, None]
    live = jnp.any(owner, axis=1)
    route_index = jnp.sum(
        jnp.where(owner, jnp.arange(route_total, dtype=jnp.int32)[None, :], 0), axis=1
    )
    token_of_slot = route_index // top_count
    slot_prob = jnp.sum(jnp.where(owner, gate_probs.reshape(-1)[None, :], 0.0), axis=1)
    dispatched = jnp.where(
        live[:, None], jnp.take(tokens, token_of_slot, axis=0), jnp.zeros((), tokens.dtype)
    )
    dispatched = dispatched.reshape(peers, local_experts, capacity, width)
    received = lax.all_to_all(dispatched, "expert", split_axis=0, concat_axis=0, tiled=True)
    gate_act = jnp.einsum("secd,edh->sech", received, w_gate, preferred_element_type=F32)
    up_act = jnp.einsum("secd,edh->sech", received, w_up, preferred_element_type=F32)
    hidden = (jax.nn.silu(gate_act) * up_act).astype(BF16)
    result = jnp.einsum("sech,edh->secd", hidden, w_down, preferred_element_type=F32).astype(BF16)
    returned = lax.all_to_all(result, "expert", split_axis=0, concat_axis=0, tiled=True)
    picked = jnp.take(returned.reshape(slot_total, width), slot, axis=0).astype(F32)
    picked = picked.reshape(token_count, top_count, width)
    mixed = jnp.sum(picked * gate_probs[:, :, None], axis=1).astype(BF16)
    dy_rows = jnp.where(
        live[:, None], jnp.take(out_grad, token_of_slot, axis=0), jnp.zeros((), out_grad.dtype)
    )
    dy_slot = (dy_rows.astype(F32) * slot_prob[:, None]).astype(BF16)
    dy_slot = dy_slot.reshape(peers, local_experts, capacity, width)
    dy_recv = lax.all_to_all(dy_slot, "expert", split_axis=0, concat_axis=0, tiled=True)
    d_hidden = jnp.einsum("secd,edh->sech", dy_recv, w_down, preferred_element_type=F32)
    sigma = jax.nn.sigmoid(gate_act)
    d_gate = (d_hidden * up_act * sigma * (1.0 + gate_act * (1.0 - sigma))).astype(BF16)
    d_up = (d_hidden * gate_act * sigma).astype(BF16)
    dx_slot = jnp.einsum("sech,edh->secd", d_gate, w_gate, preferred_element_type=F32)
    dx_slot = (
        dx_slot + jnp.einsum("sech,edh->secd", d_up, w_up, preferred_element_type=F32)
    ).astype(BF16)
    dx_back = lax.all_to_all(dx_slot, "expert", split_axis=0, concat_axis=0, tiled=True)
    dx_picked = jnp.take(dx_back.reshape(slot_total, width), slot, axis=0).astype(F32)
    tokens_grad = jnp.sum(dx_picked.reshape(token_count, top_count, width), axis=1).astype(BF16)
    first = jnp.einsum("secd,sech->deh", received, d_gate, preferred_element_type=F32)
    second = jnp.einsum("secd,sech->deh", received, d_up, preferred_element_type=F32)
    third = jnp.einsum("secd,sech->deh", dy_recv, hidden, preferred_element_type=F32)
    share = lax.psum_scatter(
        jnp.stack([first, second, third], axis=1).astype(BF16),
        "dp",
        scatter_dimension=0,
        tiled=True,
    )
    grads = [jnp.transpose(share[:, k], (1, 0, 2)) for k in range(3)]
    return (mixed, tokens_grad, *grads)


EXTRA = 16
TILE = 256
VMEM = pl.BlockSpec(memory_space=pltpu.VMEM)
SMEM = pl.BlockSpec(memory_space=pltpu.SMEM)
ANY = pl.BlockSpec(memory_space=pl.ANY)


def nn(a, b):
    return lax.dot_general(a, b, (((1,), (0,)), ((), ())), preferred_element_type=F32)


def nt(a, b):
    return lax.dot_general(a, b, (((1,), (1,)), ((), ())), preferred_element_type=F32)


def tn(a, b):
    return lax.dot_general(a, b, (((0,), (0,)), ((), ())), preferred_element_type=F32)


def shape(*sizes, dtype=BF16):
    return jax.ShapeDtypeStruct(sizes, dtype)


def run(name, kernel, operands, outs, after=(), held=None, out_held=None, scratch=(), us=1.0, limit=11):
    skip, count = len(after), len(operands) + len(outs)

    def body(*refs):
        refs = refs[skip:]
        kernel(*refs[:count], *refs[count + 1 :])

    return pl.pallas_call(
        body,
        in_specs=[ANY] * skip + list(held or [VMEM] * len(operands)),
        out_specs=list(out_held or [VMEM] * len(outs)) + [VMEM],
        out_shape=list(outs) + [shape(8, 128, dtype=F32)],
        scratch_shapes=list(scratch),
        compiler_params=pltpu.CompilerParams(vmem_limit_bytes=limit * 1024 * 1024),
        cost_estimate=pl.CostEstimate(flops=int(us * 50e7), bytes_accessed=1 << 10, transcendentals=0),
        name=name,
    )(*after, *operands)


def tie(x, after):
    return pl.pallas_call(
        lambda *refs: None,
        in_specs=[ANY] * (1 + len(after)),
        out_specs=ANY,
        out_shape=jax.ShapeDtypeStruct(x.shape, x.dtype),
        input_output_aliases={0: 0},
        compiler_params=pltpu.CompilerParams(vmem_limit_bytes=1024 * 1024),
        cost_estimate=pl.CostEstimate(flops=8, bytes_accessed=8, transcendentals=0),
        name="tie",
    )(x, *after)


def tiles(size, body, tile=TILE):
    @pl.loop(0, size // tile)
    def _(i):
        body(pl.ds(pl.multiple_of(i * tile, tile), tile))


def columns(start, size):
    return pl.ds(pl.multiple_of(start * size, size), size)


def start_all(pairs, sem):
    copies = [pltpu.make_async_copy(src, dst, sem.at[n]) for n, (src, dst) in enumerate(pairs)]
    for copy in copies:
        copy.start()
    return copies


def wait_all(copies):
    for copy in copies:
        copy.wait()


def cut_rows(ref, parts):
    size = ref.shape[0] // parts
    return [pl.ds(n * size, size) for n in range(parts)]


def pack_kernel(pos_ref, tokens_in, grad_in, ids_in, prob_in, out_ref, rows_ref, far_ref, rest_ref, raw_ref, meta_ref, ids_ref, prob_ref, sem):
    count, width = tokens_in.shape
    for n in range(pos_ref.shape[0]):
        out_ref[n] = pos_ref[n]
    small = start_all([(ids_in, ids_ref), (prob_in, prob_ref)], sem.at[0])
    chunk, rest = far_ref.shape[1], rest_ref.shape[1]
    others = pl.ds(pl.multiple_of(jnp.where(pos_ref[1] == 0, chunk, 0), chunk), rest)
    pairs = []
    for r in cut_rows(tokens_in, 2):
        pairs.append((tokens_in.at[r, :], rows_ref.at[r, :]))
        pairs.append((tokens_in.at[r, :], raw_ref.at[r, :]))
        pairs.append((grad_in.at[r, :], raw_ref.at[pl.ds(count + EXTRA + r.start, r.size), :]))
    pairs.append((grad_in.at[:, columns(pos_ref[1], chunk)], far_ref))
    pairs.append((grad_in.at[:, others], rest_ref))
    copies = start_all(pairs, sem.at[1])
    wait_all(small)
    rows = [ids_ref[...].astype(F32)]
    for k in range(2):
        rest = prob_ref[k : k + 1, :]
        for _ in range(3):
            rows.append(rest.astype(BF16).astype(F32))
            rest = rest - rows[-1]
    meta = jnp.concatenate(rows + [jnp.zeros((EXTRA - 8, count), F32)], axis=0).astype(BF16)
    meta_ref[...] = meta
    behind = pl.ds(count, EXTRA)
    for ref in (rows_ref, raw_ref):
        ref[behind, :count] = meta
        ref[behind, count:] = jnp.zeros((EXTRA, width - count), BF16)
    wait_all(copies)


def pack(pos, tokens, grad, ids, probs, chunk):
    count, width = tokens.shape
    return run(
        "pack",
        pack_kernel,
        [pos, tokens, grad, ids.T, probs.T],
        [shape(*pos.shape, dtype=jnp.int32), shape(count + EXTRA, width)]
        + [shape(count, chunk), shape(count, width - chunk)]
        + [shape(2 * count + EXTRA, width), shape(EXTRA, count)],
        held=[SMEM] + [ANY] * 4,
        out_held=[SMEM] + [VMEM] * 5,
        limit=4,
        scratch=[pltpu.VMEM((2, count), jnp.int32), pltpu.VMEM((2, count), F32), pltpu.SemaphoreType.DMA((2, 8))],
    )


def split_kernel(bx_ref, by_ref, top_ref, bottom_ref):
    half = top_ref.shape[0]
    top_ref[...] = by_ref[:half]
    bottom_ref[...] = bx_ref[half:]


def split(bx, by, half, after=()):
    rows, width = bx.shape
    return run("split", split_kernel, [bx, by], [shape(half, width), shape(rows - half, width)], after, limit=4)


def warm(weights, after):
    return run("warm", lambda *refs: None, weights, [], after, limit=11)


def group_rows(refs):
    own, bx, by, da, db, c_own, c_bx, c_by, c_da, c_db = refs
    for ref in (own, c_own, bx, c_bx, by, c_by):
        yield ref[...]
    for top, bottom in ((da, db), (c_da, c_db)):
        yield jnp.concatenate([top[...], bottom[...]], axis=0)


def route(me, metas, rank_ref, prob_ref):
    expert = me.astype(F32)
    named, probs = [], []
    for meta in metas:
        meta = meta.astype(F32)
        first, second = meta[0:1] == expert, meta[1:2] == expert
        p0 = (meta[2:3] + meta[3:4]) + meta[4:5]
        p1 = (meta[5:6] + meta[6:7]) + meta[7:8]
        named.append((first | second).astype(F32))
        probs.append(jnp.where(first, p0, jnp.where(second, p1, 0.0)))
    named = jnp.concatenate(named, axis=0)
    count = named.shape[1]
    earlier = lax.broadcasted_iota(jnp.int32, (count, count), 0) < lax.broadcasted_iota(
        jnp.int32, (count, count), 1
    )
    rank = nn(named.astype(BF16), earlier.astype(F32).astype(BF16))
    rank_ref[...] = jnp.where(named > 0, rank, -1.0)
    prob_ref[...] = jnp.concatenate(probs, axis=0)


def slot_rows(rows, rank, prob, capacity):
    hit = lax.broadcasted_iota(jnp.int32, (capacity, rank.shape[1]), 0).astype(F32) == rank
    picked = nn(hit.astype(F32).astype(BF16), rows)
    if prob is not None:
        picked = picked * jnp.sum(jnp.where(hit, prob, 0.0), axis=1, keepdims=True)
    return picked.astype(BF16)


def slot_range(me, k, capacity):
    return pl.ds(pl.multiple_of(jnp.bitwise_xor(me, k) * capacity, capacity), capacity)


def activate(cols, x, wg_ref, wu_ref, h_ref):
    g, u = nn(x, wg_ref[:, cols]), nn(x, wu_ref[:, cols])
    s = jax.nn.sigmoid(g)
    b = g * s
    h_ref[:, cols] = (b * u).astype(BF16)
    return u * s * (1.0 + g * (1.0 - s)), b


def forward_kernel(capacity, pos_ref, *refs):
    wg_ref, wu_ref, x_ref, rank_ref, prob_ref, h_ref, a_ref, b_ref = refs[10:]
    count, me = rank_ref.shape[1], pos_ref[0]
    groups = list(group_rows(refs[:10]))
    route(me, [rows[count:, :count] for rows in groups], rank_ref, prob_ref)
    for k, rows in enumerate(groups):
        x_ref[slot_range(me, k, capacity), :] = slot_rows(rows[:count], rank_ref[k : k + 1], None, capacity)

    def step(cols):
        a_ref[:, cols], b_ref[:, cols] = activate(cols, x_ref[...], wg_ref, wu_ref, h_ref)

    tiles(wg_ref.shape[1], step)


def forward(pos, groups, w_gate, w_up, capacity, after):
    width, hid = w_gate.shape
    slots, count = 8 * capacity, groups[0].shape[0] - EXTRA
    return run(
        "forward",
        functools.partial(forward_kernel, capacity),
        [pos, *groups, w_gate, w_up],
        [shape(slots, width)]
        + [shape(8, count, dtype=F32)] * 2
        + [shape(slots, hid)]
        + [shape(slots, hid, dtype=F32)] * 2,
        after,
        held=[SMEM] + [VMEM] * 12,
        us=6,
    )


def far_down_kernel(capacity, pos_ref, *refs):
    rank_ref, prob_ref, h_ref, dy_ref, far_ref = refs[8:]
    for k, ref in enumerate(refs[:8]):
        rank, prob = rank_ref[k : k + 1], prob_ref[k : k + 1]
        dy_ref[slot_range(pos_ref[0], k, capacity), :] = slot_rows(ref[...], rank, prob, capacity)
    far_ref[...] = tn(dy_ref[...], h_ref[...]).astype(BF16)


def far_down_of(pos, groups, rank, prob, h, capacity):
    chunk = groups[0].shape[1]
    slots, hid = h.shape
    return run(
        "far_down",
        functools.partial(far_down_kernel, capacity),
        [pos, *groups, rank, prob, h],
        [shape(slots, chunk), shape(chunk, hid)],
        held=[SMEM] + [VMEM] * 11,
        us=0.5,
    )


def retreat(cols, dy, wd_ref, a, b, dg_ref, du_ref):
    dh = nn(dy, wd_ref[:, cols])
    dg_ref[:, cols] = (dh * a).astype(BF16)
    du_ref[:, cols] = (dh * b).astype(BF16)


def backward_kernel(capacity, pos_ref, *refs):
    far_ref, rank_ref, prob_ref, x_ref, a_ref, b_ref, wd_ref, dy_ref, dg_ref, du_ref, out_ref = refs[10:]
    chunk, rest = far_ref.shape[1], refs[0].shape[1]
    far = columns(pos_ref[1], chunk)
    dy_ref[:, far] = far_ref[...]
    others = pl.ds(pl.multiple_of(jnp.where(pos_ref[1] == 0, chunk, 0), chunk), rest)
    for k, rows in enumerate(group_rows(refs[:10])):
        rank, prob = rank_ref[k : k + 1], prob_ref[k : k + 1]
        dy_ref[slot_range(pos_ref[0], k, capacity), others] = slot_rows(rows, rank, prob, capacity)

    def step(cols):
        retreat(cols, dy_ref[...], wd_ref, a_ref[:, cols], b_ref[:, cols], dg_ref, du_ref)
        out_ref[:, cols] = tn(x_ref[:, far], dg_ref[:, cols]).astype(BF16)

    tiles(wd_ref.shape[1], step)


def backward(pos, groups, far_rows, rank, prob, x, a, b, w_down, capacity, after):
    slots, hid = a.shape
    width, chunk = x.shape[1], far_rows.shape[1]
    return run(
        "backward",
        functools.partial(backward_kernel, capacity),
        [pos, *groups, far_rows, rank, prob, x, a, b, w_down],
        [shape(slots, width)] + [shape(slots, hid)] * 2 + [shape(chunk, hid)],
        after,
        held=[SMEM] + [VMEM] * 17,
        us=0.1,
        limit=12,
    )


def gradients_kernel(pos_ref, x_ref, dy_ref, dg_ref, du_ref, h_ref, *outs):
    for n, out in enumerate(outs):
        at = columns(pos_ref[1 + (n + 2) // 3], out.shape[0])
        left, right = ((x_ref, dg_ref), (x_ref, du_ref), (dy_ref, h_ref))[1 if n == 0 else (n - 1) % 3]
        out[...] = tn(left[:, at], right[...]).astype(out.dtype)


def gradients(pos, x, dy, dg, du, h, chunk, after):
    return run(
        "gradients",
        gradients_kernel,
        [pos, x, dy, dg, du, h],
        [shape(chunk, h.shape[1])] * 7,
        after,
        held=[SMEM] + [VMEM] * 5,
        us=14,
    )


def step_kernel(pos_ref, raw_ref, mine_ref, got_ref, *refs):
    out_ref = refs[len(refs) // 2]
    total = (mine_ref[...].astype(F32) + got_ref[...].astype(F32)).astype(BF16)
    out_ref[...] = jnp.where(pos_ref[4] == 1, raw_ref[...], total)
    if len(refs) > 1:
        split_kernel(*refs[:2], *refs[3:])


def step(pos, raw, mine, got, after, passed=(), half=0):
    outs = [shape(*mine.shape)]
    if passed:
        rows, width = passed[0].shape
        outs += [shape(half, width), shape(rows - half, width)]
    return run(
        "step",
        step_kernel,
        [pos, raw, mine, got, *passed],
        outs,
        after,
        held=[SMEM] + [VMEM] * (3 + len(passed)),
        us=16,
        limit=10 if passed else 6,
    )


def total_kernel(pos_ref, own_ref, far_ref, near_ref, out_ref):
    got = jnp.where(pos_ref[4] == 1, far_ref[...], near_ref[...])
    out_ref[...] = (own_ref[...].astype(F32) + got.astype(F32)).astype(BF16)


def total(pos, own, far_sum, near_sum, after):
    held = [SMEM] + [VMEM] * 3
    return run("total", total_kernel, [pos, own, far_sum, near_sum], [shape(*own.shape)], after, held=held, us=0.5, limit=6)


def rows_kernel(capacity, h_ref, dg_ref, du_ref, wd_ref, wg_ref, wu_ref, out_ref):
    groups = out_ref.shape[0]
    for r in cut_rows(wd_ref, 4):
        o = nt(h_ref[...], wd_ref[r, :]).astype(BF16)
        dx = (nt(dg_ref[...], wg_ref[r, :]) + nt(du_ref[...], wu_ref[r, :])).astype(BF16)
        for k in range(groups):
            at = slice(k * capacity, (k + 1) * capacity)
            out_ref[k, :capacity, r] = o[at]
            out_ref[k, capacity:, r] = dx[at]


def rows_back(h, dg, du, w_down, w_gate, w_up, capacity, after=()):
    slots, hid = h.shape
    return run(
        "rows_back",
        functools.partial(rows_kernel, capacity),
        [h, dg, du, w_down, w_gate, w_up],
        [shape(slots // capacity, 2 * capacity, w_gate.shape[0])],
        after,
        us=0.1,
    )


def combine_kernel(capacity, meta_ref, rows_ref, *refs):
    outs, (held_ref, mixed_ref, grad_ref, sem_in, sem_out) = refs[:2], refs[2:]
    parts, slots, part = held_ref.shape
    arrivals = []
    for n in range(parts):
        src = rows_ref.at[:, pl.ds(n * part, part)]
        arrivals += start_all([(src, held_ref.at[n])], sem_in.at[pl.ds(n, 1)])
    count = meta_ref.shape[1]
    same = lax.broadcasted_iota(jnp.int32, (EXTRA, EXTRA), 0) == lax.broadcasted_iota(jnp.int32, (EXTRA, EXTRA), 1)
    cols = tn(meta_ref[...], same.astype(F32).astype(BF16))
    ids = cols[:, 0:2].astype(jnp.int32)
    probs = [(cols[:, k : k + 1] + cols[:, k + 1 : k + 2]) + cols[:, k + 2 : k + 3] for k in (2, 5)]
    lane = lax.broadcasted_iota(jnp.int32, (count, 128), 1)
    named = ((lane == ids[:, 0:1]) | (lane == ids[:, 1:2])).astype(F32)
    earlier = lax.broadcasted_iota(jnp.int32, (count, count), 1) < lax.broadcasted_iota(
        jnp.int32, (count, count), 0
    )
    rank = nn(earlier.astype(F32).astype(BF16), named.astype(BF16))
    place = lax.broadcasted_iota(jnp.int32, (count, slots), 1)
    hits, both = [], 0.0
    for k in range(2):
        own = ids[:, k : k + 1]
        at = jnp.sum(jnp.where(lane == own, rank, 0.0), axis=1, keepdims=True).astype(jnp.int32)
        at = own * (2 * capacity) + at
        hits.append((place == at).astype(F32).astype(BF16))
        both = both + (place == at + capacity).astype(F32)
    both = both.astype(BF16)
    copies = []
    for n in range(parts):
        arrivals[n].wait()
        rows = held_ref[n]
        mixed_ref[n] = (nn(hits[0], rows) * probs[0] + nn(hits[1], rows) * probs[1]).astype(BF16)
        grad_ref[n] = nn(both, rows).astype(BF16)
        at = pl.ds(n * part, part)
        copies += start_all(
            [(ref.at[n], out.at[:, at]) for ref, out in zip((mixed_ref, grad_ref), outs)], sem_out.at[n]
        )
    wait_all(copies)


def combine(meta, rows, capacity, after=()):
    count = meta.shape[1]
    slots, width = rows.shape
    parts = 4
    return run(
        "combine",
        functools.partial(combine_kernel, capacity),
        [meta, rows],
        [shape(count, width)] * 2,
        after,
        held=[VMEM, ANY],
        out_held=[ANY] * 2,
        scratch=[pltpu.VMEM((parts, slots, width // parts), BF16)]
        + [pltpu.VMEM((parts, count, width // parts), BF16)] * 2
        + [pltpu.SemaphoreType.DMA((parts,)), pltpu.SemaphoreType.DMA((parts, 2))],
        us=0.5,
    )


def partner_kernel(capacity, pos_ref, *refs):
    own, bx, by, da, db, c_own, c_bx, c_by, c_da, c_db = refs[:10]
    wg_ref, wu_ref, wd_ref, x_ref, dy_ref, dg_ref, du_ref, h_ref, rank_ref, prob_ref = refs[10:]
    count = rank_ref.shape[1]
    behind = pl.ds(count + EXTRA, count)
    groups = [(ref, ref.at[behind, :]) for ref in (own, bx, by, c_own, c_bx, c_by)] + [(da, db), (c_da, c_db)]
    route(pos_ref[0], [rows[count : count + EXTRA, :count] for rows, _ in groups], rank_ref, prob_ref)
    for n, (rows, grads) in enumerate(groups):
        at = pl.ds(n * capacity, capacity)
        rank, prob = rank_ref[n : n + 1], prob_ref[n : n + 1]
        x_ref[at, :] = slot_rows(rows[:count], rank, None, capacity)
        dy_ref[at, :] = slot_rows(grads[...], rank, prob, capacity)

    def step(cols):
        a, b = activate(cols, x_ref[...], wg_ref, wu_ref, h_ref)
        retreat(cols, dy_ref[...], wd_ref, a, b, dg_ref, du_ref)

    tiles(wg_ref.shape[1], step)


def partner(pos, groups, weights, capacity, count, after):
    width, hid = weights[0].shape
    slots = 8 * capacity
    return run(
        "partner",
        functools.partial(partner_kernel, capacity),
        [pos, *groups, *weights],
        [shape(slots, width)] * 2 + [shape(slots, hid)] * 3,
        after,
        held=[SMEM] + [VMEM] * 13,
        scratch=[pltpu.VMEM((8, count), F32)] * 2,
        us=1,
        limit=14,
    )


def both_kernel(pos_ref, x_ref, dy_ref, dg_ref, du_ref, h_ref, *refs):
    for left, right, own, out in zip((x_ref, x_ref, dy_ref), (dg_ref, du_ref, h_ref), refs[:3], refs[3:]):
        total = own[...].astype(F32) + tn(left[:, columns(pos_ref[3], out.shape[0])], right[...])
        out[...] = total.astype(BF16)


def both(pos, slots, mine, after):
    return run(
        "both",
        both_kernel,
        [pos, *slots, *mine],
        [shape(*m.shape) for m in mine],
        after,
        held=[SMEM] + [VMEM] * 8,
        us=0.5,
    )


def local_pairs(tokens, expert_ids, gate_probs, w_gate, w_up, w_down, out_grad):
    count, top = expert_ids.shape
    width = tokens.shape[1]
    w_gate, w_up, w_down = w_gate[0], w_up[0], w_down[0]
    planes, peers = lax.axis_size("dp"), lax.axis_size("expert")
    capacity = 2 * count * top // peers
    chunk, half = width // planes, count // 2
    z = lax.axis_index("dp")
    me = lax.axis_index("expert")
    left = z < 2
    far = jnp.where(left, 3, 0)
    near = jnp.where(left, 2, 1)
    outer = ((z == 0) | (z == planes - 1)).astype(jnp.int32)
    pos = jnp.stack([me, far, near, z, outer]).astype(jnp.int32)

    def over(x, bit):
        return lax.ppermute(x, "expert", [(i, i ^ bit) for i in range(peers)])

    def swap(x):
        return lax.ppermute(x, "dp", [(i, i ^ 1) for i in range(planes)])

    inwards, across, middle = [(0, 1), (3, 2)], [(1, 3), (2, 0)], [(1, 2), (2, 1)]

    def along(x, pairs):
        return lax.ppermute(x, "dp", pairs)

    def relay(bx, by, half, after=()):
        top, bottom, token = split(bx, by, half, after)
        return over(top, 2), over(bottom, 4), token

    def doubled(*held):
        return held + tuple(over(t, 1) for t in held)

    pos, rows, far_grad, rest_grad, raw, meta, _ = pack(pos, tokens, out_grad, expert_ids, gate_probs, chunk)
    raw = swap(raw)
    bx, by = over(rows, 2), over(rows, 4)
    warmed = warm([w_gate, w_up, w_down], [meta])
    da, db, token = relay(bx, by, half, warmed)
    groups = doubled(rows, bx, by, da, db)
    far_grad = tie(far_grad, [da, db, raw])
    far_groups = []
    for f in (far_grad, over(far_grad, 2), over(far_grad, 4), over(far_grad, 6)):
        far_groups += [f, over(f, 1)]
    rest_grad = tie(rest_grad, [da, db])
    bx, by = over(rest_grad, 2), over(rest_grad, 4)
    x, rank, prob, h, a, b, token = forward(pos, groups, w_gate, w_up, capacity, [])
    far_rows, far_down, token = far_down_of(pos, far_groups, rank, prob, h, capacity)
    da, db, _ = relay(bx, by, half, [token])
    rest_groups = doubled(rest_grad, bx, by, da, db)
    raw = tie(raw, [da, db])
    raw_x, raw_y = over(raw, 2), over(raw, 4)

    y1 = along(far_down, inwards)
    dy, dg, du, far_gate, token = backward(
        pos, rest_groups, far_rows, rank, prob, x, a, b, w_down, capacity, [token]
    )
    y2 = along(far_gate, inwards)
    back, token = rows_back(h, dg, du, w_down, w_gate, w_up, capacity, [token])
    far_up, near_gate, near_up, near_down, *mine, token = gradients(pos, x, dy, dg, du, h, chunk, [token, y1])
    x3, top, bottom, token = step(pos, far_up, far_down, y1, [token], [raw_x, raw_y], count + EXTRA)
    y3 = along(x3, inwards + across)
    raw_a, raw_b = over(top, 2), over(bottom, 4)
    raw_groups = doubled(raw, raw_x, raw_y, raw_a, raw_b)
    back = lax.all_to_all(tie(back, [token]), "expert", split_axis=0, concat_axis=0, tiled=True)
    x4, token = step(pos, near_down, far_gate, y2, [token, raw_a, raw_b])
    y4 = along(x4, inwards + across)
    x5, token = step(pos, near_gate, far_up, y3, [token])
    y5 = along(x5, inwards + across)
    near_up = tie(near_up, [token])
    y6 = along(near_up, inwards)
    x6, token = step(pos, near_down, near_down, y4, [token])
    z_down = along(x6, middle)
    x7, token = step(pos, near_up, near_up, y6, [token, z_down])
    z_up = along(x7, middle)
    *slots, token = partner(pos, raw_groups, (w_gate, w_up, w_down), capacity, count, [token])
    x8, token = step(pos, near_gate, near_gate, y5, [token])
    z_gate = along(x8, middle)
    *mine, token = both(pos, slots, mine, [token])
    mixed, tokens_grad, token = combine(meta, back.reshape(2 * peers * capacity, width), capacity, [token])

    down, token = total(pos, mine[2], y3, z_down, [token])
    up, token = total(pos, mine[1], y5, z_up, [token])
    gate, _ = total(pos, mine[0], y4, z_gate, [token])
    grads = [g[None] for g in (gate, up, down)]
    return (mixed, tokens_grad, *grads)


def solution(mesh):
    placed = (
        P(("dp", "expert"), None),
        P(("dp", "expert"), None),
        P(("dp", "expert"), None),
        P("expert", None, None),
        P("expert", None, None),
        P("expert", None, None),
        P(("dp", "expert"), None),
    )
    paired = mesh.shape["dp"] == 4 and mesh.shape["expert"] == 8
    return jax.shard_map(
        local_pairs if paired else local_any,
        mesh=mesh,
        in_specs=placed,
        out_specs=(
            P(("dp", "expert"), None),
            P(("dp", "expert"), None),
            P("expert", "dp", None),
            P("expert", "dp", None),
            P("expert", "dp", None),
        ),
        check_vma=False,
    )
```

```python
import functools

import jax
import jax.numpy as jnp
from jax import lax
from jax.experimental import pallas as pl
from jax.experimental.pallas import tpu as pltpu
from jax.sharding import PartitionSpec as P

F32 = jnp.float32
BF16 = jnp.bfloat16


def route_slots(expert_ids, experts, capacity):
    flat = expert_ids.reshape(-1)
    onehot = (flat[:, None] == jnp.arange(experts, dtype=jnp.int32)[None, :]).astype(jnp.int32)
    before = jnp.cumsum(onehot, axis=0) - onehot
    position = jnp.sum(before * onehot, axis=1)
    return flat * capacity + position


def local_any(tokens, expert_ids, gate_probs, w_gate, w_up, w_down, out_grad):
    token_count, top_count = expert_ids.shape
    width = tokens.shape[1]
    local_experts = w_gate.shape[0]
    peers = lax.axis_size("expert")
    experts = local_experts * peers
    capacity = max(2, 2 * token_count * top_count // experts)
    slot_total = experts * capacity
    route_total = token_count * top_count
    slot = route_slots(expert_ids, experts, capacity)
    owner = slot[None, :] == jnp.arange(slot_total, dtype=jnp.int32)[:, None]
    live = jnp.any(owner, axis=1)
    route_index = jnp.sum(
        jnp.where(owner, jnp.arange(route_total, dtype=jnp.int32)[None, :], 0), axis=1
    )
    token_of_slot = route_index // top_count
    slot_prob = jnp.sum(jnp.where(owner, gate_probs.reshape(-1)[None, :], 0.0), axis=1)
    dispatched = jnp.where(
        live[:, None], jnp.take(tokens, token_of_slot, axis=0), jnp.zeros((), tokens.dtype)
    )
    dispatched = dispatched.reshape(peers, local_experts, capacity, width)
    received = lax.all_to_all(dispatched, "expert", split_axis=0, concat_axis=0, tiled=True)
    gate_act = jnp.einsum("secd,edh->sech", received, w_gate, preferred_element_type=F32)
    up_act = jnp.einsum("secd,edh->sech", received, w_up, preferred_element_type=F32)
    hidden = (jax.nn.silu(gate_act) * up_act).astype(BF16)
    result = jnp.einsum("sech,edh->secd", hidden, w_down, preferred_element_type=F32).astype(BF16)
    returned = lax.all_to_all(result, "expert", split_axis=0, concat_axis=0, tiled=True)
    picked = jnp.take(returned.reshape(slot_total, width), slot, axis=0).astype(F32)
    picked = picked.reshape(token_count, top_count, width)
    mixed = jnp.sum(picked * gate_probs[:, :, None], axis=1).astype(BF16)
    dy_rows = jnp.where(
        live[:, None], jnp.take(out_grad, token_of_slot, axis=0), jnp.zeros((), out_grad.dtype)
    )
    dy_slot = (dy_rows.astype(F32) * slot_prob[:, None]).astype(BF16)
    dy_slot = dy_slot.reshape(peers, local_experts, capacity, width)
    dy_recv = lax.all_to_all(dy_slot, "expert", split_axis=0, concat_axis=0, tiled=True)
    d_hidden = jnp.einsum("secd,edh->sech", dy_recv, w_down, preferred_element_type=F32)
    sigma = jax.nn.sigmoid(gate_act)
    d_gate = (d_hidden * up_act * sigma * (1.0 + gate_act * (1.0 - sigma))).astype(BF16)
    d_up = (d_hidden * gate_act * sigma).astype(BF16)
    dx_slot = jnp.einsum("sech,edh->secd", d_gate, w_gate, preferred_element_type=F32)
    dx_slot = (
        dx_slot + jnp.einsum("sech,edh->secd", d_up, w_up, preferred_element_type=F32)
    ).astype(BF16)
    dx_back = lax.all_to_all(dx_slot, "expert", split_axis=0, concat_axis=0, tiled=True)
    dx_picked = jnp.take(dx_back.reshape(slot_total, width), slot, axis=0).astype(F32)
    tokens_grad = jnp.sum(dx_picked.reshape(token_count, top_count, width), axis=1).astype(BF16)
    first = jnp.einsum("secd,sech->deh", received, d_gate, preferred_element_type=F32)
    second = jnp.einsum("secd,sech->deh", received, d_up, preferred_element_type=F32)
    third = jnp.einsum("secd,sech->deh", dy_recv, hidden, preferred_element_type=F32)
    share = lax.psum_scatter(
        jnp.stack([first, second, third], axis=1).astype(BF16),
        "dp",
        scatter_dimension=0,
        tiled=True,
    )
    grads = [jnp.transpose(share[:, k], (1, 0, 2)) for k in range(3)]
    return (mixed, tokens_grad, *grads)


EXTRA = 16
TILE = 256
VMEM = pl.BlockSpec(memory_space=pltpu.VMEM)
SMEM = pl.BlockSpec(memory_space=pltpu.SMEM)
ANY = pl.BlockSpec(memory_space=pl.ANY)


def nn(a, b):
    return lax.dot_general(a, b, (((1,), (0,)), ((), ())), preferred_element_type=F32)


def nt(a, b):
    return lax.dot_general(a, b, (((1,), (1,)), ((), ())), preferred_element_type=F32)


def tn(a, b):
    return lax.dot_general(a, b, (((0,), (0,)), ((), ())), preferred_element_type=F32)


def shape(*sizes, dtype=BF16):
    return jax.ShapeDtypeStruct(sizes, dtype)


def run(name, kernel, operands, outs, after=(), held=None, out_held=None, scratch=(), us=1.0, limit=11):
    skip, count = len(after), len(operands) + len(outs)

    def body(*refs):
        refs = refs[skip:]
        kernel(*refs[:count], *refs[count + 1 :])

    return pl.pallas_call(
        body,
        in_specs=[ANY] * skip + list(held or [VMEM] * len(operands)),
        out_specs=list(out_held or [VMEM] * len(outs)) + [VMEM],
        out_shape=list(outs) + [shape(8, 128, dtype=F32)],
        scratch_shapes=list(scratch),
        compiler_params=pltpu.CompilerParams(vmem_limit_bytes=limit * 1024 * 1024),
        cost_estimate=pl.CostEstimate(flops=int(us * 50e7), bytes_accessed=1 << 10, transcendentals=0),
        name=name,
    )(*after, *operands)


def tie(x, after):
    return pl.pallas_call(
        lambda *refs: None,
        in_specs=[ANY] * (1 + len(after)),
        out_specs=ANY,
        out_shape=jax.ShapeDtypeStruct(x.shape, x.dtype),
        input_output_aliases={0: 0},
        compiler_params=pltpu.CompilerParams(vmem_limit_bytes=1024 * 1024),
        cost_estimate=pl.CostEstimate(flops=8, bytes_accessed=8, transcendentals=0),
        name="tie",
    )(x, *after)


def tiles(size, body, tile=TILE):
    @pl.loop(0, size // tile)
    def _(i):
        body(pl.ds(pl.multiple_of(i * tile, tile), tile))


def columns(start, size):
    return pl.ds(pl.multiple_of(start * size, size), size)


def start_all(pairs, sem):
    copies = [pltpu.make_async_copy(src, dst, sem.at[n]) for n, (src, dst) in enumerate(pairs)]
    for copy in copies:
        copy.start()
    return copies


def wait_all(copies):
    for copy in copies:
        copy.wait()


def cut_rows(ref, parts):
    size = ref.shape[0] // parts
    return [pl.ds(n * size, size) for n in range(parts)]


def pack_kernel(pos_ref, tokens_in, grad_in, ids_in, prob_in, out_ref, rows_ref, far_ref, rest_ref, raw_ref, meta_ref, ids_ref, prob_ref, sem):
    count, width = tokens_in.shape
    for n in range(pos_ref.shape[0]):
        out_ref[n] = pos_ref[n]
    small = start_all([(ids_in, ids_ref), (prob_in, prob_ref)], sem.at[0])
    chunk, rest = far_ref.shape[1], rest_ref.shape[1]
    others = pl.ds(pl.multiple_of(jnp.where(pos_ref[1] == 0, chunk, 0), chunk), rest)
    pairs = []
    for r in cut_rows(tokens_in, 2):
        pairs.append((tokens_in.at[r, :], rows_ref.at[r, :]))
        pairs.append((tokens_in.at[r, :], raw_ref.at[r, :]))
        pairs.append((grad_in.at[r, :], raw_ref.at[pl.ds(count + EXTRA + r.start, r.size), :]))
    pairs.append((grad_in.at[:, columns(pos_ref[1], chunk)], far_ref))
    pairs.append((grad_in.at[:, others], rest_ref))
    copies = start_all(pairs, sem.at[1])
    wait_all(small)
    rows = [ids_ref[...].astype(F32)]
    for k in range(2):
        rest = prob_ref[k : k + 1, :]
        for _ in range(3):
            rows.append(rest.astype(BF16).astype(F32))
            rest = rest - rows[-1]
    meta = jnp.concatenate(rows + [jnp.zeros((EXTRA - 8, count), F32)], axis=0).astype(BF16)
    meta_ref[...] = meta
    behind = pl.ds(count, EXTRA)
    for ref in (rows_ref, raw_ref):
        ref[behind, :count] = meta
        ref[behind, count:] = jnp.zeros((EXTRA, width - count), BF16)
    wait_all(copies)


def pack(pos, tokens, grad, ids, probs, chunk):
    count, width = tokens.shape
    return run(
        "pack",
        pack_kernel,
        [pos, tokens, grad, ids.T, probs.T],
        [shape(*pos.shape, dtype=jnp.int32), shape(count + EXTRA, width)]
        + [shape(count, chunk), shape(count, width - chunk)]
        + [shape(2 * count + EXTRA, width), shape(EXTRA, count)],
        held=[SMEM] + [ANY] * 4,
        out_held=[SMEM] + [VMEM] * 5,
        limit=4,
        scratch=[pltpu.VMEM((2, count), jnp.int32), pltpu.VMEM((2, count), F32), pltpu.SemaphoreType.DMA((2, 8))],
    )


def split_kernel(bx_ref, by_ref, top_ref, bottom_ref):
    half = top_ref.shape[0]
    top_ref[...] = by_ref[:half]
    bottom_ref[...] = bx_ref[half:]


def split(bx, by, half, after=()):
    rows, width = bx.shape
    return run("split", split_kernel, [bx, by], [shape(half, width), shape(rows - half, width)], after, limit=4)


def warm(weights, after):
    return run("warm", lambda *refs: None, weights, [], after, limit=11)


def group_rows(refs):
    own, bx, by, da, db, c_own, c_bx, c_by, c_da, c_db = refs
    for ref in (own, c_own, bx, c_bx, by, c_by):
        yield ref[...]
    for top, bottom in ((da, db), (c_da, c_db)):
        yield jnp.concatenate([top[...], bottom[...]], axis=0)


def route(me, metas, rank_ref, prob_ref):
    expert = me.astype(F32)
    named, probs = [], []
    for meta in metas:
        meta = meta.astype(F32)
        first, second = meta[0:1] == expert, meta[1:2] == expert
        p0 = (meta[2:3] + meta[3:4]) + meta[4:5]
        p1 = (meta[5:6] + meta[6:7]) + meta[7:8]
        named.append((first | second).astype(F32))
        probs.append(jnp.where(first, p0, jnp.where(second, p1, 0.0)))
    named = jnp.concatenate(named, axis=0)
    count = named.shape[1]
    earlier = lax.broadcasted_iota(jnp.int32, (count, count), 0) < lax.broadcasted_iota(
        jnp.int32, (count, count), 1
    )
    rank = nn(named.astype(BF16), earlier.astype(F32).astype(BF16))
    rank_ref[...] = jnp.where(named > 0, rank, -1.0)
    prob_ref[...] = jnp.concatenate(probs, axis=0)


def slot_rows(rows, rank, prob, capacity):
    hit = lax.broadcasted_iota(jnp.int32, (capacity, rank.shape[1]), 0).astype(F32) == rank
    picked = nn(hit.astype(F32).astype(BF16), rows)
    if prob is not None:
        picked = picked * jnp.sum(jnp.where(hit, prob, 0.0), axis=1, keepdims=True)
    return picked.astype(BF16)


def slot_range(me, k, capacity):
    return pl.ds(pl.multiple_of(jnp.bitwise_xor(me, k) * capacity, capacity), capacity)


def activate(cols, x, wg_ref, wu_ref, h_ref):
    g, u = nn(x, wg_ref[:, cols]), nn(x, wu_ref[:, cols])
    s = jax.nn.sigmoid(g)
    b = g * s
    h_ref[:, cols] = (b * u).astype(BF16)
    return u * s * (1.0 + g * (1.0 - s)), b


def forward_kernel(capacity, pos_ref, *refs):
    wg_ref, wu_ref, x_ref, rank_ref, prob_ref, h_ref, a_ref, b_ref = refs[10:]
    count, me = rank_ref.shape[1], pos_ref[0]
    groups = list(group_rows(refs[:10]))
    route(me, [rows[count:, :count] for rows in groups], rank_ref, prob_ref)
    for k, rows in enumerate(groups):
        x_ref[slot_range(me, k, capacity), :] = slot_rows(rows[:count], rank_ref[k : k + 1], None, capacity)

    def step(cols):
        a_ref[:, cols], b_ref[:, cols] = activate(cols, x_ref[...], wg_ref, wu_ref, h_ref)

    tiles(wg_ref.shape[1], step)


def forward(pos, groups, w_gate, w_up, capacity, after):
    width, hid = w_gate.shape
    slots, count = 8 * capacity, groups[0].shape[0] - EXTRA
    return run(
        "forward",
        functools.partial(forward_kernel, capacity),
        [pos, *groups, w_gate, w_up],
        [shape(slots, width)]
        + [shape(8, count, dtype=F32)] * 2
        + [shape(slots, hid)]
        + [shape(slots, hid, dtype=F32)] * 2,
        after,
        held=[SMEM] + [VMEM] * 12,
        us=6,
    )


def far_down_kernel(capacity, pos_ref, *refs):
    rank_ref, prob_ref, h_ref, dy_ref, far_ref = refs[8:]
    for k, ref in enumerate(refs[:8]):
        rank, prob = rank_ref[k : k + 1], prob_ref[k : k + 1]
        dy_ref[slot_range(pos_ref[0], k, capacity), :] = slot_rows(ref[...], rank, prob, capacity)
    far_ref[...] = tn(dy_ref[...], h_ref[...]).astype(BF16)


def far_down_of(pos, groups, rank, prob, h, capacity):
    chunk = groups[0].shape[1]
    slots, hid = h.shape
    return run(
        "far_down",
        functools.partial(far_down_kernel, capacity),
        [pos, *groups, rank, prob, h],
        [shape(slots, chunk), shape(chunk, hid)],
        held=[SMEM] + [VMEM] * 11,
        us=0.5,
    )


def retreat(cols, dy, wd_ref, a, b, dg_ref, du_ref):
    dh = nn(dy, wd_ref[:, cols])
    dg_ref[:, cols] = (dh * a).astype(BF16)
    du_ref[:, cols] = (dh * b).astype(BF16)


def backward_kernel(capacity, pos_ref, *refs):
    far_ref, rank_ref, prob_ref, x_ref, a_ref, b_ref, wd_ref, dy_ref, dg_ref, du_ref, out_ref = refs[10:]
    chunk, rest = far_ref.shape[1], refs[0].shape[1]
    far = columns(pos_ref[1], chunk)
    dy_ref[:, far] = far_ref[...]
    others = pl.ds(pl.multiple_of(jnp.where(pos_ref[1] == 0, chunk, 0), chunk), rest)
    for k, rows in enumerate(group_rows(refs[:10])):
        rank, prob = rank_ref[k : k + 1], prob_ref[k : k + 1]
        dy_ref[slot_range(pos_ref[0], k, capacity), others] = slot_rows(rows, rank, prob, capacity)

    def step(cols):
        retreat(cols, dy_ref[...], wd_ref, a_ref[:, cols], b_ref[:, cols], dg_ref, du_ref)
        out_ref[:, cols] = tn(x_ref[:, far], dg_ref[:, cols]).astype(BF16)

    tiles(wd_ref.shape[1], step)


def backward(pos, groups, far_rows, rank, prob, x, a, b, w_down, capacity, after):
    slots, hid = a.shape
    width, chunk = x.shape[1], far_rows.shape[1]
    return run(
        "backward",
        functools.partial(backward_kernel, capacity),
        [pos, *groups, far_rows, rank, prob, x, a, b, w_down],
        [shape(slots, width)] + [shape(slots, hid)] * 2 + [shape(chunk, hid)],
        after,
        held=[SMEM] + [VMEM] * 17,
        us=0.1,
        limit=12,
    )


def gradients_kernel(pos_ref, x_ref, dy_ref, dg_ref, du_ref, h_ref, *outs):
    for n, out in enumerate(outs):
        at = columns(pos_ref[1 + (n + 2) // 3], out.shape[0])
        left, right = ((x_ref, dg_ref), (x_ref, du_ref), (dy_ref, h_ref))[1 if n == 0 else (n - 1) % 3]
        out[...] = tn(left[:, at], right[...]).astype(out.dtype)


def gradients(pos, x, dy, dg, du, h, chunk, after):
    return run(
        "gradients",
        gradients_kernel,
        [pos, x, dy, dg, du, h],
        [shape(chunk, h.shape[1])] * 7,
        after,
        held=[SMEM] + [VMEM] * 5,
        us=14,
    )


def step_kernel(pos_ref, raw_ref, mine_ref, got_ref, *refs):
    out_ref = refs[len(refs) // 2]
    total = (mine_ref[...].astype(F32) + got_ref[...].astype(F32)).astype(BF16)
    out_ref[...] = jnp.where(pos_ref[4] == 1, raw_ref[...], total)
    if len(refs) > 1:
        split_kernel(*refs[:2], *refs[3:])


def step(pos, raw, mine, got, after, passed=(), half=0):
    outs = [shape(*mine.shape)]
    if passed:
        rows, width = passed[0].shape
        outs += [shape(half, width), shape(rows - half, width)]
    return run(
        "step",
        step_kernel,
        [pos, raw, mine, got, *passed],
        outs,
        after,
        held=[SMEM] + [VMEM] * (3 + len(passed)),
        us=16,
        limit=10 if passed else 6,
    )


def total_kernel(pos_ref, own_ref, far_ref, near_ref, out_ref):
    got = jnp.where(pos_ref[4] == 1, far_ref[...], near_ref[...])
    out_ref[...] = (own_ref[...].astype(F32) + got.astype(F32)).astype(BF16)


def total(pos, own, far_sum, near_sum, after):
    held = [SMEM] + [VMEM] * 3
    return run("total", total_kernel, [pos, own, far_sum, near_sum], [shape(*own.shape)], after, held=held, us=0.5, limit=6)


def rows_kernel(capacity, h_ref, dg_ref, du_ref, wd_ref, wg_ref, wu_ref, out_ref):
    groups = out_ref.shape[0]
    for r in cut_rows(wd_ref, 4):
        o = nt(h_ref[...], wd_ref[r, :]).astype(BF16)
        dx = (nt(dg_ref[...], wg_ref[r, :]) + nt(du_ref[...], wu_ref[r, :])).astype(BF16)
        for k in range(groups):
            at = slice(k * capacity, (k + 1) * capacity)
            out_ref[k, :capacity, r] = o[at]
            out_ref[k, capacity:, r] = dx[at]


def rows_back(h, dg, du, w_down, w_gate, w_up, capacity, after=()):
    slots, hid = h.shape
    return run(
        "rows_back",
        functools.partial(rows_kernel, capacity),
        [h, dg, du, w_down, w_gate, w_up],
        [shape(slots // capacity, 2 * capacity, w_gate.shape[0])],
        after,
        us=0.1,
    )


def combine_kernel(capacity, meta_ref, rows_ref, *refs):
    outs, (held_ref, mixed_ref, grad_ref, sem_in, sem_out) = refs[:2], refs[2:]
    parts, slots, part = held_ref.shape
    arrivals = []
    for n in range(parts):
        src = rows_ref.at[:, pl.ds(n * part, part)]
        arrivals += start_all([(src, held_ref.at[n])], sem_in.at[pl.ds(n, 1)])
    count = meta_ref.shape[1]
    same = lax.broadcasted_iota(jnp.int32, (EXTRA, EXTRA), 0) == lax.broadcasted_iota(jnp.int32, (EXTRA, EXTRA), 1)
    cols = tn(meta_ref[...], same.astype(F32).astype(BF16))
    ids = cols[:, 0:2].astype(jnp.int32)
    probs = [(cols[:, k : k + 1] + cols[:, k + 1 : k + 2]) + cols[:, k + 2 : k + 3] for k in (2, 5)]
    lane = lax.broadcasted_iota(jnp.int32, (count, 128), 1)
    named = ((lane == ids[:, 0:1]) | (lane == ids[:, 1:2])).astype(F32)
    earlier = lax.broadcasted_iota(jnp.int32, (count, count), 1) < lax.broadcasted_iota(
        jnp.int32, (count, count), 0
    )
    rank = nn(earlier.astype(F32).astype(BF16), named.astype(BF16))
    place = lax.broadcasted_iota(jnp.int32, (count, slots), 1)
    hits, both = [], 0.0
    for k in range(2):
        own = ids[:, k : k + 1]
        at = jnp.sum(jnp.where(lane == own, rank, 0.0), axis=1, keepdims=True).astype(jnp.int32)
        at = own * (2 * capacity) + at
        hits.append((place == at).astype(F32).astype(BF16))
        both = both + (place == at + capacity).astype(F32)
    both = both.astype(BF16)
    copies = []
    for n in range(parts):
        arrivals[n].wait()
        rows = held_ref[n]
        mixed_ref[n] = (nn(hits[0], rows) * probs[0] + nn(hits[1], rows) * probs[1]).astype(BF16)
        grad_ref[n] = nn(both, rows).astype(BF16)
        at = pl.ds(n * part, part)
        copies += start_all(
            [(ref.at[n], out.at[:, at]) for ref, out in zip((mixed_ref, grad_ref), outs)], sem_out.at[n]
        )
    wait_all(copies)


def combine(meta, rows, capacity, after=()):
    count = meta.shape[1]
    slots, width = rows.shape
    parts = 4
    return run(
        "combine",
        functools.partial(combine_kernel, capacity),
        [meta, rows],
        [shape(count, width)] * 2,
        after,
        held=[VMEM, ANY],
        out_held=[ANY] * 2,
        scratch=[pltpu.VMEM((parts, slots, width // parts), BF16)]
        + [pltpu.VMEM((parts, count, width // parts), BF16)] * 2
        + [pltpu.SemaphoreType.DMA((parts,)), pltpu.SemaphoreType.DMA((parts, 2))],
        us=0.5,
    )


def partner_kernel(capacity, pos_ref, *refs):
    own, bx, by, da, db, c_own, c_bx, c_by, c_da, c_db = refs[:10]
    wg_ref, wu_ref, wd_ref, x_ref, dy_ref, dg_ref, du_ref, h_ref, rank_ref, prob_ref = refs[10:]
    count = rank_ref.shape[1]
    behind = pl.ds(count + EXTRA, count)
    groups = [(ref, ref.at[behind, :]) for ref in (own, bx, by, c_own, c_bx, c_by)] + [(da, db), (c_da, c_db)]
    route(pos_ref[0], [rows[count : count + EXTRA, :count] for rows, _ in groups], rank_ref, prob_ref)
    for n, (rows, grads) in enumerate(groups):
        at = pl.ds(n * capacity, capacity)
        rank, prob = rank_ref[n : n + 1], prob_ref[n : n + 1]
        x_ref[at, :] = slot_rows(rows[:count], rank, None, capacity)
        dy_ref[at, :] = slot_rows(grads[...], rank, prob, capacity)

    def step(cols):
        a, b = activate(cols, x_ref[...], wg_ref, wu_ref, h_ref)
        retreat(cols, dy_ref[...], wd_ref, a, b, dg_ref, du_ref)

    tiles(wg_ref.shape[1], step)


def partner(pos, groups, weights, capacity, count, after):
    width, hid = weights[0].shape
    slots = 8 * capacity
    return run(
        "partner",
        functools.partial(partner_kernel, capacity),
        [pos, *groups, *weights],
        [shape(slots, width)] * 2 + [shape(slots, hid)] * 3,
        after,
        held=[SMEM] + [VMEM] * 13,
        scratch=[pltpu.VMEM((8, count), F32)] * 2,
        us=1,
        limit=14,
    )


def both_kernel(pos_ref, x_ref, dy_ref, dg_ref, du_ref, h_ref, *refs):
    for left, right, own, out in zip((x_ref, x_ref, dy_ref), (dg_ref, du_ref, h_ref), refs[:3], refs[3:]):
        total = own[...].astype(F32) + tn(left[:, columns(pos_ref[3], out.shape[0])], right[...])
        out[...] = total.astype(BF16)


def both(pos, slots, mine, after):
    return run(
        "both",
        both_kernel,
        [pos, *slots, *mine],
        [shape(*m.shape) for m in mine],
        after,
        held=[SMEM] + [VMEM] * 8,
        us=0.5,
    )


def local_pairs(tokens, expert_ids, gate_probs, w_gate, w_up, w_down, out_grad):
    count, top = expert_ids.shape
    width = tokens.shape[1]
    w_gate, w_up, w_down = w_gate[0], w_up[0], w_down[0]
    planes, peers = lax.axis_size("dp"), lax.axis_size("expert")
    capacity = 2 * count * top // peers
    chunk, half = width // planes, count // 2
    z = lax.axis_index("dp")
    me = lax.axis_index("expert")
    left = z < 2
    far = jnp.where(left, 3, 0)
    near = jnp.where(left, 2, 1)
    outer = ((z == 0) | (z == planes - 1)).astype(jnp.int32)
    pos = jnp.stack([me, far, near, z, outer]).astype(jnp.int32)

    def over(x, bit):
        return lax.ppermute(x, "expert", [(i, i ^ bit) for i in range(peers)])

    def swap(x):
        return lax.ppermute(x, "dp", [(i, i ^ 1) for i in range(planes)])

    inwards, across, middle = [(0, 1), (3, 2)], [(1, 3), (2, 0)], [(1, 2), (2, 1)]

    def along(x, pairs):
        return lax.ppermute(x, "dp", pairs)

    def relay(bx, by, half, after=()):
        top, bottom, token = split(bx, by, half, after)
        return over(top, 2), over(bottom, 4), token

    def doubled(*held):
        return held + tuple(over(t, 1) for t in held)

    pos, rows, far_grad, rest_grad, raw, meta, _ = pack(pos, tokens, out_grad, expert_ids, gate_probs, chunk)
    raw = swap(raw)
    bx, by = over(rows, 2), over(rows, 4)
    warmed = warm([w_gate, w_up, w_down], [meta])
    da, db, token = relay(bx, by, half, warmed)
    groups = doubled(rows, bx, by, da, db)
    far_grad = tie(far_grad, [da, db, raw])
    far_groups = []
    for f in (far_grad, over(far_grad, 2), over(far_grad, 4), over(far_grad, 6)):
        far_groups += [f, over(f, 1)]
    rest_grad = tie(rest_grad, [da, db])
    bx, by = over(rest_grad, 2), over(rest_grad, 4)
    x, rank, prob, h, a, b, token = forward(pos, groups, w_gate, w_up, capacity, [])
    far_rows, far_down, token = far_down_of(pos, far_groups, rank, prob, h, capacity)
    da, db, _ = relay(bx, by, half, [token])
    rest_groups = doubled(rest_grad, bx, by, da, db)
    raw = tie(raw, [da, db])
    raw_x, raw_y = over(raw, 2), over(raw, 4)

    y1 = along(far_down, inwards)
    dy, dg, du, far_gate, token = backward(
        pos, rest_groups, far_rows, rank, prob, x, a, b, w_down, capacity, [token]
    )
    y2 = along(far_gate, inwards)
    far_up, near_gate, near_up, near_down, *mine, token = gradients(pos, x, dy, dg, du, h, chunk, [token, y1])
    x3, token = step(pos, far_up, far_down, y1, [token])
    y3 = along(x3, inwards + across)
    back, token = rows_back(h, dg, du, w_down, w_gate, w_up, capacity, [token])
    x4, top, bottom, token = step(pos, near_down, far_gate, y2, [token], [raw_x, raw_y], count + EXTRA)
    y4 = along(x4, inwards + across)
    raw_a, raw_b = over(top, 2), over(bottom, 4)
    raw_groups = doubled(raw, raw_x, raw_y, raw_a, raw_b)
    back = lax.all_to_all(tie(back, [token]), "expert", split_axis=0, concat_axis=0, tiled=True)
    near_gate = tie(near_gate, [token])
    y5 = along(near_gate, inwards)
    x5, token = step(pos, far_up, far_up, y3, [token, raw_a, raw_b])
    far_sum = along(x5, across)
    near_up = tie(near_up, [token])
    y6 = along(near_up, inwards)
    x6, token = step(pos, near_down, near_down, y4, [token])
    z_down = along(x6, middle)
    x7, token = step(pos, near_gate, near_gate, y5, [token, z_down, far_sum])
    z_gate = along(x7, middle)
    *slots, token = partner(pos, raw_groups, (w_gate, w_up, w_down), capacity, count, [token])
    x8, token = step(pos, near_up, near_up, y6, [token])
    z_up = along(x8, middle)
    *mine, token = both(pos, slots, mine, [token])
    mixed, tokens_grad, token = combine(meta, back.reshape(2 * peers * capacity, width), capacity, [token])

    down, token = total(pos, mine[2], y3, z_down, [token])
    gate, token = total(pos, mine[0], y4, z_gate, [token])
    up, _ = total(pos, mine[1], far_sum, z_up, [token])
    grads = [g[None] for g in (gate, up, down)]
    return (mixed, tokens_grad, *grads)


def solution(mesh):
    placed = (
        P(("dp", "expert"), None),
        P(("dp", "expert"), None),
        P(("dp", "expert"), None),
        P("expert", None, None),
        P("expert", None, None),
        P("expert", None, None),
        P(("dp", "expert"), None),
    )
    paired = mesh.shape["dp"] == 4 and mesh.shape["expert"] == 8
    return jax.shard_map(
        local_pairs if paired else local_any,
        mesh=mesh,
        in_specs=placed,
        out_specs=(
            P(("dp", "expert"), None),
            P(("dp", "expert"), None),
            P("expert", "dp", None),
            P("expert", "dp", None),
            P("expert", "dp", None),
        ),
        check_vma=False,
    )
```

```python
import functools

import jax
import jax.numpy as jnp
from jax import lax
from jax.experimental import pallas as pl
from jax.experimental.pallas import tpu as pltpu
from jax.sharding import PartitionSpec as P

F32 = jnp.float32
BF16 = jnp.bfloat16


def route_slots(expert_ids, experts, capacity):
    flat = expert_ids.reshape(-1)
    onehot = (flat[:, None] == jnp.arange(experts, dtype=jnp.int32)[None, :]).astype(jnp.int32)
    before = jnp.cumsum(onehot, axis=0) - onehot
    position = jnp.sum(before * onehot, axis=1)
    return flat * capacity + position


def local_any(tokens, expert_ids, gate_probs, w_gate, w_up, w_down, out_grad):
    token_count, top_count = expert_ids.shape
    width = tokens.shape[1]
    local_experts = w_gate.shape[0]
    peers = lax.axis_size("expert")
    experts = local_experts * peers
    capacity = max(2, 2 * token_count * top_count // experts)
    slot_total = experts * capacity
    route_total = token_count * top_count
    slot = route_slots(expert_ids, experts, capacity)
    owner = slot[None, :] == jnp.arange(slot_total, dtype=jnp.int32)[:, None]
    live = jnp.any(owner, axis=1)
    route_index = jnp.sum(
        jnp.where(owner, jnp.arange(route_total, dtype=jnp.int32)[None, :], 0), axis=1
    )
    token_of_slot = route_index // top_count
    slot_prob = jnp.sum(jnp.where(owner, gate_probs.reshape(-1)[None, :], 0.0), axis=1)
    dispatched = jnp.where(
        live[:, None], jnp.take(tokens, token_of_slot, axis=0), jnp.zeros((), tokens.dtype)
    )
    dispatched = dispatched.reshape(peers, local_experts, capacity, width)
    received = lax.all_to_all(dispatched, "expert", split_axis=0, concat_axis=0, tiled=True)
    gate_act = jnp.einsum("secd,edh->sech", received, w_gate, preferred_element_type=F32)
    up_act = jnp.einsum("secd,edh->sech", received, w_up, preferred_element_type=F32)
    hidden = (jax.nn.silu(gate_act) * up_act).astype(BF16)
    result = jnp.einsum("sech,edh->secd", hidden, w_down, preferred_element_type=F32).astype(BF16)
    returned = lax.all_to_all(result, "expert", split_axis=0, concat_axis=0, tiled=True)
    picked = jnp.take(returned.reshape(slot_total, width), slot, axis=0).astype(F32)
    picked = picked.reshape(token_count, top_count, width)
    mixed = jnp.sum(picked * gate_probs[:, :, None], axis=1).astype(BF16)
    dy_rows = jnp.where(
        live[:, None], jnp.take(out_grad, token_of_slot, axis=0), jnp.zeros((), out_grad.dtype)
    )
    dy_slot = (dy_rows.astype(F32) * slot_prob[:, None]).astype(BF16)
    dy_slot = dy_slot.reshape(peers, local_experts, capacity, width)
    dy_recv = lax.all_to_all(dy_slot, "expert", split_axis=0, concat_axis=0, tiled=True)
    d_hidden = jnp.einsum("secd,edh->sech", dy_recv, w_down, preferred_element_type=F32)
    sigma = jax.nn.sigmoid(gate_act)
    d_gate = (d_hidden * up_act * sigma * (1.0 + gate_act * (1.0 - sigma))).astype(BF16)
    d_up = (d_hidden * gate_act * sigma).astype(BF16)
    dx_slot = jnp.einsum("sech,edh->secd", d_gate, w_gate, preferred_element_type=F32)
    dx_slot = (
        dx_slot + jnp.einsum("sech,edh->secd", d_up, w_up, preferred_element_type=F32)
    ).astype(BF16)
    dx_back = lax.all_to_all(dx_slot, "expert", split_axis=0, concat_axis=0, tiled=True)
    dx_picked = jnp.take(dx_back.reshape(slot_total, width), slot, axis=0).astype(F32)
    tokens_grad = jnp.sum(dx_picked.reshape(token_count, top_count, width), axis=1).astype(BF16)
    first = jnp.einsum("secd,sech->deh", received, d_gate, preferred_element_type=F32)
    second = jnp.einsum("secd,sech->deh", received, d_up, preferred_element_type=F32)
    third = jnp.einsum("secd,sech->deh", dy_recv, hidden, preferred_element_type=F32)
    share = lax.psum_scatter(
        jnp.stack([first, second, third], axis=1).astype(BF16),
        "dp",
        scatter_dimension=0,
        tiled=True,
    )
    grads = [jnp.transpose(share[:, k], (1, 0, 2)) for k in range(3)]
    return (mixed, tokens_grad, *grads)


EXTRA = 16
TILE = 256
VMEM = pl.BlockSpec(memory_space=pltpu.VMEM)
SMEM = pl.BlockSpec(memory_space=pltpu.SMEM)
ANY = pl.BlockSpec(memory_space=pl.ANY)


def nn(a, b):
    return lax.dot_general(a, b, (((1,), (0,)), ((), ())), preferred_element_type=F32)


def nt(a, b):
    return lax.dot_general(a, b, (((1,), (1,)), ((), ())), preferred_element_type=F32)


def tn(a, b):
    return lax.dot_general(a, b, (((0,), (0,)), ((), ())), preferred_element_type=F32)


def shape(*sizes, dtype=BF16):
    return jax.ShapeDtypeStruct(sizes, dtype)


def run(name, kernel, operands, outs, after=(), held=None, out_held=None, scratch=(), us=1.0, limit=11):
    skip, count = len(after), len(operands) + len(outs)

    def body(*refs):
        refs = refs[skip:]
        kernel(*refs[:count], *refs[count + 1 :])

    return pl.pallas_call(
        body,
        in_specs=[ANY] * skip + list(held or [VMEM] * len(operands)),
        out_specs=list(out_held or [VMEM] * len(outs)) + [VMEM],
        out_shape=list(outs) + [shape(8, 128, dtype=F32)],
        scratch_shapes=list(scratch),
        compiler_params=pltpu.CompilerParams(vmem_limit_bytes=limit * 1024 * 1024),
        cost_estimate=pl.CostEstimate(flops=int(us * 50e7), bytes_accessed=1 << 10, transcendentals=0),
        name=name,
    )(*after, *operands)


def tie(x, after):
    return pl.pallas_call(
        lambda *refs: None,
        in_specs=[ANY] * (1 + len(after)),
        out_specs=ANY,
        out_shape=jax.ShapeDtypeStruct(x.shape, x.dtype),
        input_output_aliases={0: 0},
        compiler_params=pltpu.CompilerParams(vmem_limit_bytes=1024 * 1024),
        cost_estimate=pl.CostEstimate(flops=8, bytes_accessed=8, transcendentals=0),
        name="tie",
    )(x, *after)


def tiles(size, body, tile=TILE):
    @pl.loop(0, size // tile)
    def _(i):
        body(pl.ds(pl.multiple_of(i * tile, tile), tile))


def columns(start, size):
    return pl.ds(pl.multiple_of(start * size, size), size)


def start_all(pairs, sem):
    copies = [pltpu.make_async_copy(src, dst, sem.at[n]) for n, (src, dst) in enumerate(pairs)]
    for copy in copies:
        copy.start()
    return copies


def wait_all(copies):
    for copy in copies:
        copy.wait()


def cut_rows(ref, parts):
    size = ref.shape[0] // parts
    return [pl.ds(n * size, size) for n in range(parts)]


def pack_kernel(pos_ref, tokens_in, grad_in, ids_in, prob_in, out_ref, rows_ref, far_ref, rest_ref, raw_ref, meta_ref, ids_ref, prob_ref, sem):
    count, width = tokens_in.shape
    for n in range(pos_ref.shape[0]):
        out_ref[n] = pos_ref[n]
    small = start_all([(ids_in, ids_ref), (prob_in, prob_ref)], sem.at[0])
    chunk, rest = far_ref.shape[1], rest_ref.shape[1]
    others = pl.ds(pl.multiple_of(jnp.where(pos_ref[1] == 0, chunk, 0), chunk), rest)
    pairs = []
    for r in cut_rows(tokens_in, 2):
        pairs.append((tokens_in.at[r, :], rows_ref.at[r, :]))
        pairs.append((tokens_in.at[r, :], raw_ref.at[r, :]))
        pairs.append((grad_in.at[r, :], raw_ref.at[pl.ds(count + EXTRA + r.start, r.size), :]))
    pairs.append((grad_in.at[:, columns(pos_ref[1], chunk)], far_ref))
    pairs.append((grad_in.at[:, others], rest_ref))
    copies = start_all(pairs, sem.at[1])
    wait_all(small)
    rows = [ids_ref[...].astype(F32)]
    for k in range(2):
        rest = prob_ref[k : k + 1, :]
        for _ in range(3):
            rows.append(rest.astype(BF16).astype(F32))
            rest = rest - rows[-1]
    meta = jnp.concatenate(rows + [jnp.zeros((EXTRA - 8, count), F32)], axis=0).astype(BF16)
    meta_ref[...] = meta
    behind = pl.ds(count, EXTRA)
    for ref in (rows_ref, raw_ref):
        ref[behind, :count] = meta
        ref[behind, count:] = jnp.zeros((EXTRA, width - count), BF16)
    wait_all(copies)


def pack(pos, tokens, grad, ids, probs, chunk):
    count, width = tokens.shape
    return run(
        "pack",
        pack_kernel,
        [pos, tokens, grad, ids.T, probs.T],
        [shape(*pos.shape, dtype=jnp.int32), shape(count + EXTRA, width)]
        + [shape(count, chunk), shape(count, width - chunk)]
        + [shape(2 * count + EXTRA, width), shape(EXTRA, count)],
        held=[SMEM] + [ANY] * 4,
        out_held=[SMEM] + [VMEM] * 5,
        limit=4,
        scratch=[pltpu.VMEM((2, count), jnp.int32), pltpu.VMEM((2, count), F32), pltpu.SemaphoreType.DMA((2, 8))],
    )


def split_kernel(bx_ref, by_ref, top_ref, bottom_ref):
    half = top_ref.shape[0]
    top_ref[...] = by_ref[:half]
    bottom_ref[...] = bx_ref[half:]


def split(bx, by, half, after=()):
    rows, width = bx.shape
    return run("split", split_kernel, [bx, by], [shape(half, width), shape(rows - half, width)], after, limit=4)


def warm(weights, after):
    return run("warm", lambda *refs: None, weights, [], after, limit=11)


def group_rows(refs):
    own, bx, by, da, db, c_own, c_bx, c_by, c_da, c_db = refs
    for ref in (own, c_own, bx, c_bx, by, c_by):
        yield ref[...]
    for top, bottom in ((da, db), (c_da, c_db)):
        yield jnp.concatenate([top[...], bottom[...]], axis=0)


def route(me, metas, rank_ref, prob_ref):
    expert = me.astype(F32)
    named, probs = [], []
    for meta in metas:
        meta = meta.astype(F32)
        first, second = meta[0:1] == expert, meta[1:2] == expert
        p0 = (meta[2:3] + meta[3:4]) + meta[4:5]
        p1 = (meta[5:6] + meta[6:7]) + meta[7:8]
        named.append((first | second).astype(F32))
        probs.append(jnp.where(first, p0, jnp.where(second, p1, 0.0)))
    named = jnp.concatenate(named, axis=0)
    count = named.shape[1]
    earlier = lax.broadcasted_iota(jnp.int32, (count, count), 0) < lax.broadcasted_iota(
        jnp.int32, (count, count), 1
    )
    rank = nn(named.astype(BF16), earlier.astype(F32).astype(BF16))
    rank_ref[...] = jnp.where(named > 0, rank, -1.0)
    prob_ref[...] = jnp.concatenate(probs, axis=0)


def slot_rows(rows, rank, prob, capacity):
    hit = lax.broadcasted_iota(jnp.int32, (capacity, rank.shape[1]), 0).astype(F32) == rank
    picked = nn(hit.astype(F32).astype(BF16), rows)
    if prob is not None:
        picked = picked * jnp.sum(jnp.where(hit, prob, 0.0), axis=1, keepdims=True)
    return picked.astype(BF16)


def slot_range(me, k, capacity):
    return pl.ds(pl.multiple_of(jnp.bitwise_xor(me, k) * capacity, capacity), capacity)


def activate(cols, x, wg_ref, wu_ref, h_ref):
    g, u = nn(x, wg_ref[:, cols]), nn(x, wu_ref[:, cols])
    s = jax.nn.sigmoid(g)
    b = g * s
    h_ref[:, cols] = (b * u).astype(BF16)
    return u * s * (1.0 + g * (1.0 - s)), b


def forward_kernel(capacity, pos_ref, *refs):
    wg_ref, wu_ref, x_ref, rank_ref, prob_ref, h_ref, a_ref, b_ref = refs[10:]
    count, me = rank_ref.shape[1], pos_ref[0]
    groups = list(group_rows(refs[:10]))
    route(me, [rows[count:, :count] for rows in groups], rank_ref, prob_ref)
    for k, rows in enumerate(groups):
        x_ref[slot_range(me, k, capacity), :] = slot_rows(rows[:count], rank_ref[k : k + 1], None, capacity)

    def step(cols):
        a_ref[:, cols], b_ref[:, cols] = activate(cols, x_ref[...], wg_ref, wu_ref, h_ref)

    tiles(wg_ref.shape[1], step)


def forward(pos, groups, w_gate, w_up, capacity, after):
    width, hid = w_gate.shape
    slots, count = 8 * capacity, groups[0].shape[0] - EXTRA
    return run(
        "forward",
        functools.partial(forward_kernel, capacity),
        [pos, *groups, w_gate, w_up],
        [shape(slots, width)]
        + [shape(8, count, dtype=F32)] * 2
        + [shape(slots, hid)]
        + [shape(slots, hid, dtype=F32)] * 2,
        after,
        held=[SMEM] + [VMEM] * 12,
        us=6,
    )


def far_down_kernel(capacity, pos_ref, *refs):
    rank_ref, prob_ref, h_ref, dy_ref, far_ref = refs[8:]
    for k, ref in enumerate(refs[:8]):
        rank, prob = rank_ref[k : k + 1], prob_ref[k : k + 1]
        dy_ref[slot_range(pos_ref[0], k, capacity), :] = slot_rows(ref[...], rank, prob, capacity)
    far_ref[...] = tn(dy_ref[...], h_ref[...]).astype(BF16)


def far_down_of(pos, groups, rank, prob, h, capacity):
    chunk = groups[0].shape[1]
    slots, hid = h.shape
    return run(
        "far_down",
        functools.partial(far_down_kernel, capacity),
        [pos, *groups, rank, prob, h],
        [shape(slots, chunk), shape(chunk, hid)],
        held=[SMEM] + [VMEM] * 11,
        us=0.5,
    )


def retreat(cols, dy, wd_ref, a, b, dg_ref, du_ref):
    dh = nn(dy, wd_ref[:, cols])
    dg_ref[:, cols] = (dh * a).astype(BF16)
    du_ref[:, cols] = (dh * b).astype(BF16)


def backward_kernel(capacity, pos_ref, *refs):
    far_ref, rank_ref, prob_ref, x_ref, a_ref, b_ref, wd_ref, dy_ref, dg_ref, du_ref, out_ref = refs[10:]
    chunk, rest = far_ref.shape[1], refs[0].shape[1]
    far = columns(pos_ref[1], chunk)
    dy_ref[:, far] = far_ref[...]
    others = pl.ds(pl.multiple_of(jnp.where(pos_ref[1] == 0, chunk, 0), chunk), rest)
    for k, rows in enumerate(group_rows(refs[:10])):
        rank, prob = rank_ref[k : k + 1], prob_ref[k : k + 1]
        dy_ref[slot_range(pos_ref[0], k, capacity), others] = slot_rows(rows, rank, prob, capacity)

    def step(cols):
        retreat(cols, dy_ref[...], wd_ref, a_ref[:, cols], b_ref[:, cols], dg_ref, du_ref)
        out_ref[:, cols] = tn(x_ref[:, far], dg_ref[:, cols]).astype(BF16)

    tiles(wd_ref.shape[1], step)


def backward(pos, groups, far_rows, rank, prob, x, a, b, w_down, capacity, after):
    slots, hid = a.shape
    width, chunk = x.shape[1], far_rows.shape[1]
    return run(
        "backward",
        functools.partial(backward_kernel, capacity),
        [pos, *groups, far_rows, rank, prob, x, a, b, w_down],
        [shape(slots, width)] + [shape(slots, hid)] * 2 + [shape(chunk, hid)],
        after,
        held=[SMEM] + [VMEM] * 17,
        us=0.1,
        limit=12,
    )


def gradients_kernel(pos_ref, x_ref, dy_ref, dg_ref, du_ref, h_ref, *outs):
    for n, out in enumerate(outs):
        at = columns(pos_ref[1 + (n + 2) // 3], out.shape[0])
        left, right = ((x_ref, dg_ref), (x_ref, du_ref), (dy_ref, h_ref))[1 if n == 0 else (n - 1) % 3]
        out[...] = tn(left[:, at], right[...]).astype(out.dtype)


def gradients(pos, x, dy, dg, du, h, chunk, after):
    return run(
        "gradients",
        gradients_kernel,
        [pos, x, dy, dg, du, h],
        [shape(chunk, h.shape[1])] * 7,
        after,
        held=[SMEM] + [VMEM] * 5,
        us=14,
    )


def step_kernel(pos_ref, raw_ref, mine_ref, got_ref, *refs):
    out_ref = refs[len(refs) // 2]
    total = (mine_ref[...].astype(F32) + got_ref[...].astype(F32)).astype(BF16)
    out_ref[...] = jnp.where(pos_ref[4] == 1, raw_ref[...], total)
    if len(refs) > 1:
        split_kernel(*refs[:2], *refs[3:])


def step(pos, raw, mine, got, after, passed=(), half=0):
    outs = [shape(*mine.shape)]
    if passed:
        rows, width = passed[0].shape
        outs += [shape(half, width), shape(rows - half, width)]
    return run(
        "step",
        step_kernel,
        [pos, raw, mine, got, *passed],
        outs,
        after,
        held=[SMEM] + [VMEM] * (3 + len(passed)),
        us=16,
        limit=10 if passed else 6,
    )


def total_kernel(pos_ref, own_ref, far_ref, near_ref, out_ref):
    got = jnp.where(pos_ref[4] == 1, far_ref[...], near_ref[...])
    out_ref[...] = (own_ref[...].astype(F32) + got.astype(F32)).astype(BF16)


def total(pos, own, far_sum, near_sum, after):
    held = [SMEM] + [VMEM] * 3
    return run("total", total_kernel, [pos, own, far_sum, near_sum], [shape(*own.shape)], after, held=held, us=0.5, limit=6)


def rows_kernel(capacity, h_ref, dg_ref, du_ref, wd_ref, wg_ref, wu_ref, out_ref):
    groups = out_ref.shape[0]
    for r in cut_rows(wd_ref, 4):
        o = nt(h_ref[...], wd_ref[r, :]).astype(BF16)
        dx = (nt(dg_ref[...], wg_ref[r, :]) + nt(du_ref[...], wu_ref[r, :])).astype(BF16)
        for k in range(groups):
            at = slice(k * capacity, (k + 1) * capacity)
            out_ref[k, :capacity, r] = o[at]
            out_ref[k, capacity:, r] = dx[at]


def rows_back(h, dg, du, w_down, w_gate, w_up, capacity, after=()):
    slots, hid = h.shape
    return run(
        "rows_back",
        functools.partial(rows_kernel, capacity),
        [h, dg, du, w_down, w_gate, w_up],
        [shape(slots // capacity, 2 * capacity, w_gate.shape[0])],
        after,
        us=0.1,
    )


def combine_kernel(capacity, meta_ref, rows_ref, *refs):
    outs, (held_ref, mixed_ref, grad_ref, sem_in, sem_out) = refs[:2], refs[2:]
    parts, slots, part = held_ref.shape
    arrivals = []
    for n in range(parts):
        src = rows_ref.at[:, pl.ds(n * part, part)]
        arrivals += start_all([(src, held_ref.at[n])], sem_in.at[pl.ds(n, 1)])
    count = meta_ref.shape[1]
    same = lax.broadcasted_iota(jnp.int32, (EXTRA, EXTRA), 0) == lax.broadcasted_iota(jnp.int32, (EXTRA, EXTRA), 1)
    cols = tn(meta_ref[...], same.astype(F32).astype(BF16))
    ids = cols[:, 0:2].astype(jnp.int32)
    probs = [(cols[:, k : k + 1] + cols[:, k + 1 : k + 2]) + cols[:, k + 2 : k + 3] for k in (2, 5)]
    lane = lax.broadcasted_iota(jnp.int32, (count, 128), 1)
    named = ((lane == ids[:, 0:1]) | (lane == ids[:, 1:2])).astype(F32)
    earlier = lax.broadcasted_iota(jnp.int32, (count, count), 1) < lax.broadcasted_iota(
        jnp.int32, (count, count), 0
    )
    rank = nn(earlier.astype(F32).astype(BF16), named.astype(BF16))
    place = lax.broadcasted_iota(jnp.int32, (count, slots), 1)
    hits, both = [], 0.0
    for k in range(2):
        own = ids[:, k : k + 1]
        at = jnp.sum(jnp.where(lane == own, rank, 0.0), axis=1, keepdims=True).astype(jnp.int32)
        at = own * (2 * capacity) + at
        hits.append((place == at).astype(F32).astype(BF16))
        both = both + (place == at + capacity).astype(F32)
    both = both.astype(BF16)
    copies = []
    for n in range(parts):
        arrivals[n].wait()
        rows = held_ref[n]
        mixed_ref[n] = (nn(hits[0], rows) * probs[0] + nn(hits[1], rows) * probs[1]).astype(BF16)
        grad_ref[n] = nn(both, rows).astype(BF16)
        at = pl.ds(n * part, part)
        copies += start_all(
            [(ref.at[n], out.at[:, at]) for ref, out in zip((mixed_ref, grad_ref), outs)], sem_out.at[n]
        )
    wait_all(copies)


def combine(meta, rows, capacity, after=()):
    count = meta.shape[1]
    slots, width = rows.shape
    parts = 4
    return run(
        "combine",
        functools.partial(combine_kernel, capacity),
        [meta, rows],
        [shape(count, width)] * 2,
        after,
        held=[VMEM, ANY],
        out_held=[ANY] * 2,
        scratch=[pltpu.VMEM((parts, slots, width // parts), BF16)]
        + [pltpu.VMEM((parts, count, width // parts), BF16)] * 2
        + [pltpu.SemaphoreType.DMA((parts,)), pltpu.SemaphoreType.DMA((parts, 2))],
        us=0.5,
    )


def partner_kernel(capacity, pos_ref, *refs):
    own, bx, by, da, db, c_own, c_bx, c_by, c_da, c_db = refs[:10]
    wg_ref, wu_ref, wd_ref, x_ref, dy_ref, dg_ref, du_ref, h_ref, rank_ref, prob_ref = refs[10:]
    count = rank_ref.shape[1]
    behind = pl.ds(count + EXTRA, count)
    groups = [(ref, ref.at[behind, :]) for ref in (own, bx, by, c_own, c_bx, c_by)] + [(da, db), (c_da, c_db)]
    route(pos_ref[0], [rows[count : count + EXTRA, :count] for rows, _ in groups], rank_ref, prob_ref)
    for n, (rows, grads) in enumerate(groups):
        at = pl.ds(n * capacity, capacity)
        rank, prob = rank_ref[n : n + 1], prob_ref[n : n + 1]
        x_ref[at, :] = slot_rows(rows[:count], rank, None, capacity)
        dy_ref[at, :] = slot_rows(grads[...], rank, prob, capacity)

    def step(cols):
        a, b = activate(cols, x_ref[...], wg_ref, wu_ref, h_ref)
        retreat(cols, dy_ref[...], wd_ref, a, b, dg_ref, du_ref)

    tiles(wg_ref.shape[1], step)


def partner(pos, groups, weights, capacity, count, after):
    width, hid = weights[0].shape
    slots = 8 * capacity
    return run(
        "partner",
        functools.partial(partner_kernel, capacity),
        [pos, *groups, *weights],
        [shape(slots, width)] * 2 + [shape(slots, hid)] * 3,
        after,
        held=[SMEM] + [VMEM] * 13,
        scratch=[pltpu.VMEM((8, count), F32)] * 2,
        us=1,
        limit=14,
    )


def both_kernel(pos_ref, x_ref, dy_ref, dg_ref, du_ref, h_ref, *refs):
    for left, right, own, out in zip((x_ref, x_ref, dy_ref), (dg_ref, du_ref, h_ref), refs[:3], refs[3:]):
        total = own[...].astype(F32) + tn(left[:, columns(pos_ref[3], out.shape[0])], right[...])
        out[...] = total.astype(BF16)


def both(pos, slots, mine, after):
    return run(
        "both",
        both_kernel,
        [pos, *slots, *mine],
        [shape(*m.shape) for m in mine],
        after,
        held=[SMEM] + [VMEM] * 8,
        us=0.5,
    )


def local_pairs(tokens, expert_ids, gate_probs, w_gate, w_up, w_down, out_grad):
    count, top = expert_ids.shape
    width = tokens.shape[1]
    w_gate, w_up, w_down = w_gate[0], w_up[0], w_down[0]
    planes, peers = lax.axis_size("dp"), lax.axis_size("expert")
    capacity = 2 * count * top // peers
    chunk, half = width // planes, count // 2
    z = lax.axis_index("dp")
    me = lax.axis_index("expert")
    left = z < 2
    far = jnp.where(left, 3, 0)
    near = jnp.where(left, 2, 1)
    outer = ((z == 0) | (z == planes - 1)).astype(jnp.int32)
    pos = jnp.stack([me, far, near, z, outer]).astype(jnp.int32)

    def over(x, bit):
        return lax.ppermute(x, "expert", [(i, i ^ bit) for i in range(peers)])

    def swap(x):
        return lax.ppermute(x, "dp", [(i, i ^ 1) for i in range(planes)])

    inwards, across, middle = [(0, 1), (3, 2)], [(1, 3), (2, 0)], [(1, 2), (2, 1)]

    def along(x, pairs):
        return lax.ppermute(x, "dp", pairs)

    def relay(bx, by, half, after=()):
        top, bottom, token = split(bx, by, half, after)
        return over(top, 2), over(bottom, 4), token

    def doubled(*held):
        return held + tuple(over(t, 1) for t in held)

    pos, rows, far_grad, rest_grad, raw, meta, _ = pack(pos, tokens, out_grad, expert_ids, gate_probs, chunk)
    raw = swap(raw)
    bx, by = over(rows, 2), over(rows, 4)
    warmed = warm([w_gate, w_up, w_down], [meta])
    da, db, token = relay(bx, by, half, warmed)
    groups = doubled(rows, bx, by, da, db)
    far_grad = tie(far_grad, [da, db, raw])
    far_groups = []
    for f in (far_grad, over(far_grad, 2), over(far_grad, 4), over(far_grad, 6)):
        far_groups += [f, over(f, 1)]
    rest_grad = tie(rest_grad, [da, db])
    bx, by = over(rest_grad, 2), over(rest_grad, 4)
    x, rank, prob, h, a, b, token = forward(pos, groups, w_gate, w_up, capacity, [])
    far_rows, far_down, token = far_down_of(pos, far_groups, rank, prob, h, capacity)
    da, db, _ = relay(bx, by, half, [token])
    rest_groups = doubled(rest_grad, bx, by, da, db)
    raw = tie(raw, [da, db])
    raw_x, raw_y = over(raw, 2), over(raw, 4)

    y1 = along(far_down, inwards)
    dy, dg, du, far_gate, token = backward(
        pos, rest_groups, far_rows, rank, prob, x, a, b, w_down, capacity, [token]
    )
    y2 = along(far_gate, inwards)
    far_up, near_gate, near_up, near_down, *mine, token = gradients(pos, x, dy, dg, du, h, chunk, [token, y1])
    x3, token = step(pos, far_up, far_down, y1, [token])
    y3 = along(x3, inwards + across)
    back, token = rows_back(h, dg, du, w_down, w_gate, w_up, capacity, [token])
    x4, top, bottom, token = step(pos, near_down, far_gate, y2, [token], [raw_x, raw_y], count + EXTRA)
    y4 = along(x4, inwards + across)
    raw_a, raw_b = over(top, 2), over(bottom, 4)
    raw_groups = doubled(raw, raw_x, raw_y, raw_a, raw_b)
    near_gate = tie(near_gate, [token])
    y5 = along(near_gate, inwards)
    x5, token = step(pos, far_up, far_up, y3, [token, raw_a, raw_b])
    far_sum = along(x5, across)
    back = lax.all_to_all(tie(back, [token]), "expert", split_axis=0, concat_axis=0, tiled=True)
    near_up = tie(near_up, [token])
    y6 = along(near_up, inwards)
    x6, token = step(pos, near_down, near_down, y4, [token])
    z_down = along(x6, middle)
    x7, token = step(pos, near_gate, near_gate, y5, [token, z_down, far_sum])
    z_gate = along(x7, middle)
    *slots, token = partner(pos, raw_groups, (w_gate, w_up, w_down), capacity, count, [token])
    x8, token = step(pos, near_up, near_up, y6, [token])
    z_up = along(x8, middle)
    *mine, token = both(pos, slots, mine, [token])
    mixed, tokens_grad, token = combine(meta, back.reshape(2 * peers * capacity, width), capacity, [token])

    down, token = total(pos, mine[2], y3, z_down, [token])
    gate, token = total(pos, mine[0], y4, z_gate, [token])
    up, _ = total(pos, mine[1], far_sum, z_up, [token])
    grads = [g[None] for g in (gate, up, down)]
    return (mixed, tokens_grad, *grads)


def solution(mesh):
    placed = (
        P(("dp", "expert"), None),
        P(("dp", "expert"), None),
        P(("dp", "expert"), None),
        P("expert", None, None),
        P("expert", None, None),
        P("expert", None, None),
        P(("dp", "expert"), None),
    )
    paired = mesh.shape["dp"] == 4 and mesh.shape["expert"] == 8
    return jax.shard_map(
        local_pairs if paired else local_any,
        mesh=mesh,
        in_specs=placed,
        out_specs=(
            P(("dp", "expert"), None),
            P(("dp", "expert"), None),
            P("expert", "dp", None),
            P("expert", "dp", None),
            P("expert", "dp", None),
        ),
        check_vma=False,
    )
```

```python
import functools

import jax
import jax.numpy as jnp
from jax import lax
from jax.experimental import pallas as pl
from jax.experimental.pallas import tpu as pltpu
from jax.sharding import PartitionSpec as P

F32 = jnp.float32
BF16 = jnp.bfloat16


def route_slots(expert_ids, experts, capacity):
    flat = expert_ids.reshape(-1)
    onehot = (flat[:, None] == jnp.arange(experts, dtype=jnp.int32)[None, :]).astype(jnp.int32)
    before = jnp.cumsum(onehot, axis=0) - onehot
    position = jnp.sum(before * onehot, axis=1)
    return flat * capacity + position


def local_any(tokens, expert_ids, gate_probs, w_gate, w_up, w_down, out_grad):
    token_count, top_count = expert_ids.shape
    width = tokens.shape[1]
    local_experts = w_gate.shape[0]
    peers = lax.axis_size("expert")
    experts = local_experts * peers
    capacity = max(2, 2 * token_count * top_count // experts)
    slot_total = experts * capacity
    route_total = token_count * top_count
    slot = route_slots(expert_ids, experts, capacity)
    owner = slot[None, :] == jnp.arange(slot_total, dtype=jnp.int32)[:, None]
    live = jnp.any(owner, axis=1)
    route_index = jnp.sum(
        jnp.where(owner, jnp.arange(route_total, dtype=jnp.int32)[None, :], 0), axis=1
    )
    token_of_slot = route_index // top_count
    slot_prob = jnp.sum(jnp.where(owner, gate_probs.reshape(-1)[None, :], 0.0), axis=1)
    dispatched = jnp.where(
        live[:, None], jnp.take(tokens, token_of_slot, axis=0), jnp.zeros((), tokens.dtype)
    )
    dispatched = dispatched.reshape(peers, local_experts, capacity, width)
    received = lax.all_to_all(dispatched, "expert", split_axis=0, concat_axis=0, tiled=True)
    gate_act = jnp.einsum("secd,edh->sech", received, w_gate, preferred_element_type=F32)
    up_act = jnp.einsum("secd,edh->sech", received, w_up, preferred_element_type=F32)
    hidden = (jax.nn.silu(gate_act) * up_act).astype(BF16)
    result = jnp.einsum("sech,edh->secd", hidden, w_down, preferred_element_type=F32).astype(BF16)
    returned = lax.all_to_all(result, "expert", split_axis=0, concat_axis=0, tiled=True)
    picked = jnp.take(returned.reshape(slot_total, width), slot, axis=0).astype(F32)
    picked = picked.reshape(token_count, top_count, width)
    mixed = jnp.sum(picked * gate_probs[:, :, None], axis=1).astype(BF16)
    dy_rows = jnp.where(
        live[:, None], jnp.take(out_grad, token_of_slot, axis=0), jnp.zeros((), out_grad.dtype)
    )
    dy_slot = (dy_rows.astype(F32) * slot_prob[:, None]).astype(BF16)
    dy_slot = dy_slot.reshape(peers, local_experts, capacity, width)
    dy_recv = lax.all_to_all(dy_slot, "expert", split_axis=0, concat_axis=0, tiled=True)
    d_hidden = jnp.einsum("secd,edh->sech", dy_recv, w_down, preferred_element_type=F32)
    sigma = jax.nn.sigmoid(gate_act)
    d_gate = (d_hidden * up_act * sigma * (1.0 + gate_act * (1.0 - sigma))).astype(BF16)
    d_up = (d_hidden * gate_act * sigma).astype(BF16)
    dx_slot = jnp.einsum("sech,edh->secd", d_gate, w_gate, preferred_element_type=F32)
    dx_slot = (
        dx_slot + jnp.einsum("sech,edh->secd", d_up, w_up, preferred_element_type=F32)
    ).astype(BF16)
    dx_back = lax.all_to_all(dx_slot, "expert", split_axis=0, concat_axis=0, tiled=True)
    dx_picked = jnp.take(dx_back.reshape(slot_total, width), slot, axis=0).astype(F32)
    tokens_grad = jnp.sum(dx_picked.reshape(token_count, top_count, width), axis=1).astype(BF16)
    first = jnp.einsum("secd,sech->deh", received, d_gate, preferred_element_type=F32)
    second = jnp.einsum("secd,sech->deh", received, d_up, preferred_element_type=F32)
    third = jnp.einsum("secd,sech->deh", dy_recv, hidden, preferred_element_type=F32)
    share = lax.psum_scatter(
        jnp.stack([first, second, third], axis=1).astype(BF16),
        "dp",
        scatter_dimension=0,
        tiled=True,
    )
    grads = [jnp.transpose(share[:, k], (1, 0, 2)) for k in range(3)]
    return (mixed, tokens_grad, *grads)


EXTRA = 16
TILE = 256
VMEM = pl.BlockSpec(memory_space=pltpu.VMEM)
SMEM = pl.BlockSpec(memory_space=pltpu.SMEM)
ANY = pl.BlockSpec(memory_space=pl.ANY)


def nn(a, b):
    return lax.dot_general(a, b, (((1,), (0,)), ((), ())), preferred_element_type=F32)


def nt(a, b):
    return lax.dot_general(a, b, (((1,), (1,)), ((), ())), preferred_element_type=F32)


def tn(a, b):
    return lax.dot_general(a, b, (((0,), (0,)), ((), ())), preferred_element_type=F32)


def shape(*sizes, dtype=BF16):
    return jax.ShapeDtypeStruct(sizes, dtype)


def run(name, kernel, operands, outs, after=(), held=None, out_held=None, scratch=(), us=1.0, limit=11):
    skip, count = len(after), len(operands) + len(outs)

    def body(*refs):
        refs = refs[skip:]
        kernel(*refs[:count], *refs[count + 1 :])

    return pl.pallas_call(
        body,
        in_specs=[ANY] * skip + list(held or [VMEM] * len(operands)),
        out_specs=list(out_held or [VMEM] * len(outs)) + [VMEM],
        out_shape=list(outs) + [shape(8, 128, dtype=F32)],
        scratch_shapes=list(scratch),
        compiler_params=pltpu.CompilerParams(vmem_limit_bytes=limit * 1024 * 1024),
        cost_estimate=pl.CostEstimate(flops=int(us * 50e7), bytes_accessed=1 << 10, transcendentals=0),
        name=name,
    )(*after, *operands)


def tie(x, after):
    return pl.pallas_call(
        lambda *refs: None,
        in_specs=[ANY] * (1 + len(after)),
        out_specs=ANY,
        out_shape=jax.ShapeDtypeStruct(x.shape, x.dtype),
        input_output_aliases={0: 0},
        compiler_params=pltpu.CompilerParams(vmem_limit_bytes=1024 * 1024),
        cost_estimate=pl.CostEstimate(flops=8, bytes_accessed=8, transcendentals=0),
        name="tie",
    )(x, *after)


def tiles(size, body, tile=TILE):
    @pl.loop(0, size // tile)
    def _(i):
        body(pl.ds(pl.multiple_of(i * tile, tile), tile))


def columns(start, size):
    return pl.ds(pl.multiple_of(start * size, size), size)


def start_all(pairs, sem):
    copies = [pltpu.make_async_copy(src, dst, sem.at[n]) for n, (src, dst) in enumerate(pairs)]
    for copy in copies:
        copy.start()
    return copies


def wait_all(copies):
    for copy in copies:
        copy.wait()


def cut_rows(ref, parts):
    size = ref.shape[0] // parts
    return [pl.ds(n * size, size) for n in range(parts)]


def pack_kernel(pos_ref, tokens_in, grad_in, ids_in, prob_in, out_ref, rows_ref, far_ref, rest_ref, raw_ref, meta_ref, ids_ref, prob_ref, sem):
    count, width = tokens_in.shape
    for n in range(pos_ref.shape[0]):
        out_ref[n] = pos_ref[n]
    small = start_all([(ids_in, ids_ref), (prob_in, prob_ref)], sem.at[0])
    chunk, rest = far_ref.shape[1], rest_ref.shape[1]
    others = pl.ds(pl.multiple_of(jnp.where(pos_ref[1] == 0, chunk, 0), chunk), rest)
    pairs = []
    for r in cut_rows(tokens_in, 2):
        pairs.append((tokens_in.at[r, :], rows_ref.at[r, :]))
        pairs.append((tokens_in.at[r, :], raw_ref.at[r, :]))
        pairs.append((grad_in.at[r, :], raw_ref.at[pl.ds(count + EXTRA + r.start, r.size), :]))
    pairs.append((grad_in.at[:, columns(pos_ref[1], chunk)], far_ref))
    pairs.append((grad_in.at[:, others], rest_ref))
    copies = start_all(pairs, sem.at[1])
    wait_all(small)
    rows = [ids_ref[...].astype(F32)]
    for k in range(2):
        rest = prob_ref[k : k + 1, :]
        for _ in range(3):
            rows.append(rest.astype(BF16).astype(F32))
            rest = rest - rows[-1]
    meta = jnp.concatenate(rows + [jnp.zeros((EXTRA - 8, count), F32)], axis=0).astype(BF16)
    meta_ref[...] = meta
    behind = pl.ds(count, EXTRA)
    for ref in (rows_ref, raw_ref):
        ref[behind, :count] = meta
        ref[behind, count:] = jnp.zeros((EXTRA, width - count), BF16)
    wait_all(copies)


def pack(pos, tokens, grad, ids, probs, chunk):
    count, width = tokens.shape
    return run(
        "pack",
        pack_kernel,
        [pos, tokens, grad, ids.T, probs.T],
        [shape(*pos.shape, dtype=jnp.int32), shape(count + EXTRA, width)]
        + [shape(count, chunk), shape(count, width - chunk)]
        + [shape(2 * count + EXTRA, width), shape(EXTRA, count)],
        held=[SMEM] + [ANY] * 4,
        out_held=[SMEM] + [VMEM] * 5,
        limit=4,
        scratch=[pltpu.VMEM((2, count), jnp.int32), pltpu.VMEM((2, count), F32), pltpu.SemaphoreType.DMA((2, 8))],
    )


def split_kernel(bx_ref, by_ref, top_ref, bottom_ref):
    half = top_ref.shape[0]
    top_ref[...] = by_ref[:half]
    bottom_ref[...] = bx_ref[half:]


def split(bx, by, half, after=()):
    rows, width = bx.shape
    return run("split", split_kernel, [bx, by], [shape(half, width), shape(rows - half, width)], after, limit=4)


def warm(weights, after):
    return run("warm", lambda *refs: None, weights, [], after, limit=11)


def group_rows(refs):
    own, bx, by, da, db, c_own, c_bx, c_by, c_da, c_db = refs
    for ref in (own, c_own, bx, c_bx, by, c_by):
        yield ref[...]
    for top, bottom in ((da, db), (c_da, c_db)):
        yield jnp.concatenate([top[...], bottom[...]], axis=0)


def route(me, metas, rank_ref, prob_ref):
    expert = me.astype(F32)
    named, probs = [], []
    for meta in metas:
        meta = meta.astype(F32)
        first, second = meta[0:1] == expert, meta[1:2] == expert
        p0 = (meta[2:3] + meta[3:4]) + meta[4:5]
        p1 = (meta[5:6] + meta[6:7]) + meta[7:8]
        named.append((first | second).astype(F32))
        probs.append(jnp.where(first, p0, jnp.where(second, p1, 0.0)))
    named = jnp.concatenate(named, axis=0)
    count = named.shape[1]
    earlier = lax.broadcasted_iota(jnp.int32, (count, count), 0) < lax.broadcasted_iota(
        jnp.int32, (count, count), 1
    )
    rank = nn(named.astype(BF16), earlier.astype(F32).astype(BF16))
    rank_ref[...] = jnp.where(named > 0, rank, -1.0)
    prob_ref[...] = jnp.concatenate(probs, axis=0)


def slot_rows(rows, rank, prob, capacity):
    hit = lax.broadcasted_iota(jnp.int32, (capacity, rank.shape[1]), 0).astype(F32) == rank
    picked = nn(hit.astype(F32).astype(BF16), rows)
    if prob is not None:
        picked = picked * jnp.sum(jnp.where(hit, prob, 0.0), axis=1, keepdims=True)
    return picked.astype(BF16)


def slot_range(me, k, capacity):
    return pl.ds(pl.multiple_of(jnp.bitwise_xor(me, k) * capacity, capacity), capacity)


def activate(cols, x, wg_ref, wu_ref, h_ref):
    g, u = nn(x, wg_ref[:, cols]), nn(x, wu_ref[:, cols])
    s = jax.nn.sigmoid(g)
    b = g * s
    h_ref[:, cols] = (b * u).astype(BF16)
    return u * s * (1.0 + g * (1.0 - s)), b


def forward_kernel(capacity, pos_ref, *refs):
    wg_ref, wu_ref, x_ref, rank_ref, prob_ref, h_ref, a_ref, b_ref = refs[10:]
    count, me = rank_ref.shape[1], pos_ref[0]
    groups = list(group_rows(refs[:10]))
    route(me, [rows[count:, :count] for rows in groups], rank_ref, prob_ref)
    for k, rows in enumerate(groups):
        x_ref[slot_range(me, k, capacity), :] = slot_rows(rows[:count], rank_ref[k : k + 1], None, capacity)

    def step(cols):
        a_ref[:, cols], b_ref[:, cols] = activate(cols, x_ref[...], wg_ref, wu_ref, h_ref)

    tiles(wg_ref.shape[1], step)


def forward(pos, groups, w_gate, w_up, capacity, after):
    width, hid = w_gate.shape
    slots, count = 8 * capacity, groups[0].shape[0] - EXTRA
    return run(
        "forward",
        functools.partial(forward_kernel, capacity),
        [pos, *groups, w_gate, w_up],
        [shape(slots, width)]
        + [shape(8, count, dtype=F32)] * 2
        + [shape(slots, hid)]
        + [shape(slots, hid, dtype=F32)] * 2,
        after,
        held=[SMEM] + [VMEM] * 12,
        us=6,
    )


def far_down_kernel(capacity, pos_ref, *refs):
    rank_ref, prob_ref, h_ref, dy_ref, far_ref = refs[8:]
    for k, ref in enumerate(refs[:8]):
        rank, prob = rank_ref[k : k + 1], prob_ref[k : k + 1]
        dy_ref[slot_range(pos_ref[0], k, capacity), :] = slot_rows(ref[...], rank, prob, capacity)
    far_ref[...] = tn(dy_ref[...], h_ref[...]).astype(BF16)


def far_down_of(pos, groups, rank, prob, h, capacity):
    chunk = groups[0].shape[1]
    slots, hid = h.shape
    return run(
        "far_down",
        functools.partial(far_down_kernel, capacity),
        [pos, *groups, rank, prob, h],
        [shape(slots, chunk), shape(chunk, hid)],
        held=[SMEM] + [VMEM] * 11,
        us=0.5,
    )


def retreat(cols, dy, wd_ref, a, b, dg_ref, du_ref):
    dh = nn(dy, wd_ref[:, cols])
    dg_ref[:, cols] = (dh * a).astype(BF16)
    du_ref[:, cols] = (dh * b).astype(BF16)


def backward_kernel(capacity, pos_ref, *refs):
    far_ref, rank_ref, prob_ref, x_ref, a_ref, b_ref, wd_ref, dy_ref, dg_ref, du_ref, out_ref = refs[10:]
    chunk, rest = far_ref.shape[1], refs[0].shape[1]
    far = columns(pos_ref[1], chunk)
    dy_ref[:, far] = far_ref[...]
    others = pl.ds(pl.multiple_of(jnp.where(pos_ref[1] == 0, chunk, 0), chunk), rest)
    for k, rows in enumerate(group_rows(refs[:10])):
        rank, prob = rank_ref[k : k + 1], prob_ref[k : k + 1]
        dy_ref[slot_range(pos_ref[0], k, capacity), others] = slot_rows(rows, rank, prob, capacity)

    def step(cols):
        retreat(cols, dy_ref[...], wd_ref, a_ref[:, cols], b_ref[:, cols], dg_ref, du_ref)
        out_ref[:, cols] = tn(x_ref[:, far], dg_ref[:, cols]).astype(BF16)

    tiles(wd_ref.shape[1], step)


def backward(pos, groups, far_rows, rank, prob, x, a, b, w_down, capacity, after):
    slots, hid = a.shape
    width, chunk = x.shape[1], far_rows.shape[1]
    return run(
        "backward",
        functools.partial(backward_kernel, capacity),
        [pos, *groups, far_rows, rank, prob, x, a, b, w_down],
        [shape(slots, width)] + [shape(slots, hid)] * 2 + [shape(chunk, hid)],
        after,
        held=[SMEM] + [VMEM] * 17,
        us=0.1,
        limit=12,
    )


def gradients_kernel(pos_ref, x_ref, dy_ref, dg_ref, du_ref, h_ref, *outs):
    for n, out in enumerate(outs):
        at = columns(pos_ref[1 + (n + 2) // 3], out.shape[0])
        left, right = ((x_ref, dg_ref), (x_ref, du_ref), (dy_ref, h_ref))[1 if n == 0 else (n - 1) % 3]
        out[...] = tn(left[:, at], right[...]).astype(out.dtype)


def gradients(pos, x, dy, dg, du, h, chunk, after):
    return run(
        "gradients",
        gradients_kernel,
        [pos, x, dy, dg, du, h],
        [shape(chunk, h.shape[1])] * 7,
        after,
        held=[SMEM] + [VMEM] * 5,
        us=14,
    )


def step_kernel(pos_ref, raw_ref, mine_ref, got_ref, *refs):
    out_ref = refs[len(refs) // 2]
    total = (mine_ref[...].astype(F32) + got_ref[...].astype(F32)).astype(BF16)
    out_ref[...] = jnp.where(pos_ref[4] == 1, raw_ref[...], total)
    if len(refs) > 1:
        split_kernel(*refs[:2], *refs[3:])


def step(pos, raw, mine, got, after, passed=(), half=0):
    outs = [shape(*mine.shape)]
    if passed:
        rows, width = passed[0].shape
        outs += [shape(half, width), shape(rows - half, width)]
    return run(
        "step",
        step_kernel,
        [pos, raw, mine, got, *passed],
        outs,
        after,
        held=[SMEM] + [VMEM] * (3 + len(passed)),
        us=16,
        limit=10 if passed else 6,
    )


def total_kernel(pos_ref, own_ref, far_ref, near_ref, out_ref):
    got = jnp.where(pos_ref[4] == 1, far_ref[...], near_ref[...])
    out_ref[...] = (own_ref[...].astype(F32) + got.astype(F32)).astype(BF16)


def total(pos, own, far_sum, near_sum, after):
    held = [SMEM] + [VMEM] * 3
    return run("total", total_kernel, [pos, own, far_sum, near_sum], [shape(*own.shape)], after, held=held, us=0.5, limit=6)


def rows_kernel(capacity, h_ref, dg_ref, du_ref, wd_ref, wg_ref, wu_ref, out_ref):
    groups = out_ref.shape[0]
    for r in cut_rows(wd_ref, 4):
        o = nt(h_ref[...], wd_ref[r, :]).astype(BF16)
        dx = (nt(dg_ref[...], wg_ref[r, :]) + nt(du_ref[...], wu_ref[r, :])).astype(BF16)
        for k in range(groups):
            at = slice(k * capacity, (k + 1) * capacity)
            out_ref[k, :capacity, r] = o[at]
            out_ref[k, capacity:, r] = dx[at]


def rows_back(h, dg, du, w_down, w_gate, w_up, capacity, after=()):
    slots, hid = h.shape
    return run(
        "rows_back",
        functools.partial(rows_kernel, capacity),
        [h, dg, du, w_down, w_gate, w_up],
        [shape(slots // capacity, 2 * capacity, w_gate.shape[0])],
        after,
        us=0.1,
    )


def combine_kernel(capacity, meta_ref, rows_ref, *refs):
    outs, (held_ref, mixed_ref, grad_ref, sem_in, sem_out) = refs[:2], refs[2:]
    parts, slots, part = held_ref.shape
    arrivals = []
    for n in range(parts):
        src = rows_ref.at[:, pl.ds(n * part, part)]
        arrivals += start_all([(src, held_ref.at[n])], sem_in.at[pl.ds(n, 1)])
    count = meta_ref.shape[1]
    same = lax.broadcasted_iota(jnp.int32, (EXTRA, EXTRA), 0) == lax.broadcasted_iota(jnp.int32, (EXTRA, EXTRA), 1)
    cols = tn(meta_ref[...], same.astype(F32).astype(BF16))
    ids = cols[:, 0:2].astype(jnp.int32)
    probs = [(cols[:, k : k + 1] + cols[:, k + 1 : k + 2]) + cols[:, k + 2 : k + 3] for k in (2, 5)]
    lane = lax.broadcasted_iota(jnp.int32, (count, 128), 1)
    named = ((lane == ids[:, 0:1]) | (lane == ids[:, 1:2])).astype(F32)
    earlier = lax.broadcasted_iota(jnp.int32, (count, count), 1) < lax.broadcasted_iota(
        jnp.int32, (count, count), 0
    )
    rank = nn(earlier.astype(F32).astype(BF16), named.astype(BF16))
    place = lax.broadcasted_iota(jnp.int32, (count, slots), 1)
    hits, both = [], 0.0
    for k in range(2):
        own = ids[:, k : k + 1]
        at = jnp.sum(jnp.where(lane == own, rank, 0.0), axis=1, keepdims=True).astype(jnp.int32)
        at = own * (2 * capacity) + at
        hits.append((place == at).astype(F32).astype(BF16))
        both = both + (place == at + capacity).astype(F32)
    both = both.astype(BF16)
    copies = []
    for n in range(parts):
        arrivals[n].wait()
        rows = held_ref[n]
        mixed_ref[n] = (nn(hits[0], rows) * probs[0] + nn(hits[1], rows) * probs[1]).astype(BF16)
        grad_ref[n] = nn(both, rows).astype(BF16)
        at = pl.ds(n * part, part)
        copies += start_all(
            [(ref.at[n], out.at[:, at]) for ref, out in zip((mixed_ref, grad_ref), outs)], sem_out.at[n]
        )
    wait_all(copies)


def combine(meta, rows, capacity, after=()):
    count = meta.shape[1]
    slots, width = rows.shape
    parts = 4
    return run(
        "combine",
        functools.partial(combine_kernel, capacity),
        [meta, rows],
        [shape(count, width)] * 2,
        after,
        held=[VMEM, ANY],
        out_held=[ANY] * 2,
        scratch=[pltpu.VMEM((parts, slots, width // parts), BF16)]
        + [pltpu.VMEM((parts, count, width // parts), BF16)] * 2
        + [pltpu.SemaphoreType.DMA((parts,)), pltpu.SemaphoreType.DMA((parts, 2))],
        us=0.5,
    )


def partner_kernel(capacity, pos_ref, *refs):
    own, bx, by, da, db, c_own, c_bx, c_by, c_da, c_db = refs[:10]
    wg_ref, wu_ref, wd_ref, x_ref, dy_ref, dg_ref, du_ref, h_ref, rank_ref, prob_ref = refs[10:]
    count = rank_ref.shape[1]
    behind = pl.ds(count + EXTRA, count)
    groups = [(ref, ref.at[behind, :]) for ref in (own, bx, by, c_own, c_bx, c_by)] + [(da, db), (c_da, c_db)]
    route(pos_ref[0], [rows[count : count + EXTRA, :count] for rows, _ in groups], rank_ref, prob_ref)
    for n, (rows, grads) in enumerate(groups):
        at = pl.ds(n * capacity, capacity)
        rank, prob = rank_ref[n : n + 1], prob_ref[n : n + 1]
        x_ref[at, :] = slot_rows(rows[:count], rank, None, capacity)
        dy_ref[at, :] = slot_rows(grads[...], rank, prob, capacity)

    def step(cols):
        a, b = activate(cols, x_ref[...], wg_ref, wu_ref, h_ref)
        retreat(cols, dy_ref[...], wd_ref, a, b, dg_ref, du_ref)

    tiles(wg_ref.shape[1], step)


def partner(pos, groups, weights, capacity, count, after):
    width, hid = weights[0].shape
    slots = 8 * capacity
    return run(
        "partner",
        functools.partial(partner_kernel, capacity),
        [pos, *groups, *weights],
        [shape(slots, width)] * 2 + [shape(slots, hid)] * 3,
        after,
        held=[SMEM] + [VMEM] * 13,
        scratch=[pltpu.VMEM((8, count), F32)] * 2,
        us=1,
        limit=14,
    )


def both_kernel(pos_ref, x_ref, dy_ref, dg_ref, du_ref, h_ref, *refs):
    for left, right, own, out in zip((x_ref, x_ref, dy_ref), (dg_ref, du_ref, h_ref), refs[:3], refs[3:]):
        total = own[...].astype(F32) + tn(left[:, columns(pos_ref[3], out.shape[0])], right[...])
        out[...] = total.astype(BF16)


def both(pos, slots, mine, after):
    return run(
        "both",
        both_kernel,
        [pos, *slots, *mine],
        [shape(*m.shape) for m in mine],
        after,
        held=[SMEM] + [VMEM] * 8,
        us=0.5,
    )


def local_pairs(tokens, expert_ids, gate_probs, w_gate, w_up, w_down, out_grad):
    count, top = expert_ids.shape
    width = tokens.shape[1]
    w_gate, w_up, w_down = w_gate[0], w_up[0], w_down[0]
    planes, peers = lax.axis_size("dp"), lax.axis_size("expert")
    capacity = 2 * count * top // peers
    chunk, half = width // planes, count // 2
    z = lax.axis_index("dp")
    me = lax.axis_index("expert")
    left = z < 2
    far = jnp.where(left, 3, 0)
    near = jnp.where(left, 2, 1)
    outer = ((z == 0) | (z == planes - 1)).astype(jnp.int32)
    pos = jnp.stack([me, far, near, z, outer]).astype(jnp.int32)

    def over(x, bit):
        return lax.ppermute(x, "expert", [(i, i ^ bit) for i in range(peers)])

    def swap(x):
        return lax.ppermute(x, "dp", [(i, i ^ 1) for i in range(planes)])

    inwards, across, middle = [(0, 1), (3, 2)], [(1, 3), (2, 0)], [(1, 2), (2, 1)]

    def along(x, pairs):
        return lax.ppermute(x, "dp", pairs)

    def relay(bx, by, half, after=()):
        top, bottom, token = split(bx, by, half, after)
        return over(top, 2), over(bottom, 4), token

    def doubled(*held):
        return held + tuple(over(t, 1) for t in held)

    pos, rows, far_grad, rest_grad, raw, meta, _ = pack(pos, tokens, out_grad, expert_ids, gate_probs, chunk)
    raw = swap(raw)
    bx, by = over(rows, 2), over(rows, 4)
    warmed = warm([w_gate, w_up, w_down], [meta])
    da, db, token = relay(bx, by, half, warmed)
    groups = doubled(rows, bx, by, da, db)
    far_grad = tie(far_grad, [da, db, raw])
    far_groups = []
    for f in (far_grad, over(far_grad, 2), over(far_grad, 4), over(far_grad, 6)):
        far_groups += [f, over(f, 1)]
    rest_grad = tie(rest_grad, [da, db])
    bx, by = over(rest_grad, 2), over(rest_grad, 4)
    x, rank, prob, h, a, b, token = forward(pos, groups, w_gate, w_up, capacity, [])
    far_rows, far_down, token = far_down_of(pos, far_groups, rank, prob, h, capacity)
    da, db, _ = relay(bx, by, half, [token])
    rest_groups = doubled(rest_grad, bx, by, da, db)
    raw = tie(raw, [da, db])
    raw_x, raw_y = over(raw, 2), over(raw, 4)

    y1 = along(far_down, inwards)
    dy, dg, du, far_gate, token = backward(
        pos, rest_groups, far_rows, rank, prob, x, a, b, w_down, capacity, [token]
    )
    y2 = along(far_gate, inwards)
    far_up, near_gate, near_up, near_down, *mine, token = gradients(pos, x, dy, dg, du, h, chunk, [token, y1])
    x3, token = step(pos, far_up, far_down, y1, [token])
    y3 = along(x3, inwards + across)
    back, token = rows_back(h, dg, du, w_down, w_gate, w_up, capacity, [token])
    x4, top, bottom, token = step(pos, near_down, far_gate, y2, [token], [raw_x, raw_y], count + EXTRA)
    y4 = along(x4, inwards + across)
    raw_a, raw_b = over(top, 2), over(bottom, 4)
    raw_groups = doubled(raw, raw_x, raw_y, raw_a, raw_b)
    near_gate = tie(near_gate, [token])
    y5 = along(near_gate, inwards)
    x5, token = step(pos, far_up, far_up, y3, [token, raw_a, raw_b])
    far_sum = along(x5, across)
    back = lax.all_to_all(tie(back, [token]), "expert", split_axis=0, concat_axis=0, tiled=True)
    near_up = tie(near_up, [token])
    y6 = along(near_up, inwards)
    x6, token = step(pos, near_down, near_down, y4, [token])
    z_down = along(x6, middle)
    x7, token = step(pos, near_gate, near_gate, y5, [token, z_down, far_sum])
    z_gate = along(x7, middle)
    x8, token = step(pos, near_up, near_up, y6, [token])
    z_up = along(x8, middle)
    *slots, token = partner(pos, raw_groups, (w_gate, w_up, w_down), capacity, count, [token])
    *mine, token = both(pos, slots, mine, [token])
    mixed, tokens_grad, token = combine(meta, back.reshape(2 * peers * capacity, width), capacity, [token])

    down, token = total(pos, mine[2], y3, z_down, [token])
    gate, token = total(pos, mine[0], y4, z_gate, [token])
    up, _ = total(pos, mine[1], far_sum, z_up, [token])
    grads = [g[None] for g in (gate, up, down)]
    return (mixed, tokens_grad, *grads)


def solution(mesh):
    placed = (
        P(("dp", "expert"), None),
        P(("dp", "expert"), None),
        P(("dp", "expert"), None),
        P("expert", None, None),
        P("expert", None, None),
        P("expert", None, None),
        P(("dp", "expert"), None),
    )
    paired = mesh.shape["dp"] == 4 and mesh.shape["expert"] == 8
    return jax.shard_map(
        local_pairs if paired else local_any,
        mesh=mesh,
        in_specs=placed,
        out_specs=(
            P(("dp", "expert"), None),
            P(("dp", "expert"), None),
            P("expert", "dp", None),
            P("expert", "dp", None),
            P("expert", "dp", None),
        ),
        check_vma=False,
    )
```
